128 devices in a mesh: section: 2 (over core), expert: 16 (over z, y), mp: 4 (over x).
Axes of the slice: x: 4, y: 4, z: 4, core: 2. Of those that a mesh axis runs over, the one named last changes fastest.
Arguments:
- block_input: bfloat16 [2, 16, 128, 768], P(None, 'expert'), may hold values from -6 to 6
- segments: int32 [2, 16, 128], P(None, 'expert'), may hold values from 0 to 3, never falling along the last dimension, each value on 1 to 64 neighbouring positions
- routes: int32 [2, 16, 128, 2], P(None, 'expert'), may hold values from 0 to 15, all different within a row; in each aligned block of 128 rows (0 to 127, 128 to 255, ..., all dimensions but the last counted through in order) at most 32 rows name the same one
- cotangent: bfloat16 [2, 16, 128, 768], P(None, 'expert'), may hold values from -6 to 6
- attn_gain: float32 [2, 768], P('section'), may hold values from 0.1 to 1.9
- query_weight: bfloat16 [2, 768, 768], P('section', None, 'mp'), may hold values from -0.21875 to 0.21875
- key_weight: bfloat16 [2, 768, 768], P('section', None, 'mp'), may hold values from -0.21875 to 0.21875
- value_weight: bfloat16 [2, 768, 768], P('section', None, 'mp'), may hold values from -0.21875 to 0.21875
- out_weight: bfloat16 [2, 768, 768], P('section', 'mp'), may hold values from -0.875 to 0.875
- pos_bias: float32 [2, 32, 12], P('section', None, 'mp'), may hold values from -3 to 3
- ffn_gain: float32 [2, 768], P('section'), may hold values from 0.1 to 1.9
- dense_gate: bfloat16 [768, 3072], P(None, ('section', 'mp')), may hold values from -0.21875 to 0.21875
- dense_up: bfloat16 [768, 3072], P(None, ('section', 'mp')), may hold values from -0.21875 to 0.21875
- dense_down: bfloat16 [3072, 768], P(('section', 'mp')), may hold values from -0.109375 to 0.109375
- router: bfloat16 [768, 16], replicated, may hold values from -0.15625 to 0.15625
- expert_gate: bfloat16 [16, 768, 3072], P('expert', None, ('section', 'mp')), may hold values from -0.21875 to 0.21875
- expert_up: bfloat16 [16, 768, 3072], P('expert', None, ('section', 'mp')), may hold values from -0.21875 to 0.21875
- expert_down: bfloat16 [16, 3072, 768], P('expert', ('section', 'mp')), may hold values from -0.109375 to 0.109375
Outputs:
- block_output: float32 [2, 16, 128, 768], P(None, 'expert')
- input_grad: float32 [2, 16, 128, 768], P(None, 'expert')
- grad_attn_gain: float32 [2, 768], P('section')
- grad_query: float32 [2, 768, 768], P('section', None, 'mp')
- grad_key: float32 [2, 768, 768], P('section', None, 'mp')
- grad_value: float32 [2, 768, 768], P('section', None, 'mp')
- grad_out: float32 [2, 768, 768], P('section', 'mp')
- grad_bias: float32 [2, 32, 12], P('section', None, 'mp')
- grad_ffn_gain: float32 [2, 768], P('section')
- grad_dense_gate: float32 [768, 3072], P(None, ('section', 'mp'))
- grad_dense_up: float32 [768, 3072], P(None, ('section', 'mp'))
- grad_dense_down: float32 [3072, 768], P(('section', 'mp'))
- grad_router: float32 [768, 16], replicated
- grad_expert_gate: float32 [16, 768, 3072], P('expert', None, ('section', 'mp'))
- grad_expert_up: float32 [16, 768, 3072], P('expert', None, ('section', 'mp'))
- grad_expert_down: float32 [16, 3072, 768], P('expert', ('section', 'mp'))
The draws below stay inside these ranges and needn't reach their ends.
Inputs may be any that keep to these rules, and one draw needn't show every extreme that they name: `routes`: each token names two different experts. In the rows of one sequence of one micro-batch (aligned blocks of 128 tokens) no expert is named more than 32 times, a bound that some block reaches. `segments`: within a sequence the numbers never fall; each document (run of equal numbers) has 1 to 64 tokens, and some has exactly 64.
All inputs are finite; a program needn't handle non-finite values.
Results may differ from the reference program's by a relative error of at most 0.025.
Values may be sent and summed in bfloat16 or wider, within the bound.
A program may use at most 128 MiB of HBM per device.

```python
import math
import jax
import jax.numpy as jnp
import numpy as np
from jax import lax

D = 768
H = 12
HD = 64
FF = 3072
BUCKETS = 32
MICRO = 2
SEQ = 128
SEQS = 16
EXPERTS = 16
CAP = 32


def shard_levels(own_key, shape, shards, least, top_value):
    loudness = 1.0
    for axis_at, blocks in shards:
        steps = jax.random.uniform(jax.random.fold_in(jax.random.fold_in(own_key, 6), axis_at), (blocks,), jnp.float32, least / len(shards), top_value / len(shards))
        loudness = loudness * jnp.repeat(jnp.exp(steps), shape[axis_at] // blocks).reshape((-1,) + (1,) * (len(shape) - 1 - axis_at))
    return loudness


def length_profile(number_of, total, reach, lean):
    weights = [(1 << 20) // math.isqrt(grade ** lean) + 1 for grade in range(2, number_of + 1)]
    surplus, given = total - reach - (number_of - 1), [1] * (number_of - 1)
    while surplus > 0:
        candidates = [i for i in range(number_of - 1) if given[i] < reach]
        whole, left = sum([weights[i] for i in candidates]), surplus
        for i in candidates:
            extra = min(reach - given[i], max(1, left * weights[i] // whole), surplus)
            given[i] = given[i] + extra
            surplus = surplus - extra
    return np.array([reach] + given)


def uneven(key, amount, total, most, slope):
    if amount == 2:
        one = jax.random.randint(key, (), max(1, total - most), min(most, total - 1) + 1)
        return jnp.stack([one, total - one])
    lengths = jnp.asarray(length_profile(amount, total, most, slope), jnp.int32)
    pairs = (amount - 1) // 2
    giver, taker = lengths[1:1 + 2 * pairs:2], lengths[2:2 + 2 * pairs:2]
    room = jnp.minimum(giver - 1, most - taker)
    shifted = jax.random.randint(jax.random.fold_in(key, 1), (pairs,), 0, 1 << 20) % (room + 1)
    lengths = lengths.at[1:1 + 2 * pairs:2].set(giver - shifted).at[2:2 + 2 * pairs:2].set(taker + shifted)
    return lengths[jax.random.permutation(jax.random.fold_in(key, 2), amount)]


def assign_block(stream_key, own, number, rows, count, top, bound, slope):
    sequence = jax.random.permutation(stream_key, count)
    crowded, usual = shares(count, rows * top, bound, slope, True), shares(count, rows * top, bound, slope, False)
    places = jnp.arange(count)

    def named(tallies, rotation):
        used = int((tallies > 0).sum())
        fixed = max(1, used // 4)
        shifted = fixed + (places - fixed + rotation * (used - fixed)) % max(1, count - fixed)
        return jnp.zeros((count,), jnp.int32).at[sequence[jnp.where(places < fixed, places, shifted)]].set(jnp.asarray(tallies, jnp.int32))

    tallies = jnp.where(number % 4 == 0, named(crowded, number // 4), named(usual, number - number // 4 - 1))
    mixed = jax.random.permutation(jax.random.fold_in(own, 3), count)
    donor, receiver = mixed[0:count // 2 * 2:2], mixed[1:count // 2 * 2:2]
    room = jnp.minimum(tallies[donor] - 1, bound - tallies[receiver]) // 2
    room = jnp.where((donor == sequence[0]) | (receiver == sequence[0]) | (tallies[receiver] == 0), 0, jnp.maximum(room, 0))
    shifted = jax.random.randint(jax.random.fold_in(own, 4), (count // 2,), 0, 1 << 20) % (room + 1)
    tallies = tallies.at[donor].add(-shifted).at[receiver].add(shifted)
    items = jnp.searchsorted(jnp.cumsum(tallies), jnp.arange(rows * top), side="right").astype(jnp.int32)
    table = items.reshape(top, rows).T
    table = table[jax.random.permutation(jax.random.fold_in(own, 1), rows)]
    rotation = jax.random.randint(jax.random.fold_in(own, 2), (rows, 1), 0, top)
    return jnp.take_along_axis(table, (jnp.arange(top)[None, :] + rotation) % top, axis=1)


def shares(number_of, total, most, skew, full):
    portions = [(1 << 20) // math.isqrt(standing ** skew) + 1 for standing in range(1, number_of + 1)]
    largest = most if full else min(most, max(-(-total // number_of), total * portions[0] // sum(portions)))
    least = 1 if total - largest >= number_of - 1 else 0
    given, rest = [largest] + [least] * (number_of - 1), total - largest - least * (number_of - 1)
    while rest > 0:
        candidates = [i for i in range(1, number_of) if given[i] < largest] or [i for i in range(1, number_of) if given[i] < most]
        pool, remaining = sum([portions[i] for i in candidates]), rest
        for i in candidates:
            extra = min(most - given[i], max(1, remaining * portions[i] // pool), rest)
            given[i] = given[i] + extra
            rest = rest - extra
    return np.array(given)


def normal_values(stream_key, extent, scale, most, split=(), kind=jnp.bfloat16):
    level = shard_levels(stream_key, extent, split, -0.22, 0.18) if split else 1.0
    values = jax.random.normal(stream_key, extent, jnp.float32) * scale * level
    return jnp.minimum(jnp.maximum(values, -most), most).astype(kind)


def setup_inputs(seed: int = 0) -> dict:
    seeds = jax.random.split(jax.random.key(seed), 19)
    block_input = normal_values(seeds[0], (MICRO, SEQS, SEQ, D), 1.0, 6.0, ((1, 16),))
    segments = jax.vmap(lambda own: jnp.searchsorted(jnp.cumsum(uneven(own, 4, SEQ, SEQ // 2, 1)), jnp.arange(SEQ), side="right"))(jax.random.split(seeds[1], MICRO * SEQS)).reshape((MICRO, SEQS, SEQ)).astype(jnp.int32)
    routes_keys = jax.random.split(jax.random.fold_in(seeds[2], 1), MICRO * SEQS * SEQ // SEQ)
    routes_turns = jax.random.permutation(jax.random.fold_in(seeds[2], 3), MICRO * SEQS * SEQ // SEQ)
    routes = jax.vmap(lambda own, number: assign_block(jax.random.fold_in(seeds[2], 2), own, number, SEQ, EXPERTS, 2, CAP, 1))(routes_keys, routes_turns).reshape((MICRO, SEQS, SEQ, 2))
    cotangent = normal_values(seeds[3], (MICRO, SEQS, SEQ, D), 1.0, 6.0, ((1, 16),))
    attn_gain = jnp.clip(1.0 + 0.18 * jax.random.normal(seeds[4], (2, D), jnp.float32), 0.1, 1.9)
    query_weight = normal_values(seeds[5], (2, D, H * HD), D ** -0.5, 0.21875, ((0, 2), (2, 4)))
    key_weight = normal_values(seeds[6], (2, D, H * HD), D ** -0.5, 0.21875, ((0, 2), (2, 4)))
    value_weight = normal_values(seeds[7], (2, D, H * HD), D ** -0.5, 0.21875, ((0, 2), (2, 4)))
    out_weight = normal_values(seeds[8], (2, H * HD, D), (H * HD // 16) ** -0.5, 0.875, ((0, 2), (1, 4)))
    pos_bias = normal_values(seeds[9], (2, BUCKETS, H), 0.5, 3.0, ((0, 2), (2, 4)), jnp.float32)
    ffn_gain = jnp.clip(1.0 + 0.18 * jax.random.normal(seeds[10], (2, D), jnp.float32), 0.1, 1.9)
    dense_gate = normal_values(seeds[11], (D, FF), D ** -0.5, 0.21875, ((1, 8),))
    dense_up = normal_values(seeds[12], (D, FF), D ** -0.5, 0.21875, ((1, 8),))
    dense_down = normal_values(seeds[13], (FF, D), FF ** -0.5, 0.109375, ((0, 8),))
    router = normal_values(seeds[14], (D, EXPERTS), (2 * D) ** -0.5, 0.15625)
    expert_gate = normal_values(seeds[15], (EXPERTS, D, FF), D ** -0.5, 0.21875, ((0, 16), (2, 8)))
    expert_up = normal_values(seeds[16], (EXPERTS, D, FF), D ** -0.5, 0.21875, ((0, 16), (2, 8)))
    expert_down = normal_values(seeds[17], (EXPERTS, FF, D), FF ** -0.5, 0.109375, ((0, 16), (1, 8)))
    return {"block_input": block_input, "segments": segments, "routes": routes, "cotangent": cotangent, "attn_gain": attn_gain, "query_weight": query_weight, "key_weight": key_weight, "value_weight": value_weight, "out_weight": out_weight, "pos_bias": pos_bias, "ffn_gain": ffn_gain, "dense_gate": dense_gate, "dense_up": dense_up, "dense_down": dense_down, "router": router, "expert_gate": expert_gate, "expert_up": expert_up, "expert_down": expert_down}


EPSILON = 1e-06
NEGATIVE = -1e+30

@jax.custom_vjp
def low(v):
    return lax.optimization_barrier(v.astype(jnp.bfloat16)).astype(jnp.float32)

@jax.custom_vjp
def low_back(v):
    return v

def low_keep(v):
    return (low(v), None)

def low_pass(kept, grad):
    return (grad,)

def back_keep(v):
    return (v, None)

def back_low(kept, grad):
    return (low(grad),)
low.defvjp(low_keep, low_pass)
low_back.defvjp(back_keep, back_low)

def bucket_limits(count):
    exact = count // 2
    limits = []
    for level in range(1, count):
        if level < exact:
            limits.append(level)
        else:
            distance = exact
            while min(count - 1, exact + int(np.floor(np.log(distance / exact) / np.log(128.0 / exact) * exact))) < level:
                distance += 1
            limits.append(distance)
    return limits

def bucket_hot(length, count):
    rows = lax.broadcasted_iota(jnp.int32, (length, length), 0)
    cols = lax.broadcasted_iota(jnp.int32, (length, length), 1)
    distance = rows - cols
    bucket = jnp.zeros((length, length), jnp.int32)
    for limit in bucket_limits(count):
        bucket = bucket + (distance >= limit).astype(jnp.int32)
    levels = lax.broadcasted_iota(jnp.int32, (length, length, count), 2)
    return (bucket[:, :, None] == levels).astype(jnp.float32)

def rms_norm(values_in, gain_row):
    return values_in * lax.rsqrt(lax.optimization_barrier(jnp.mean(values_in * values_in, axis=-1, keepdims=True)) + EPSILON) * gain_row

def gated_hidden(gate_in, up_in):
    return jax.nn.gelu(gate_in, approximate=True) * up_in

def matrix_product(left, right):
    return jnp.einsum('bsd,df->bsf', left, right, precision=lax.Precision.HIGHEST)

def attention(rows_in, doc_ids, weight_query, weight_key, weight_value, weight_out, bias_table, gain_row, position_hot):
    batch, length, width = rows_in.shape
    head_count = bias_table.shape[1]
    head_size = weight_query.shape[1] // head_count
    normed = low(rms_norm(rows_in, gain_row))

    def project(weight_in):
        return low(low_back(matrix_product(normed, weight_in))).reshape(batch, length, head_count, head_size)
    query_heads, key_heads, value_heads = (project(weight_query), project(weight_key), project(weight_value))
    position_bias = jnp.einsum('qkb,bh->hqk', position_hot, bias_table, precision=lax.Precision.HIGHEST)
    scores = jnp.einsum('bqhe,bkhe->bhqk', query_heads, key_heads, precision=lax.Precision.HIGHEST) * head_size ** (-0.5) + position_bias[None]
    rows = lax.broadcasted_iota(jnp.int32, (length, length), 0)
    cols = lax.broadcasted_iota(jnp.int32, (length, length), 1)
    doc_mask = (cols <= rows)[None] & (doc_ids[:, :, None] == doc_ids[:, None, :])
    scores = low_back(jnp.where(doc_mask[:, None], scores, NEGATIVE))
    attn_probs = low(jax.nn.softmax(scores, axis=-1))
    head_mix = jnp.einsum('bhqk,bkhe->bqhe', attn_probs, value_heads, precision=lax.Precision.HIGHEST)
    head_mix = low(low_back(head_mix)).reshape(batch, length, head_count * head_size)
    return rows_in + low_back(matrix_product(head_mix, weight_out))

def dense_block(hidden_in, gain_row, gate_dense, up_dense, down_dense):
    normed = low(rms_norm(hidden_in, gain_row))
    gate_pre = low_back(matrix_product(normed, gate_dense))
    up_pre = low_back(matrix_product(normed, up_dense))
    dense_hid = low(gated_hidden(gate_pre, up_pre))
    return hidden_in + low_back(matrix_product(dense_hid, down_dense))

def mixture(hidden_in, route_ids, gain_row, router_weight, gate_expert, up_expert, down_expert):
    seq_count, length, width = hidden_in.shape
    expert_count = router_weight.shape[1]
    normed = low(rms_norm(hidden_in, gain_row))
    logits = matrix_product(normed, router_weight)
    expert_ids = jnp.arange(expert_count, dtype=jnp.int32)
    route_hot = (route_ids[..., None] == expert_ids).astype(jnp.float32)
    chosen = lax.optimization_barrier(jnp.sum(route_hot * logits[:, :, None, :], axis=-1))
    gate_probs = jax.nn.softmax(chosen, axis=-1)
    flat_ids = route_ids.reshape(seq_count, length * 2)
    flat_hot = (flat_ids[..., None] == expert_ids).astype(jnp.int32)
    ranks = (jnp.cumsum(flat_hot, axis=1).astype(jnp.int32) - 1) * flat_hot
    rank_sel = lax.optimization_barrier(jnp.sum(ranks, axis=-1)).astype(jnp.int32)
    source = lax.broadcasted_iota(jnp.int32, (seq_count, length * 2), 0)
    slot_ids = (flat_ids * (seq_count * CAP) + source * CAP + rank_sel).reshape(-1)
    rows = jnp.broadcast_to(normed[:, :, None, :], (seq_count, length, 2, width)).reshape(-1, width)
    buffer = jnp.zeros((expert_count * seq_count * CAP, width), normed.dtype).at[slot_ids].set(rows)
    buffer = buffer.reshape(expert_count, seq_count * CAP, width)
    gate_pre = low_back(jnp.einsum('erd,edf->erf', buffer, gate_expert, precision=lax.Precision.HIGHEST))
    up_pre = low_back(jnp.einsum('erd,edf->erf', buffer, up_expert, precision=lax.Precision.HIGHEST))
    expert_hidden_rows = low(gated_hidden(gate_pre, up_pre))
    expert_out = jnp.einsum('erf,efd->erd', expert_hidden_rows, down_expert, precision=lax.Precision.HIGHEST).reshape(-1, width)
    picked = low_back(expert_out[slot_ids].reshape(seq_count, length, 2, width))
    return hidden_in + lax.optimization_barrier(jnp.sum(gate_probs[..., None] * picked, axis=2))

def reference(block_input, segments, routes, cotangent, attn_gain, query_weight, key_weight, value_weight, out_weight, pos_bias, ffn_gain, dense_gate, dense_up, dense_down, router, expert_gate, expert_up, expert_down):
    position_hot = bucket_hot(SEQ, BUCKETS)

    def forward(inputs, gain_attn, weight_query, weight_key, weight_value, weight_out, bias_table, gain_ffn, gate_dense, up_dense, down_dense, router_weight, gate_expert, up_expert, down_expert):

        def layer_one(pieces):
            rows_in, doc_ids = pieces
            hidden_in = attention(rows_in, doc_ids, weight_query[0], weight_key[0], weight_value[0], weight_out[0], bias_table[0], gain_attn[0], position_hot)
            return dense_block(hidden_in, gain_ffn[0], gate_dense, up_dense, down_dense)

        def layer_two(pieces):
            rows_in, doc_ids, route_ids = pieces
            hidden_in = attention(rows_in, doc_ids, weight_query[1], weight_key[1], weight_value[1], weight_out[1], bias_table[1], gain_attn[1], position_hot)
            return mixture(hidden_in, route_ids, gain_ffn[1], router_weight, gate_expert, up_expert, down_expert)
        middle = lax.map(jax.checkpoint(layer_one), (inputs, segments))
        return lax.map(jax.checkpoint(layer_two), (middle, segments, routes))
    floats = [array_in.astype(jnp.float32) for array_in in (block_input, attn_gain, query_weight, key_weight, value_weight, out_weight, pos_bias, ffn_gain, dense_gate, dense_up, dense_down, router, expert_gate, expert_up, expert_down)]
    result, backward = jax.vjp(forward, *floats)
    grads = backward(cotangent.astype(jnp.float32))
    return (result, grads[0], grads[1], grads[2], grads[3], grads[4], grads[5], grads[6], grads[7], grads[8], grads[9], grads[10], grads[11], grads[12], grads[13], grads[14])
```

```python
import jax
import jax.numpy as jnp
import numpy as np
from jax import lax
from jax.sharding import PartitionSpec as P

EPSILON = 1e-06
NEGATIVE = -1e30
GROUP = ("section", "mp")


def bucket_limits(count):
    exact = count // 2
    limits = []
    for level in range(1, count):
        if level < exact:
            limits.append(level)
        else:
            distance = exact
            while (
                min(
                    count - 1,
                    exact + int(np.floor(np.log(distance / exact) / np.log(128.0 / exact) * exact)),
                )
                < level
            ):
                distance += 1
            limits.append(distance)
    return limits


def bucket_hot(length, count):
    rows = lax.broadcasted_iota(jnp.int32, (length, length), 0)
    cols = lax.broadcasted_iota(jnp.int32, (length, length), 1)
    distance = rows - cols
    bucket = jnp.zeros((length, length), jnp.int32)
    for limit in bucket_limits(count):
        bucket = bucket + (distance >= limit).astype(jnp.int32)
    levels = lax.broadcasted_iota(jnp.int32, (length, length, count), 2)
    return (bucket[:, :, None] == levels).astype(jnp.float32)


def mm(left, right):
    return jnp.dot(left, right, preferred_element_type=jnp.float32)


def low(value):
    return value.astype(jnp.bfloat16)


def spread_sum(partial):
    devices = lax.axis_size(GROUP)
    rows, width = partial.shape
    pieces = low(partial).reshape(devices, rows // devices, width)
    pieces = lax.all_to_all(pieces, GROUP, 0, 0, tiled=True)
    return pieces.astype(jnp.float32).sum(axis=0)


def collect(rows):
    devices = lax.axis_size(GROUP)
    copies = jnp.broadcast_to(rows[None], (devices, *rows.shape))
    return lax.all_to_all(copies, GROUP, 0, 0, tiled=True).reshape(-1, rows.shape[1])


def inverse_rms(rows):
    return lax.rsqrt(jnp.mean(rows * rows, axis=-1, keepdims=True) + EPSILON)


def normed(rows, gain):
    return low(rows * inverse_rms(rows) * gain[None])


def normed_back(rows, gain, grad):
    rho = inverse_rms(rows)
    scaled = grad * gain[None]
    back = scaled * rho - rows * (rho * rho * rho) * jnp.mean(scaled * rows, axis=-1, keepdims=True)
    return back, jnp.sum(grad * rows * rho, axis=0)


def gelu_parts(a):
    inner = 0.7978845608028654 * (a + 0.044715 * a * a * a)
    t = jnp.tanh(inner)
    value = 0.5 * a * (1.0 + t)
    slope = 0.5 * (1.0 + t) + 0.5 * a * (1.0 - t * t) * 0.7978845608028654 * (1.0 + 3 * 0.044715 * a * a)
    return value, slope


def attention(rows_in, wq, wk, wv, wo, mask, bias, micro, heads):
    rows = rows_in.shape[0]
    size = wq.shape[1] // heads

    def split(w):
        return low(mm(rows_in, w)).reshape(micro, rows // micro, heads, size)

    q, k, v = split(wq), split(wk), split(wv)
    scores = jnp.einsum("mqhe,mkhe->mhqk", q, k, preferred_element_type=jnp.float32) * size**-0.5
    scores = jnp.where(mask[:, None], scores + bias[None], NEGATIVE)
    top = jnp.max(scores, axis=-1, keepdims=True)
    e = jnp.exp(scores - top)
    probs = e / jnp.sum(e, axis=-1, keepdims=True)
    o = jnp.einsum("mhqk,mkhe->mqhe", low(probs), v, preferred_element_type=jnp.float32)
    o = low(o).reshape(rows, -1)
    return mm(o, wo), (rows_in, q, k, v, probs, o)


def attention_back(state, grad, wq, wk, wv, wo, hot):
    rows_in, q, k, v, probs, o = state
    rows = rows_in.shape[0]
    size = q.shape[-1]
    g_out = mm(o.T, grad)
    do = low(mm(grad, wo.T)).reshape(q.shape)
    dv = low(jnp.einsum("mhqk,mqhe->mkhe", low(probs), do, preferred_element_type=jnp.float32))
    dp = jnp.einsum("mqhe,mkhe->mhqk", do, v, preferred_element_type=jnp.float32)
    ds = low(probs * (dp - jnp.sum(dp * probs, axis=-1, keepdims=True)))
    g_bias = jnp.einsum("hqk,qkb->bh", ds.astype(jnp.float32).sum(axis=0), hot, precision=lax.Precision.HIGHEST)
    dq = low(jnp.einsum("mhqk,mkhe->mqhe", ds, k, preferred_element_type=jnp.float32) * size**-0.5)
    dk = low(jnp.einsum("mhqk,mqhe->mkhe", ds, q, preferred_element_type=jnp.float32) * size**-0.5)
    dq, dk, dv = (t.reshape(rows, -1) for t in (dq, dk, dv))
    n_t = rows_in.T
    dn = mm(dq, wq.T) + mm(dk, wk.T) + mm(dv, wv.T)
    return dn, (mm(n_t, dq), mm(n_t, dk), mm(n_t, dv), g_out, g_bias)


def shards(
    block_input,
    segments,
    routes,
    cotangent,
    attn_gain,
    query_weight,
    key_weight,
    value_weight,
    out_weight,
    pos_bias,
    ffn_gain,
    dense_gate,
    dense_up,
    dense_down,
    router,
    expert_gate,
    expert_up,
    expert_down,
):
    section = lax.axis_index("section")
    first = section == 0
    place = section * lax.axis_size("mp") + lax.axis_index("mp")
    devices = lax.axis_size(GROUP)
    micro, _, length, width = block_input.shape
    experts = router.shape[1]
    cap = 4 * length // experts
    heads = pos_bias.shape[2]
    rows = micro * length
    part = rows // devices
    wq, wk, wv, wo = query_weight[0], key_weight[0], value_weight[0], out_weight[0]
    gate_w, up_w, down_w = expert_gate[0], expert_up[0], expert_down[0]

    def own_rows(whole):
        return lax.dynamic_slice_in_dim(whole, place * part, part, axis=0)

    x = block_input.reshape(rows, width)
    gy = cotangent.reshape(rows, width)
    gains = lax.all_gather(jnp.concatenate([attn_gain, ffn_gain]), "section")
    hot = bucket_hot(length, pos_bias.shape[1])
    bias = jnp.einsum("qkb,bh->hqk", hot, pos_bias[0], precision=lax.Precision.HIGHEST)
    docs = segments[:, 0]
    causal = lax.broadcasted_iota(jnp.int32, (length, length), 1) <= lax.broadcasted_iota(
        jnp.int32, (length, length), 0
    )
    mask = causal[None] & (docs[:, :, None] == docs[:, None, :])

    x_f = x.astype(jnp.float32)
    term, state_one = attention(normed(x_f, gains[0, 0]), wq, wk, wv, wo, mask, bias, micro, heads)
    h1 = own_rows(x_f) + spread_sum(jnp.where(first, term, 0.0))
    r1 = collect(normed(h1, gains[0, 1]))
    a1, u1 = mm(r1, dense_gate), mm(r1, dense_up)
    value1, slope1 = gelu_parts(a1)
    hid1 = low(value1 * u1)
    y1 = h1 + spread_sum(mm(hid1, dense_down))
    n2 = collect(normed(y1, gains[1, 0]))
    term, state_two = attention(n2, wq, wk, wv, wo, mask, bias, micro, heads)
    h2 = y1 + spread_sum(jnp.where(first, 0.0, term))
    r2_own = normed(h2, gains[1, 1])
    r2 = collect(r2_own)
    route = routes.reshape(micro, length, 2)
    ids = jnp.arange(experts, dtype=jnp.int32)
    route_hot = (route[..., None] == ids).astype(jnp.float32)
    logits = mm(r2, router).reshape(micro, length, experts)
    gates = jax.nn.softmax(jnp.sum(route_hot * logits[:, :, None], axis=-1), axis=-1)
    named = route_hot.sum(axis=2)
    rank = jnp.cumsum(named, axis=1) - named
    slots = jnp.arange(cap, dtype=jnp.float32)
    pick = (route_hot.transpose(0, 2, 3, 1)[:, :, :, None] > 0) & (
        rank.transpose(0, 2, 1)[:, None, :, None] == slots[:, None]
    )
    pick = low(pick)
    both = pick.sum(axis=1)
    gate_slot = jnp.einsum("mceki,mic->emk", pick.astype(jnp.float32), gates, precision=lax.Precision.HIGHEST)
    x_send = jnp.einsum("meki,mid->emkd", both, r2.reshape(micro, length, width))
    g_send = jnp.einsum(
        "meki,mid->emkd", both, gy.reshape(micro, length, width), preferred_element_type=jnp.float32
    )
    g_send = low(g_send * gate_slot[..., None])
    sent = jnp.concatenate([x_send, g_send], axis=-1).reshape(experts, micro * cap, 2 * width)
    arrived = lax.all_to_all(sent, "expert", 0, 0, tiled=True).reshape(-1, 2 * width)
    xr, dout = arrived[:, :width], arrived[:, width:]
    a, u = mm(xr, gate_w), mm(xr, up_w)
    value, slope = gelu_parts(a)
    hid = low(value * u)
    dhid = mm(dout, down_w.T)
    da, du = low(dhid * u * slope), low(dhid * value)
    e_out = low(mm(hid, down_w))
    d_x = low(mm(da, gate_w.T) + mm(du, up_w.T))
    back = jnp.concatenate([e_out, d_x], axis=-1).reshape(experts, micro * cap, 2 * width)
    back = lax.all_to_all(back, "expert", 0, 0, tiled=True).reshape(experts, micro, cap, 2 * width)
    g_expert = (mm(xr.T, da), mm(xr.T, du), mm(hid.T, dout))
    chosen = jnp.einsum(
        "mceki,emkd->cmid", pick, back[..., :width], preferred_element_type=jnp.float32
    ).reshape(2, rows, width)
    d_rows = jnp.einsum(
        "meki,emkd->mid", both, back[..., width:], preferred_element_type=jnp.float32
    ).reshape(rows, width)
    flat_gates = gates.reshape(rows, 2)
    moe = flat_gates[:, :1] * chosen[0] + flat_gates[:, 1:] * chosen[1]
    gate_terms = jnp.sum(chosen * gy.astype(jnp.float32)[None], axis=-1).T
    gate_terms = jnp.pad(gate_terms, ((0, 0), (0, 126)))
    summed = spread_sum(jnp.concatenate([moe, d_rows, gate_terms], axis=-1))
    out_own = h2 + summed[:, :width]
    block_output = collect(out_own)
    gate_own = own_rows(flat_gates)
    gate_grad = summed[:, 2 * width : 2 * width + 2]
    d_sel = gate_own * (gate_grad - jnp.sum(gate_own * gate_grad, axis=-1, keepdims=True))
    d_logits = jnp.sum(d_sel[:, :, None] * own_rows(route_hot.reshape(rows, 2, experts)), axis=1)
    g_router = jnp.dot(r2_own.astype(jnp.float32).T, d_logits, precision=lax.Precision.HIGHEST)
    dr2 = summed[:, width : 2 * width] + jnp.dot(
        d_logits, router.astype(jnp.float32).T, precision=lax.Precision.HIGHEST
    )
    back2, g_ffn2 = normed_back(h2, gains[1, 1], dr2)
    dh2 = own_rows(gy).astype(jnp.float32) + back2
    dn2, grads_two = attention_back(state_two, collect(low(dh2)), wq, wk, wv, wo, hot)
    back2, g_attn2 = normed_back(y1, gains[1, 0], spread_sum(jnp.where(first, 0.0, dn2)))
    gy1 = dh2 + back2
    dout1 = collect(low(gy1))
    dhid1 = mm(dout1, dense_down.T)
    da1, du1 = low(dhid1 * u1 * slope1), low(dhid1 * value1)
    dr1 = spread_sum(mm(da1, dense_gate.T) + mm(du1, dense_up.T))
    g_dense = (mm(r1.T, da1), mm(r1.T, du1), mm(hid1.T, dout1))
    back1, g_ffn1 = normed_back(h1, gains[0, 1], dr1)
    dh1 = gy1 + back1
    dn1, grads_one = attention_back(state_one, collect(low(dh1)), wq, wk, wv, wo, hot)
    back1, g_attn1 = normed_back(own_rows(x_f), gains[0, 0], spread_sum(jnp.where(first, dn1, 0.0)))
    input_grad = collect(low(dh1 + back1)).astype(jnp.float32)
    grads = jax.tree.map(lambda one, two: jnp.where(first, one, two), grads_one, grads_two)
    everyone = ("section", "expert", "mp")
    g_gains = jnp.stack([jnp.stack([g_attn1, g_attn2]), jnp.stack([g_ffn1, g_ffn2])])
    g_gains, g_router = lax.psum((g_gains, g_router), everyone)
    g_own = lax.dynamic_index_in_dim(g_gains, section, axis=1)
    grads, g_dense = jax.tree.map(
        lambda a: a.astype(jnp.float32), lax.psum(jax.tree.map(low, (grads, g_dense)), "expert")
    )
    return (
        block_output.reshape(block_input.shape),
        input_grad.reshape(block_input.shape),
        g_own[0],
        grads[0][None],
        grads[1][None],
        grads[2][None],
        grads[3][None],
        grads[4][None],
        g_own[1],
        *g_dense,
        g_router,
        *(g[None] for g in g_expert),
    )


def solution(mesh):
    placed = (
        P(None, "expert", None, None),
        P(None, "expert", None),
        P(None, "expert", None, None),
        P(None, "expert", None, None),
        P("section", None),
        P("section", None, "mp"),
        P("section", None, "mp"),
        P("section", None, "mp"),
        P("section", "mp", None),
        P("section", None, "mp"),
        P("section", None),
        P(None, ("section", "mp")),
        P(None, ("section", "mp")),
        P(("section", "mp"), None),
        P(),
        P("expert", None, ("section", "mp")),
        P("expert", None, ("section", "mp")),
        P("expert", ("section", "mp"), None),
    )
    return jax.shard_map(
        shards,
        mesh=mesh,
        in_specs=placed,
        out_specs=(
            P(None, "expert", None, None),
            P(None, "expert", None, None),
            P("section", None),
            P("section", None, "mp"),
            P("section", None, "mp"),
            P("section", None, "mp"),
            P("section", "mp", None),
            P("section", None, "mp"),
            P("section", None),
            P(None, ("section", "mp")),
            P(None, ("section", "mp")),
            P(("section", "mp"), None),
            P(),
            P("expert", None, ("section", "mp")),
            P("expert", None, ("section", "mp")),
            P("expert", ("section", "mp"), None),
        ),
        check_vma=False,
    )
```

```python
import functools

import jax
import jax.numpy as jnp
import numpy as np
from jax import lax
from jax.experimental import pallas as pl
from jax.experimental.pallas import tpu as pltpu
from jax.sharding import PartitionSpec as P

EPSILON = 1e-06
NEGATIVE = -1e30
BF16, F32 = jnp.bfloat16, jnp.float32
MESH = pl.DeviceIdType.MESH
HIGHEST = lax.Precision.HIGHEST

GAINS, TERM1, ROWS1, DENSE, ROWS2, TERM2, ROWS3, MOE, OUT, GRAD2, BACK2 = range(11)
GRAD1, BACK1, GRAD0, BACK0, INPUT, SMALL_A, SMALL_A2, SMALL_B, SMALL_B2 = range(11, 20)
DISPATCH, FORWARD, CORE, RETURN = 20, 24, 28, 32
DENSE_RS, DENSE_AG, ATTN_RS, ATTN_AG = 33, 34, 35, 36
SEMAPHORES = 37


def bucket_limits(count):
    exact = count // 2
    limits = []
    for level in range(1, count):
        if level < exact:
            limits.append(level)
        else:
            distance = exact
            while (
                min(
                    count - 1,
                    exact + int(np.floor(np.log(distance / exact) / np.log(128.0 / exact) * exact)),
                )
                < level
            ):
                distance += 1
            limits.append(distance)
    return limits


def dot(left, right, dims, precision=None):
    return lax.dot_general(
        left, right, (((dims[0],), (dims[1],)), ((), ())), precision=precision, preferred_element_type=F32
    )


def nn(left, right, precision=None):
    return dot(left, right, (1, 0), precision)


def nt(left, right, precision=None):
    return dot(left, right, (1, 1), precision)


def tn(left, right, precision=None):
    return dot(left, right, (0, 0), precision)


def low(value):
    return value.astype(BF16)


def full(value):
    return value.astype(F32)


def inverse_rms(rows):
    return lax.rsqrt(jnp.mean(rows * rows, axis=-1, keepdims=True) + EPSILON)


def normed(rows, gain):
    return low(rows * inverse_rms(rows) * gain)


def normed_back(rows, gain, grad):
    rho = inverse_rms(rows)
    scaled = grad * gain
    back = scaled * rho - rows * (rho * rho * rho) * jnp.mean(scaled * rows, axis=-1, keepdims=True)
    return back, jnp.sum(grad * rows * rho, axis=0, keepdims=True)


def gelu_parts(a):
    t = jnp.tanh(0.7978845608028654 * (a + 0.044715 * a * a * a))
    half = 0.5 * (1.0 + t)
    slope = half + 0.5 * a * (1.0 - t * t) * (0.7978845608028654 * (1.0 + 0.134145 * a * a))
    return a * half, slope


def kernel(
    c,
    x_ref,
    gy_ref,
    ints_ref,
    routes_ref,
    attn_gain_ref,
    ffn_gain_ref,
    table_ref,
    wq_ref,
    wk_ref,
    wv_ref,
    wo_ref,
    dense_gate_ref,
    dense_up_ref,
    dense_down_ref,
    router_ref,
    gate_ref,
    up_ref,
    down_ref,
    out_ref,
    input_ref,
    attn_ref,
    dense_ref,
    ge_gate_ref,
    ge_up_ref,
    ge_down_ref,
    small_ref,
    bias_grad_ref,
    send_sem,
    recv_sem,
    gains,
    bucket,
    bias,
    mask,
    n1,
    qkv,
    probs,
    o,
    do,
    dqkv,
    dsum,
    bias_rows,
    sends,
    recv4,
    recv8,
    rows1,
    rows2,
    rows3,
    grad2,
    grad1,
    grad0,
    chunk,
    hid1,
    gate1,
    up1,
    da1,
    du1,
    pick0,
    pick1,
    gate_slot,
    sx,
    rx,
    hid,
    da,
    du,
    cs,
    cr,
    rt,
    rb,
    moe_send,
    moe_recv,
    small,
    small_send,
    small_recv,
    small2_send,
    small2_recv,
    smallb_send,
    smallb_recv,
    smallb2_send,
    smallb2_recv,
    dense_own,
    dense_recv,
    attn_own,
    attn_recv,
):
    sections, experts, mps = c["section"], c["expert"], c["mp"]
    micro, length, heads, size, cap = c["micro"], c["length"], c["heads"], c["size"], c["cap"]
    width, ff = c["width"], c["ff"]
    group = sections * mps
    rows = micro * length
    part = rows // group
    half = width // sections
    local = heads * size
    scale = size**-0.5
    slots = micro * cap
    s, me, mp = lax.axis_index("section"), lax.axis_index("expert"), lax.axis_index("mp")
    place = s * mps + mp
    own = pl.ds(pl.multiple_of(place * part, part), part)
    mine = pl.ds(pl.multiple_of(s * half, 128), half)
    H2, Y1, H1, GRAD = 0, 1, 2, 3

    def on_expert(k):
        return {"expert": lax.rem(me + k, experts)}

    def in_group(p):
        return {"section": p // mps, "mp": lax.rem(p, mps)}

    def send(src, dst, phase, device, arrival=None):
        pltpu.make_async_remote_copy(
            src_ref=src,
            dst_ref=dst,
            send_sem=send_sem.at[phase],
            recv_sem=recv_sem.at[phase if arrival is None else arrival],
            device_id=device,
            device_id_type=MESH,
        ).start()

    def drain(sem, view):
        pltpu.make_async_copy(view, view, sem).wait()

    def arrived(phase, view):
        drain(recv_sem.at[phase], view)

    def left(phase, view):
        drain(send_sem.at[phase], view)

    barrier = pltpu.get_barrier_semaphore()
    for k in range(1, group):
        pl.semaphore_signal(barrier, inc=1, device_id=in_group(lax.rem(place + k, group)), device_id_type=MESH)
    for k in range(1, experts):
        pl.semaphore_signal(barrier, inc=1, device_id=on_expert(k), device_id_type=MESH)

    gains[s] = jnp.zeros((8, width), F32)
    gains[s, 0:1] = attn_gain_ref[...]
    gains[s, 1:2] = ffn_gain_ref[...]
    row_at = lax.broadcasted_iota(jnp.int32, (length, length), 0)
    col_at = lax.broadcasted_iota(jnp.int32, (length, length), 1)
    found = jnp.zeros((length, length), jnp.int32)
    for limit in bucket_limits(c["buckets"]):
        found = found + jnp.where(row_at - col_at >= limit, 1, 0)
    bucket[...] = found
    for h in range(heads):
        total = jnp.zeros((length, length), F32)
        for b in range(c["buckets"]):
            total = jnp.where(found == b, table_ref[b, h], total)
        bias[h] = total
    for m in range(micro):
        docs = jnp.broadcast_to(full(ints_ref[m : m + 1, :]), (length, length))
        same = (docs == jnp.transpose(docs)) & (col_at <= row_at)
        mask[m] = jnp.where(same, 1.0, 0.0)
    pl.semaphore_wait(barrier, group - 1 + experts - 1)
    send(gains.at[s], gains.at[s], GAINS, {"section": 1 - s})

    def gather_all(buf, phase):
        for k in range(1, group):
            send(buf.at[own], buf.at[own], phase, in_group(lax.rem(place + k, group)))

    def wait_all(buf, phase):
        arrived(phase, buf.at[pl.ds(0, (group - 1) * part)])

    def gather_to(target, buf, phase):
        for k in range(1, mps):
            send(buf.at[own], buf.at[own], phase, {"section": target, "mp": lax.rem(mp + k, mps)})

        @pl.when(s != target)
        def _():
            send(buf.at[own], buf.at[own], phase, {"section": 1 - s})

    def left_to(target, buf, phase):
        @pl.when(s != target)
        def _():
            left(phase, buf.at[pl.ds(0, mps * part)])

        @pl.when(s == target)
        def _():
            left(phase, buf.at[pl.ds(0, (mps - 1) * part)])

    def scatter(src, dst, phase):
        for k in range(1, group):
            p = lax.rem(place + k, group)
            send(src.at[pl.ds(pl.multiple_of(p * part, part), part)], dst.at[place], phase, in_group(p))
        dst[place] = src[own]

    def scatter_from(src, dst, phase):
        for k in range(1, group):
            p = lax.rem(place + k, group)
            send(src.at[pl.ds(pl.multiple_of(p * part, part), part)], dst.at[mp], phase, in_group(p))
        dst[mp] = src[own]

    def wait_from(source, dst, phase):
        @pl.when(s == source)
        def _():
            arrived(phase, dst.at[pl.ds(0, mps - 1)])

        @pl.when(s != source)
        def _():
            arrived(phase, dst)

    def total(ref, first=0, last=None):
        last = ref.shape[0] if last is None else last
        value = full(ref[first])
        for i in range(first + 1, last):
            value = value + full(ref[i])
        return value

    def attention(n_ref, out):
        for t, w in enumerate((wq_ref, wk_ref, wv_ref)):
            qkv[t] = low(nn(n_ref[...], w[...]))
        for m in range(micro):
            r = slice(m * length, (m + 1) * length)
            for h in range(heads):
                lanes = slice(h * size, (h + 1) * size)
                scores = nt(qkv[0, r, lanes], qkv[1, r, lanes]) * scale + bias[h]
                scores = jnp.where(mask[m] > 0, scores, NEGATIVE)
                e = jnp.exp(scores - jnp.max(scores, axis=-1, keepdims=True))
                p = e / jnp.sum(e, axis=-1, keepdims=True)
                probs[m * heads + h] = p
                o[r, lanes] = low(nn(low(p), qkv[2, r, lanes]))
        out[...] = low(nn(o[...], wo_ref[...]))

    def attention_back(g_ref, out):
        do[...] = low(nt(g_ref[...], wo_ref[...]))
        for m in range(micro):
            r = slice(m * length, (m + 1) * length)
            for h in range(heads):
                lanes = slice(h * size, (h + 1) * size)
                d, p = do[r, lanes], probs[m * heads + h]
                q, k, v = (qkv[t, r, lanes] for t in range(3))
                dp = nt(d, v)
                ds = low(p * (dp - jnp.sum(dp * p, axis=-1, keepdims=True)))
                dqkv[r, h * size : (h + 1) * size] = low(nn(ds, k) * scale)
                dqkv[r, local + h * size : local + (h + 1) * size] = low(tn(ds, q) * scale)
                dqkv[r, 2 * local + h * size : 2 * local + (h + 1) * size] = low(tn(low(p), d))
                dsum[h] = full(ds) if m == 0 else dsum[h] + full(ds)
        dn = nt(dqkv[:, 0:local], wq_ref[...]) + nt(dqkv[:, local : 2 * local], wk_ref[...])
        dn = dn + nt(dqkv[:, 2 * local : 3 * local], wv_ref[...])
        out[...] = low(dn)
        return dn

    def attention_weights(n_ref, g_ref):
        attn_own[:, 0 : 3 * local] = low(tn(n_ref[...], dqkv[...]))
        attn_own[:, 3 * local :] = low(tn(g_ref[...], o[...]))
        share(attn_own, attn_recv, ATTN_RS)
        found = bucket[...]
        for h in range(heads):
            held = dsum[h]
            for b in range(c["buckets"]):
                bias_rows[b : b + 1, :] = jnp.sum(jnp.where(found == b, held, 0.0), axis=0, keepdims=True)
            sums = nt(jnp.ones((8, length), F32), bias_rows[...], HIGHEST)
            smallb_send[1 + h : 2 + h, 0 : c["buckets"]] = sums[0:1]

    def piece(ref, p):
        step = width // experts
        at = pl.ds(pl.multiple_of(p * step, 16), step)
        return ref.at[:, at] if len(ref.shape) == 3 else ref.at[at]

    def share(src, dst, phase):
        for k in range(1, experts):
            p = lax.rem(me + k, experts)
            send(piece(src, p), dst.at[me], phase, on_expert(k))
        dst[me] = piece(src, me)[...]

    def hand_back(src, out, phase):
        piece(out, me)[...] = low(total(src))
        for k in range(1, experts):
            send(piece(out, me), piece(out, me), phase, on_expert(k))

    x = full(x_ref[...])
    @pl.when(s == 0)
    def _():
        n1[...] = normed(x, gains[0, 0:1])
        attention(n1, sends.at[0])
        scatter_from(sends.at[0], recv4.at[0], TERM1)

    arrived(GAINS, gains.at[1 - s])
    wait_from(0, recv4.at[0], TERM1)
    h1 = full(x_ref[own]) + total(recv4.at[0])
    chunk[H1] = h1
    rows1[own] = normed(h1, gains[0, 1:2])
    gather_all(rows1, ROWS1)
    wait_all(rows1, ROWS1)
    gate1[...] = nn(rows1[...], dense_gate_ref[...])
    up1[...] = nn(rows1[...], dense_up_ref[...])
    hid1[...] = low(gelu_parts(gate1[...])[0] * up1[...])
    sends[1] = low(nn(hid1[...], dense_down_ref[...]))
    scatter(sends.at[1], recv8.at[0], DENSE)
    arrived(DENSE, recv8.at[0, pl.ds(0, group - 1)])
    y1 = chunk[H1] + total(recv8.at[0])
    chunk[Y1] = y1
    rows2[own] = normed(y1, gains[1, 0:1])
    gather_to(1, rows2, ROWS2)

    @pl.when(s == 1)
    def _():
        wait_all(rows2, ROWS2)
        attention(rows2, sends.at[2])
        scatter_from(sends.at[2], recv4.at[1], TERM2)

    named = []
    before = low(jnp.where(row_at < col_at, 1.0, 0.0))
    expert_at = lax.broadcasted_iota(jnp.int32, (experts, length), 0)
    slot_at = full(lax.broadcasted_iota(jnp.int32, (cap, length), 0))
    for m in range(micro):
        hots = [
            jnp.where(expert_at == ints_ref[micro + 2 * m + ch : micro + 2 * m + ch + 1, :], 1.0, 0.0)
            for ch in range(2)
        ]
        rank = nn(low(hots[0] + hots[1]), before)
        for e in range(experts):
            fit = slot_at == rank[e : e + 1]
            at = slice(e * cap, (e + 1) * cap)
            pick0[m, at] = low(jnp.where(fit, hots[0][e : e + 1], 0.0))
            pick1[m, at] = low(jnp.where(fit, hots[1][e : e + 1], 0.0))
        named.append(hots)

    wait_from(1, recv4.at[1], TERM2)
    h2 = chunk[Y1] + total(recv4.at[1])
    chunk[H2] = h2
    rows3[own] = normed(h2, gains[1, 1:2])
    gather_all(rows3, ROWS3)
    wait_all(rows3, ROWS3)
    logits = nt(router_ref[...], rows3[...])
    for m in range(micro):
        hots = named[m]
        r = slice(m * length, (m + 1) * length)
        here = logits[:, r]
        l0 = jnp.sum(hots[0] * here, axis=0, keepdims=True)
        l1 = jnp.sum(hots[1] * here, axis=0, keepdims=True)
        top = jnp.maximum(l0, l1)
        e0, e1 = jnp.exp(l0 - top), jnp.exp(l1 - top)
        by_expert = (hots[0] * e0 + hots[1] * e1) / (e0 + e1)
        both = pick0[m] + pick1[m]
        for e in range(experts):
            at = slice(e * cap, (e + 1) * cap)
            gate = jnp.sum(full(both[at]) * by_expert[e : e + 1], axis=1, keepdims=True)
            gate_slot[m, at] = jnp.broadcast_to(gate, (cap, 128))
        place_rows = slice(m * cap, (m + 1) * cap)
        out_rows = low(nn(both, rows3[r, mine]))
        sx[:, place_rows, 0:half] = out_rows.reshape(experts, cap, half)
        out_rows = low(nn(both, gy_ref[r, mine]) * gate_slot[m][:, 0:1])
        sx[:, place_rows, half:] = out_rows.reshape(experts, cap, half)
    blocks = 4
    per = experts // blocks
    block = per * slots
    for k in range(1, experts):
        p = lax.rem(me + k, experts)
        send(sx.at[p], rx.at[s, pl.ds(k * slots, slots)], DISPATCH, {"expert": p}, DISPATCH + k // per)
    pltpu.make_async_copy(sx.at[me], rx.at[s, pl.ds(0, slots)], recv_sem.at[DISPATCH]).start()

    def forward(j):
        at = pl.ds(j * block, block)
        arrived(DISPATCH + j, rx.at[s, at])
        send(rx.at[s, at], rx.at[s, at], FORWARD + j, {"section": 1 - s})

    def give_back(j):
        at = pl.ds(j * block, block)
        arrived(CORE + j, cr.at[at])
        rt[at] = low(full(cs[s, at]) + full(cr[at]))
        for k in range(j * per, (j + 1) * per):
            src = rt.at[pl.ds(k * slots, slots)]
            if k == 0:
                pltpu.make_async_copy(src, rb.at[me], recv_sem.at[RETURN]).start()
            else:
                send(src, rb.at[me], RETURN, on_expert(experts - k))

    forward(0)
    for j in range(blocks):
        if j + 1 < blocks:
            forward(j + 1)
        at = pl.ds(j * block, block)
        arrived(FORWARD + j, rx.at[1 - s, at])
        x0, x1 = rx[0, at, 0:half], rx[1, at, 0:half]
        g0, g1 = rx[0, at, half:], rx[1, at, half:]
        a = nn(x0, gate_ref[0:half]) + nn(x1, gate_ref[half:])
        u = nn(x0, up_ref[0:half]) + nn(x1, up_ref[half:])
        d = nt(g0, down_ref[:, 0:half]) + nt(g1, down_ref[:, half:])
        value, slope = gelu_parts(a)
        hid[at] = low(value * u)
        da[at] = low(d * u * slope)
        du[at] = low(d * value)
        for side in range(sections):
            w = slice(side * half, (side + 1) * half)
            cs[side, at, 0:half] = low(nn(hid[at], down_ref[:, w]))
            cs[side, at, half:] = low(nt(da[at], gate_ref[w]) + nt(du[at], up_ref[w]))
        send(cs.at[1 - s, at], cr.at[at], CORE + j, {"section": 1 - s})
        if j > 0:
            give_back(j - 1)
    give_back(blocks - 1)
    for side in range(sections):
        w = slice(side * half, (side + 1) * half)
        ge_gate_ref[w] = low(tn(rx[side, :, 0:half], da[...]))
        ge_up_ref[w] = low(tn(rx[side, :, 0:half], du[...]))
        ge_down_ref[:, w] = low(tn(hid[...], rx[side, :, half:]))
    arrived(RETURN, rb)
    lane = lax.broadcasted_iota(jnp.int32, (length, 128), 1)
    for m in range(micro):
        r = slice(m * length, (m + 1) * length)
        held = rb[:, m * cap : (m + 1) * cap, :].reshape(experts * cap, width)
        scaled = low(full(held[:, 0:half]) * gate_slot[m][:, 0:1])
        first, second = tn(pick0[m], scaled), tn(pick1[m], scaled)
        gy = full(gy_ref[r, mine])
        t0 = jnp.sum(gy * first, axis=-1, keepdims=True)
        t1 = jnp.sum(gy * second, axis=-1, keepdims=True)
        moe_send[r, 0:half] = low(first + second)
        moe_send[r, half : 2 * half] = low(tn(pick0[m] + pick1[m], held[:, half:]))
        moe_send[r, 2 * half :] = low(jnp.where(lane == 0, t0, jnp.where(lane == 1, t1, 0.0)))
    scatter(moe_send, moe_recv, MOE)
    arrived(MOE, moe_recv.at[pl.ds(0, group - 1)])
    lower, upper = total(moe_recv, 0, mps), total(moe_recv, mps, group)
    h2 = chunk[H2]
    out_ref[own, 0:half] = low(h2[:, 0:half] + lower[:, 0:half])
    out_ref[own, half:] = low(h2[:, half:] + upper[:, 0:half])
    terms = lower[:, 2 * half :] + upper[:, 2 * half :]
    t0, t1 = terms[:, 0:1], terms[:, 1:2]
    here = routes_ref[own]
    expert_at = lax.broadcasted_iota(jnp.int32, (part, experts), 1)
    hot0 = jnp.where(expert_at == here[:, 0:1], 1.0, 0.0)
    hot1 = jnp.where(expert_at == here[:, 1:2], 1.0, 0.0)
    logits = nt(rows3[own], router_ref[...])
    l0 = jnp.sum(hot0 * logits, axis=-1, keepdims=True)
    l1 = jnp.sum(hot1 * logits, axis=-1, keepdims=True)
    top = jnp.maximum(l0, l1)
    e0, e1 = jnp.exp(l0 - top), jnp.exp(l1 - top)
    dlogits = hot0 * (t0 - e0 / (e0 + e1) * (t0 + t1)) + hot1 * (t1 - e1 / (e0 + e1) * (t0 + t1))
    dr = jnp.concatenate([lower[:, half : 2 * half], upper[:, half : 2 * half]], axis=1)
    dr = dr + nn(dlogits, full(router_ref[...]), HIGHEST)
    back, gain = normed_back(h2, gains[1, 1:2], dr)
    grad = full(gy_ref[own]) + back
    chunk[GRAD] = grad
    grad2[own] = low(grad)
    gather_to(1, grad2, GRAD2)
    small[...] = jnp.zeros_like(small)
    small[0:1] = gain
    small[8 : 8 + experts] = tn(dlogits, full(rows3[own]), HIGHEST)
    smallb_send[...] = jnp.zeros_like(smallb_send)
    gather_all(out_ref, OUT)

    @pl.when(s == 1)
    def _():
        wait_all(grad2, GRAD2)
        attention_back(grad2, sends.at[3])
        scatter_from(sends.at[3], recv4.at[2], BACK2)
        attention_weights(rows2, grad2)

    wait_from(1, recv4.at[2], BACK2)
    back, gain = normed_back(chunk[Y1], gains[1, 0:1], total(recv4.at[2]))
    small[1:2] = gain
    grad = chunk[GRAD] + back
    chunk[GRAD] = grad
    grad1[own] = low(grad)
    gather_all(grad1, GRAD1)
    wait_all(grad1, GRAD1)
    d = nt(grad1[...], dense_down_ref[...])
    value, slope = gelu_parts(gate1[...])
    da1[...] = low(d * up1[...] * slope)
    du1[...] = low(d * value)
    sends[4] = low(nt(da1[...], dense_gate_ref[...]) + nt(du1[...], dense_up_ref[...]))
    scatter(sends.at[4], recv8.at[1], BACK1)
    dense_own[0] = low(tn(rows1[...], da1[...]))
    dense_own[1] = low(tn(rows1[...], du1[...]))
    for side in range(sections):
        w = slice(side * half, (side + 1) * half)
        dense_own[2, side * ff : (side + 1) * ff] = low(tn(hid1[...], grad1[:, w]))
    share(dense_own, dense_recv, DENSE_RS)
    arrived(BACK1, recv8.at[1, pl.ds(0, group - 1)])
    back, gain = normed_back(chunk[H1], gains[0, 1:2], total(recv8.at[1]))
    small[2:3] = gain
    grad = chunk[GRAD] + back
    chunk[GRAD] = grad
    grad0[own] = low(grad)
    gather_to(0, grad0, GRAD0)
    small_send[...] = low(small[...])
    for k in range(1, group):
        send(small_send, small_recv.at[place], SMALL_A, in_group(lax.rem(place + k, group)))
    small_recv[place] = small_send[...]

    @pl.when(s == 0)
    def _():
        wait_all(grad0, GRAD0)
        dn = attention_back(grad0, sends.at[5])
        scatter_from(sends.at[5], recv4.at[3], BACK0)
        x = full(x_ref[...])
        smallb_send[0:1] = jnp.sum(dn * x * inverse_rms(x), axis=0, keepdims=True)
        attention_weights(n1, grad0)

    for k in range(1, experts):
        send(smallb_send, smallb_recv.at[me], SMALL_B, on_expert(k))
    smallb_recv[me] = smallb_send[...]
    arrived(SMALL_A, small_recv.at[pl.ds(0, group - 1)])
    small2_send[...] = low(total(small_recv))
    for k in range(1, experts):
        send(small2_send, small2_recv.at[me], SMALL_A2, on_expert(k))
    small2_recv[me] = small2_send[...]
    wait_from(0, recv4.at[3], BACK0)
    back, gain = normed_back(full(x_ref[own]), gains[0, 0:1], total(recv4.at[3]))
    input_ref[own] = low(chunk[GRAD] + back)
    gather_all(input_ref, INPUT)
    arrived(DENSE_RS, dense_recv.at[pl.ds(0, experts - 1)])
    hand_back(dense_recv, dense_ref, DENSE_AG)
    arrived(SMALL_B, smallb_recv.at[pl.ds(0, experts - 1)])
    smallb2_send[...] = total(smallb_recv)
    for k in range(1, mps):
        send(smallb2_send, smallb2_recv.at[mp], SMALL_B2, {"mp": lax.rem(mp + k, mps)})
    smallb2_recv[mp] = smallb2_send[...]
    arrived(ATTN_RS, attn_recv.at[pl.ds(0, experts - 1)])
    hand_back(attn_recv, attn_ref, ATTN_AG)
    arrived(SMALL_A2, small2_recv.at[pl.ds(0, experts - 1)])
    summed = total(small2_recv)
    bias_grad_ref[...] = smallb2_send[...]
    arrived(SMALL_B2, smallb2_recv.at[pl.ds(0, mps - 1)])
    gain0 = total(smallb2_recv)[0:1]
    small_ref[...] = summed
    small_ref[0:1] = jnp.where(s == 0, gain0, summed[1:2])
    small_ref[1:2] = jnp.where(s == 0, summed[2:3], summed[0:1])
    wait_all(out_ref, OUT)
    wait_all(input_ref, INPUT)
    others = pl.ds(0, width - width // experts)
    arrived(DENSE_AG, dense_ref.at[:, others])
    arrived(ATTN_AG, attn_ref.at[others])
    left(GAINS, gains.at[s])
    seven = pl.ds(0, (group - 1) * part)
    for phase, ref in ((ROWS1, rows1), (ROWS3, rows3), (OUT, out_ref), (GRAD1, grad1), (INPUT, input_ref)):
        left(phase, ref.at[seven])
    for phase, at in ((DENSE, 1), (BACK1, 4)):
        left(phase, sends.at[at, seven])
    left(MOE, moe_send.at[seven])
    left_to(1, rows2, ROWS2)
    left_to(1, grad2, GRAD2)
    left_to(0, grad0, GRAD0)

    @pl.when(s == 0)
    def _():
        left(TERM1, sends.at[0, seven])
        left(BACK0, sends.at[5, seven])

    @pl.when(s == 1)
    def _():
        left(TERM2, sends.at[2, seven])
        left(BACK2, sends.at[3, seven])

    left(DISPATCH, rx.at[0, pl.ds(0, (experts - 1) * slots)])
    for j in range(blocks):
        left(FORWARD + j, rx.at[0, pl.ds(0, block)])
        left(CORE + j, cr.at[pl.ds(0, block)])
    left(RETURN, rb.at[pl.ds(0, experts - 1)])
    left(SMALL_A, small_recv.at[pl.ds(0, group - 1)])
    left(SMALL_A2, small2_recv.at[pl.ds(0, experts - 1)])
    left(SMALL_B, smallb_recv.at[pl.ds(0, experts - 1)])
    left(SMALL_B2, smallb2_recv.at[pl.ds(0, mps - 1)])
    left(DENSE_RS, dense_recv.at[pl.ds(0, experts - 1)])
    left(DENSE_AG, dense_ref.at[:, others])
    left(ATTN_RS, attn_recv.at[pl.ds(0, experts - 1)])
    left(ATTN_AG, attn_ref.at[others])


def shards(
    block_input,
    segments,
    routes,
    cotangent,
    attn_gain,
    query_weight,
    key_weight,
    value_weight,
    out_weight,
    pos_bias,
    ffn_gain,
    dense_gate,
    dense_up,
    dense_down,
    router,
    expert_gate,
    expert_up,
    expert_down,
):
    micro, _, length, width = block_input.shape
    experts = router.shape[1]
    cap = 4 * length // experts
    buckets, heads = pos_bias.shape[1:]
    local = query_weight.shape[2]
    size = local // heads
    ff = dense_gate.shape[1]
    sections, mps = lax.axis_size("section"), lax.axis_size("mp")
    group = sections * mps
    rows = micro * length
    part = rows // group
    half = width // sections
    slots = micro * cap
    every = experts * slots
    step = width // experts
    c = dict(
        section=sections, expert=experts, mp=mps, micro=micro, length=length, heads=heads, size=size,
        cap=cap, width=width, ff=ff, buckets=buckets,
    )
    ints = jnp.concatenate(
        [segments[:, 0], routes[:, 0].transpose(0, 2, 1).reshape(2 * micro, length)], axis=0
    )
    ints = jnp.pad(ints, ((0, 8 - 3 * micro), (0, 0)))
    vmem = pl.BlockSpec(memory_space=pltpu.VMEM)
    smem = pl.BlockSpec(memory_space=pltpu.SMEM)

    def held(*shape):
        return pltpu.VMEM(shape, BF16)

    def exact(*shape):
        return pltpu.VMEM(shape, F32)

    scratch = [
        pltpu.SemaphoreType.DMA((SEMAPHORES,)),
        pltpu.SemaphoreType.DMA((SEMAPHORES,)),
        exact(sections, 8, width),
        pltpu.VMEM((length, length), jnp.int32),
        exact(heads, length, length),
        exact(micro, length, length),
        held(rows, width),
        held(3, rows, local),
        exact(micro * heads, length, length),
        held(rows, local),
        held(rows, local),
        held(rows, 3 * local),
        exact(heads, length, length),
        exact(buckets, length),
        held(6, rows, width),
        held(4, mps, part, width),
        held(2, group, part, width),
        held(rows, width),
        held(rows, width),
        held(rows, width),
        held(rows, width),
        held(rows, width),
        held(rows, width),
        exact(4, part, width),
        held(rows, ff),
        exact(rows, ff),
        exact(rows, ff),
        held(rows, ff),
        held(rows, ff),
        held(micro, experts * cap, length),
        held(micro, experts * cap, length),
        exact(micro, experts * cap, 128),
        held(experts, slots, 2 * half),
        held(sections, every, 2 * half),
        held(every, ff),
        held(every, ff),
        held(every, ff),
        held(sections, every, 2 * half),
        held(every, 2 * half),
        held(every, 2 * half),
        held(experts, slots, 2 * half),
        held(rows, 2 * half + 128),
        held(group, part, 2 * half + 128),
        exact(32, width),
        held(32, width),
        held(group, 32, width),
        held(32, width),
        held(experts, 32, width),
        exact(8, width),
        exact(experts, 8, width),
        exact(8, width),
        exact(mps, 8, width),
        held(3, width, ff),
        held(experts, 3, step, ff),
        held(width, 4 * local),
        held(experts, step, 4 * local),
    ]
    shape = jax.ShapeDtypeStruct
    block_output, input_grad, attn, dense, ge_gate, ge_up, ge_down, small, bias_grad = pl.pallas_call(
        functools.partial(kernel, c),
        out_shape=(
            shape((rows, width), BF16),
            shape((rows, width), BF16),
            shape((width, 4 * local), BF16),
            shape((3, width, ff), BF16),
            shape((width, ff), BF16),
            shape((width, ff), BF16),
            shape((ff, width), BF16),
            shape((32, width), F32),
            shape((8, width), F32),
        ),
        in_specs=[vmem] * 6 + [smem] + [vmem] * 11,
        out_specs=(vmem,) * 9,
        scratch_shapes=scratch,
        compiler_params=pltpu.CompilerParams(
            collective_id=0, has_side_effects=True, vmem_limit_bytes=60 * 1024 * 1024
        ),
    )(
        block_input.reshape(rows, width),
        cotangent.reshape(rows, width),
        ints,
        routes.reshape(rows, 2),
        attn_gain,
        ffn_gain,
        pos_bias[0],
        query_weight[0],
        key_weight[0],
        value_weight[0],
        out_weight[0],
        dense_gate,
        dense_up,
        dense_down,
        router.T,
        expert_gate[0],
        expert_up[0],
        expert_down[0],
    )
    attn, dense = attn.astype(F32), dense.astype(F32)
    return (
        block_output.astype(F32).reshape(block_input.shape),
        input_grad.astype(F32).reshape(block_input.shape),
        small[0:1],
        attn[None, :, 0:local],
        attn[None, :, local : 2 * local],
        attn[None, :, 2 * local : 3 * local],
        attn[:, 3 * local :].T[None],
        bias_grad[None, 1 : 1 + heads, 0:buckets].transpose(0, 2, 1),
        small[1:2],
        dense[0],
        dense[1],
        jnp.concatenate([dense[2, 0:ff], dense[2, ff:]], axis=1),
        small[8 : 8 + experts].T,
        ge_gate.astype(F32)[None],
        ge_up.astype(F32)[None],
        ge_down.astype(F32)[None],
    )


def solution(mesh):
    placed = (
        P(None, "expert", None, None),
        P(None, "expert", None),
        P(None, "expert", None, None),
        P(None, "expert", None, None),
        P("section", None),
        P("section", None, "mp"),
        P("section", None, "mp"),
        P("section", None, "mp"),
        P("section", "mp", None),
        P("section", None, "mp"),
        P("section", None),
        P(None, ("section", "mp")),
        P(None, ("section", "mp")),
        P(("section", "mp"), None),
        P(),
        P("expert", None, ("section", "mp")),
        P("expert", None, ("section", "mp")),
        P("expert", ("section", "mp"), None),
    )
    return jax.shard_map(
        shards,
        mesh=mesh,
        in_specs=placed,
        out_specs=(
            P(None, "expert", None, None),
            P(None, "expert", None, None),
            P("section", None),
            P("section", None, "mp"),
            P("section", None, "mp"),
            P("section", None, "mp"),
            P("section", "mp", None),
            P("section", None, "mp"),
            P("section", None),
            P(None, ("section", "mp")),
            P(None, ("section", "mp")),
            P(("section", "mp"), None),
            P(),
            P("expert", None, ("section", "mp")),
            P("expert", None, ("section", "mp")),
            P("expert", ("section", "mp"), None),
        ),
        check_vma=False,
    )
```

```python
import contextlib
import functools

import jax
import jax.numpy as jnp
import numpy as np
from jax import lax
from jax.experimental import pallas as pl
from jax.experimental.pallas import tpu as pltpu
from jax.sharding import PartitionSpec as P

EPSILON = 1e-06
NEGATIVE = -1e30
BF16, F32 = jnp.bfloat16, jnp.float32
MESH = pl.DeviceIdType.MESH
HIGHEST = lax.Precision.HIGHEST

GAINS, TERM1, ROWS1, DENSE, ROWS2, TERM2, ROWS3, MOE, OUT, GRAD2, BACK2 = range(11)
GRAD1, BACK1, GRAD0, BACK0, INPUT, SMALL_A, SMALL_A2, SMALL_B, SMALL_B2 = range(11, 20)
DISPATCH, FORWARD, CORE, RETURN = 20, 24, 28, 32
DENSE_SUM, ATTN_SUM = 33, 41
SEMAPHORES = 49


def bucket_limits(count):
    exact = count // 2
    limits = []
    for level in range(1, count):
        if level < exact:
            limits.append(level)
        else:
            distance = exact
            while (
                min(
                    count - 1,
                    exact + int(np.floor(np.log(distance / exact) / np.log(128.0 / exact) * exact)),
                )
                < level
            ):
                distance += 1
            limits.append(distance)
    return limits


def dot(left, right, dims, precision=None):
    return lax.dot_general(
        left, right, (((dims[0],), (dims[1],)), ((), ())), precision=precision, preferred_element_type=F32
    )


def nn(left, right, precision=None):
    return dot(left, right, (1, 0), precision)


def nt(left, right, precision=None):
    return dot(left, right, (1, 1), precision)


def tn(left, right, precision=None):
    return dot(left, right, (0, 0), precision)


def low(value):
    return value.astype(BF16)


def full(value):
    return value.astype(F32)


def inverse_rms(rows):
    return lax.rsqrt(jnp.mean(rows * rows, axis=-1, keepdims=True) + EPSILON)


def normed(rows, gain):
    return low(rows * inverse_rms(rows) * gain)


def normed_back(rows, gain, grad):
    rho = inverse_rms(rows)
    scaled = grad * gain
    back = scaled * rho - rows * (rho * rho * rho) * jnp.mean(scaled * rows, axis=-1, keepdims=True)
    return back, jnp.sum(grad * rows * rho, axis=0, keepdims=True)


def gelu_parts(a):
    t = jnp.tanh(0.7978845608028654 * (a + 0.044715 * a * a * a))
    half = 0.5 * (1.0 + t)
    slope = half + 0.5 * a * (1.0 - t * t) * (0.7978845608028654 * (1.0 + 0.134145 * a * a))
    return a * half, slope


def kernel(
    c,
    x_ref,
    gy_ref,
    docs_ref,
    routes_ref,
    attn_gain_ref,
    ffn_gain_ref,
    table_ref,
    wq_ref,
    wk_ref,
    wv_ref,
    wo_ref,
    router_ref,
    dense_gate_hbm,
    dense_up_hbm,
    dense_down_hbm,
    gate_hbm,
    up_hbm,
    down_hbm,
    out_ref,
    input_ref,
    attn_ref,
    dense_ref,
    ge_gate_hbm,
    ge_up_hbm,
    ge_down_hbm,
    small_ref,
    bias_grad_ref,
    send_sem,
    recv_sem,
    gains,
    bucket,
    bias,
    mask,
    n1,
    qkv,
    probs,
    o,
    do,
    dqkv,
    dsum,
    bias_rows,
    sends,
    recv4,
    recv8,
    rows1,
    rows2,
    rows3,
    grad2,
    grad1,
    grad0,
    chunk,
    hid1,
    gate1,
    up1,
    da1,
    du1,
    pick0,
    pick1,
    gate_slot,
    sx,
    rx,
    hid,
    da,
    du,
    cs,
    cr,
    rt,
    rb,
    moe_send,
    moe_recv,
    small,
    small_send,
    small_recv,
    small2_send,
    small2_recv,
    smallb_send,
    smallb_recv,
    smallb2_send,
    smallb2_recv,
    dense_own,
    dense_a1,
    dense_b1,
    dense_am,
    dense_bm,
    dense_a2,
    dense_b2,
    attn_own,
    attn_a1,
    attn_b1,
    attn_am,
    attn_bm,
    attn_a2,
    attn_b2,
    dense_gate_ref,
    dense_up_ref,
    dense_down_ref,
    gate_ref,
    up_ref,
    down_ref,
    ge_gate_ref,
    ge_up_ref,
    ge_down_ref,
    stage_sem,
):
    sections, experts, mps = c["section"], c["expert"], c["mp"]
    micro, length, heads, size, cap = c["micro"], c["length"], c["heads"], c["size"], c["cap"]
    width, ff = c["width"], c["ff"]
    group = sections * mps
    rows = micro * length
    part = rows // group
    half = width // sections
    local = heads * size
    scale = size**-0.5
    slots = micro * cap
    s, me, mp = lax.axis_index("section"), lax.axis_index("expert"), lax.axis_index("mp")
    place = s * mps + mp
    own = pl.ds(pl.multiple_of(place * part, part), part)
    mine = pl.ds(pl.multiple_of(s * half, 128), half)
    H2, Y1, H1, GRAD = 0, 1, 2, 3
    staged = [
        pltpu.make_async_copy(src, dst, stage_sem.at[i])
        for i, (src, dst) in enumerate(
            (
                (dense_gate_hbm, dense_gate_ref),
                (dense_up_hbm, dense_up_ref),
                (dense_down_hbm, dense_down_ref),
                (gate_hbm, gate_ref),
                (up_hbm, up_ref),
                (down_hbm, down_ref),
                (ge_gate_ref, ge_gate_hbm),
                (ge_up_ref, ge_up_hbm),
                (ge_down_ref, ge_down_hbm),
            )
        )
    ]
    for copy in staged[0:6]:
        copy.start()
    blocks = 4
    per = experts // blocks
    block = per * slots
    side_size = c["side"]
    slow, fast = me // side_size, lax.rem(me, side_size)

    def at_offset(dz, dy):
        z, y = lax.rem(slow + dz, side_size), lax.rem(fast + dy, side_size)
        return z * side_size + y

    scopes = contextlib.ExitStack()

    def phase(name):
        scopes.close()
        scopes.enter_context(jax.named_scope(name))

    def on_expert(k):
        return {"expert": lax.rem(me + k, experts)}

    def in_group(p):
        return {"section": p // mps, "mp": lax.rem(p, mps)}

    def send(src, dst, which, device, arrival=None):
        pltpu.make_async_remote_copy(
            src_ref=src,
            dst_ref=dst,
            send_sem=send_sem.at[which],
            recv_sem=recv_sem.at[which if arrival is None else arrival],
            device_id=device,
            device_id_type=MESH,
        ).start()

    def drain(sem, view):
        pltpu.make_async_copy(view, view, sem).wait()

    def arrived(phase, view):
        drain(recv_sem.at[phase], view)

    def left(phase, view):
        drain(send_sem.at[phase], view)

    phase("signals")
    barrier = pltpu.get_barrier_semaphore()
    for k in range(1, group):
        pl.semaphore_signal(barrier, inc=1, device_id=in_group(lax.rem(place + k, group)), device_id_type=MESH)
    for k in range(1, experts):
        pl.semaphore_signal(barrier, inc=1, device_id=on_expert(k), device_id_type=MESH)

    phase("tables")
    gains[s] = jnp.zeros((8, width), F32)
    gains[s, 0:1] = attn_gain_ref[...]
    gains[s, 1:2] = ffn_gain_ref[...]
    row_at = lax.broadcasted_iota(jnp.int32, (length, length), 0)
    col_at = lax.broadcasted_iota(jnp.int32, (length, length), 1)
    found = jnp.zeros((length, length), jnp.int32)
    for limit in bucket_limits(c["buckets"]):
        found = found + jnp.where(row_at - col_at >= limit, 1, 0)
    bucket[...] = found
    for h in range(heads):
        total = jnp.zeros((length, length), F32)
        for b in range(c["buckets"]):
            total = jnp.where(found == b, table_ref[h][:, b : b + 1], total)
        bias[h] = total
    for m in range(micro):
        docs = jnp.broadcast_to(full(docs_ref[m : m + 1, :]), (length, length))
        same = (docs == jnp.transpose(docs)) & (col_at <= row_at)
        mask[m] = jnp.where(same, 1.0, 0.0)
    phase("barrier")
    pl.semaphore_wait(barrier, group - 1 + experts - 1)
    send(gains.at[s], gains.at[s], GAINS, {"section": 1 - s})

    def gather_all(buf, phase):
        for k in range(1, group):
            send(buf.at[own], buf.at[own], phase, in_group(lax.rem(place + k, group)))

    def wait_all(buf, phase):
        arrived(phase, buf.at[pl.ds(0, (group - 1) * part)])

    def gather_to(target, buf, phase):
        for k in range(1, mps):
            send(buf.at[own], buf.at[own], phase, {"section": target, "mp": lax.rem(mp + k, mps)})

        @pl.when(s != target)
        def _():
            send(buf.at[own], buf.at[own], phase, {"section": 1 - s})

    def left_to(target, buf, phase):
        @pl.when(s != target)
        def _():
            left(phase, buf.at[pl.ds(0, mps * part)])

        @pl.when(s == target)
        def _():
            left(phase, buf.at[pl.ds(0, (mps - 1) * part)])

    def scatter(src, dst, phase):
        for k in range(1, group):
            p = lax.rem(place + k, group)
            send(src.at[pl.ds(pl.multiple_of(p * part, part), part)], dst.at[place], phase, in_group(p))
        dst[place] = src[own]

    def scatter_from(src, dst, phase):
        for k in range(1, group):
            p = lax.rem(place + k, group)
            send(src.at[pl.ds(pl.multiple_of(p * part, part), part)], dst.at[mp], phase, in_group(p))
        dst[mp] = src[own]

    def wait_from(source, dst, phase):
        @pl.when(s == source)
        def _():
            arrived(phase, dst.at[pl.ds(0, mps - 1)])

        @pl.when(s != source)
        def _():
            arrived(phase, dst)

    def total(ref, first=0, last=None):
        last = ref.shape[0] if last is None else last
        value = full(ref[first])
        for i in range(first + 1, last):
            value = value + full(ref[i])
        return value

    pairs = [
        (m, h, slice(m * length, (m + 1) * length), slice(h * size, (h + 1) * size))
        for m in range(micro)
        for h in range(heads)
    ]

    def attention(n_ref, out):
        for t, w in enumerate((wq_ref, wk_ref, wv_ref)):
            qkv[t] = low(nt(n_ref[...], w[...]))
        tops, scores = [], []
        for m, h, r, lanes in pairs:
            raw = nt(qkv[0, r, lanes], qkv[1, r, lanes]) * scale + bias[h]
            scores.append(jnp.where(mask[m] > 0, raw, NEGATIVE))
        tops = [jnp.max(raw, axis=-1, keepdims=True) for raw in scores]
        powers = [jnp.exp(raw - top) for raw, top in zip(scores, tops)]
        sums = [jnp.sum(e, axis=-1, keepdims=True) for e in powers]
        lows = []
        for i, (m, h, r, lanes) in enumerate(pairs):
            p = powers[i] / sums[i]
            probs[m * heads + h] = p
            lows.append(low(p))
        for i, (m, h, r, lanes) in enumerate(pairs):
            o[r, lanes] = low(nn(lows[i], qkv[2, r, lanes]))
        out[...] = low(nn(o[...], wo_ref[...]))

    def attention_back(g_ref, out):
        do[...] = low(nt(g_ref[...], wo_ref[...]))
        dps = [nt(do[r, lanes], qkv[2, r, lanes]) for m, h, r, lanes in pairs]
        for m, h, r, lanes in pairs:
            dv = tn(low(probs[m * heads + h]), do[r, lanes])
            dqkv[r, 2 * local + h * size : 2 * local + (h + 1) * size] = low(dv)
        sums = [
            jnp.sum(dp * probs[m * heads + h], axis=-1, keepdims=True)
            for dp, (m, h, r, lanes) in zip(dps, pairs)
        ]
        grads = [
            low(probs[m * heads + h] * (dp - total_row))
            for dp, total_row, (m, h, r, lanes) in zip(dps, sums, pairs)
        ]
        for ds, (m, h, r, lanes) in zip(grads, pairs):
            dqkv[r, h * size : (h + 1) * size] = low(nn(ds, qkv[1, r, lanes]) * scale)
        for ds, (m, h, r, lanes) in zip(grads, pairs):
            dqkv[r, local + h * size : local + (h + 1) * size] = low(tn(ds, qkv[0, r, lanes]) * scale)
        for h in range(heads):
            dsum[h] = sum(full(grads[m * heads + h]) for m in range(micro))
        dn = nn(dqkv[:, 0:local], wq_ref[...]) + nn(dqkv[:, local : 2 * local], wk_ref[...])
        dn = dn + nn(dqkv[:, 2 * local : 3 * local], wv_ref[...])
        out[...] = low(dn)
        return dn

    def attention_weights(n_ref, g_ref):
        grads = low(tn(dqkv[...], n_ref[...]))
        last = low(tn(o[...], g_ref[...]))
        for t in range(width // 128):
            lanes = slice(t * 128, (t + 1) * 128)
            attn_own[t, 0 : 3 * local] = grads[:, lanes]
            attn_own[t, 3 * local :] = last[:, lanes]
        attn_sum[0]()
        found = bucket[...]
        for h in range(heads):
            held = dsum[h]
            for b in range(c["buckets"]):
                bias_rows[b : b + 1, :] = jnp.sum(jnp.where(found == b, held, 0.0), axis=0, keepdims=True)
            sums = nt(jnp.ones((8, length), F32), bias_rows[...], HIGHEST)
            smallb_send[1 + h : 2 + h, 0 : c["buckets"]] = sums[0:1]

    def reducer(own, out, base, split, first_recv, middles, second_recv):
        n = side_size
        quarter, step = width // n, width // (n * n)
        tiles = own.shape[0]

        def half_of(i):
            f, g = (fast, slow) if i == 0 else (slow, fast)
            to_f = (lambda p: slow * n + p) if i == 0 else (lambda p: p * n + fast)
            to_g = (lambda p: p * n + fast) if i == 0 else (lambda p: slow * n + p)
            lanes = pl.ds(0, split) if i == 0 else pl.ds(split, tiles - split)
            return f, g, to_f, to_g, lanes, base + i

        def many(p, size):
            return pl.ds(pl.multiple_of(p * size, 16), size)

        def one():
            for i in range(2):
                f, g, to_f, to_g, lanes, which = half_of(i)
                for k in range(1, n):
                    p = lax.rem(f + k, n)
                    src = own.at[lanes, many(p, quarter)]
                    send(src, first_recv[i].at[f], which, {"expert": to_f(p)})
                first_recv[i][f] = own[lanes, many(f, quarter)]

        def two():
            for i in range(2):
                f, g, to_f, to_g, lanes, which = half_of(i)
                arrived(which, first_recv[i].at[pl.ds(0, n - 1)])
                middles[i][...] = low(total(first_recv[i]))
                for k in range(1, n):
                    p = lax.rem(g + k, n)
                    src = middles[i].at[:, many(p, step)]
                    send(src, second_recv[i].at[g], which + 2, {"expert": to_g(p)})
                second_recv[i][g] = middles[i][:, many(g, step)]

        def three():
            for i in range(2):
                f, g, to_f, to_g, lanes, which = half_of(i)
                arrived(which + 2, second_recv[i].at[pl.ds(0, n - 1)])
                at = out.at[lanes, many(f * n + g, step)]
                at[...] = low(total(second_recv[i]))
                for k in range(1, n):
                    send(at, at, which + 4, {"expert": to_g(lax.rem(g + k, n))})

        def four():
            for i in range(2):
                f, g, to_f, to_g, lanes, which = half_of(i)
                arrived(which + 4, second_recv[i].at[pl.ds(0, n - 1)])
                at = out.at[lanes, many(f, quarter)]
                for k in range(1, n):
                    send(at, at, which + 6, {"expert": to_f(lax.rem(f + k, n))})

        def five():
            for i in range(2):
                arrived(base + i + 6, first_recv[i].at[pl.ds(0, n - 1)])

        def done():
            for i in range(2):
                for stage in range(4):
                    ref = (first_recv, second_recv, second_recv, first_recv)[stage][i]
                    left(base + i + 2 * stage, ref.at[pl.ds(0, n - 1)])

        return one, two, three, four, five, done

    phase("attention1")
    dense_sum = reducer(
        dense_own, dense_ref, DENSE_SUM, 5, (dense_a1, dense_b1), (dense_am, dense_bm), (dense_a2, dense_b2)
    )
    attn_sum = reducer(
        attn_own, attn_ref, ATTN_SUM, 3, (attn_a1, attn_b1), (attn_am, attn_bm), (attn_a2, attn_b2)
    )

    x = full(x_ref[...])
    @pl.when(s == 0)
    def _():
        n1[...] = normed(x, gains[0, 0:1])
        attention(n1, sends.at[0])
        scatter_from(sends.at[0], recv4.at[0], TERM1)

    phase("term1_wait")
    arrived(GAINS, gains.at[1 - s])
    wait_from(0, recv4.at[0], TERM1)
    phase("norm1")
    h1 = full(x_ref[own]) + total(recv4.at[0])
    chunk[H1] = h1
    rows1[own] = normed(h1, gains[0, 1:2])
    gather_all(rows1, ROWS1)
    phase("rows1_wait")
    wait_all(rows1, ROWS1)
    phase("dense")
    for copy in staged[0:3]:
        copy.wait()
    gate1[...] = nn(rows1[...], dense_gate_ref[...])
    up1[...] = nn(rows1[...], dense_up_ref[...])
    hid1[...] = low(gelu_parts(gate1[...])[0] * up1[...])
    sends[1] = low(nn(hid1[...], dense_down_ref[...]))
    scatter(sends.at[1], recv8.at[0], DENSE)
    phase("dense_wait")
    arrived(DENSE, recv8.at[0, pl.ds(0, group - 1)])
    phase("norm2")
    y1 = chunk[H1] + total(recv8.at[0])
    chunk[Y1] = y1
    rows2[own] = normed(y1, gains[1, 0:1])
    gather_to(1, rows2, ROWS2)

    phase("attention2")
    @pl.when(s == 1)
    def _():
        wait_all(rows2, ROWS2)
        attention(rows2, sends.at[2])
        scatter_from(sends.at[2], recv4.at[1], TERM2)

    phase("routing")
    named = []
    before = low(jnp.where(row_at < col_at, 1.0, 0.0))
    expert_at = lax.broadcasted_iota(jnp.int32, (experts, length), 0)
    slot_at = full(lax.broadcasted_iota(jnp.int32, (cap, length), 0))
    for m in range(micro):
        hots = [
            jnp.where(expert_at == routes_ref[2 * m + ch : 2 * m + ch + 1, :], 1.0, 0.0)
            for ch in range(2)
        ]
        rank = nn(low(hots[0] + hots[1]), before)
        for e in range(experts):
            fit = slot_at == rank[e : e + 1]
            at = slice(e * cap, (e + 1) * cap)
            pick0[m, at] = low(jnp.where(fit, hots[0][e : e + 1], 0.0))
            pick1[m, at] = low(jnp.where(fit, hots[1][e : e + 1], 0.0))
        named.append(hots)

    phase("term2_wait")
    wait_from(1, recv4.at[1], TERM2)
    phase("norm3")
    h2 = chunk[Y1] + total(recv4.at[1])
    chunk[H2] = h2
    rows3[own] = normed(h2, gains[1, 1:2])
    gather_all(rows3, ROWS3)
    phase("rows3_wait")
    wait_all(rows3, ROWS3)
    phase("slots")
    logits = nt(router_ref[...], rows3[...])
    for m in range(micro):
        hots = named[m]
        r = slice(m * length, (m + 1) * length)
        here = logits[:, r]
        l0 = jnp.sum(hots[0] * here, axis=0, keepdims=True)
        l1 = jnp.sum(hots[1] * here, axis=0, keepdims=True)
        top = jnp.maximum(l0, l1)
        e0, e1 = jnp.exp(l0 - top), jnp.exp(l1 - top)
        by_expert = (hots[0] * e0 + hots[1] * e1) / (e0 + e1)
        both = pick0[m] + pick1[m]
        for e in range(experts):
            at = slice(e * cap, (e + 1) * cap)
            gate = jnp.sum(full(both[at]) * by_expert[e : e + 1], axis=1, keepdims=True)
            gate_slot[m, at] = jnp.broadcast_to(gate, (cap, 128))
        place_rows = slice(m * cap, (m + 1) * cap)
        out_rows = low(nn(both, rows3[r, mine]))
        sx[:, place_rows, 0:half] = out_rows.reshape(experts, cap, half)
        out_rows = low(nn(both, gy_ref[r, mine]) * gate_slot[m][:, 0:1])
        sx[:, place_rows, half:] = out_rows.reshape(experts, cap, half)
    if side_size == 4:
        offsets = [(0, 1), (0, 3), (1, 0), (3, 0), (1, 1), (3, 3), (1, 3), (3, 1)]
        offsets += [(2, 1), (2, 3), (1, 2), (3, 2), (0, 0), (0, 2), (2, 0), (2, 2)]
    else:
        offsets = [(a, b) for a in range(side_size) for b in range(side_size)]

    def dispatch(j):
        for k in range(j * per, (j + 1) * per):
            to = rx.at[s, pl.ds(k * slots, slots)]
            if offsets[k] == (0, 0):
                pltpu.make_async_copy(sx.at[me], to, recv_sem.at[DISPATCH + j]).start()
            else:
                p = at_offset(*offsets[k])
                send(sx.at[p], to, DISPATCH + j, {"expert": p})

    def dispatched(j):
        count = sum(offsets[k] != (0, 0) for k in range(j * per, (j + 1) * per))
        if count:
            left(DISPATCH + j, rx.at[0, pl.ds(0, count * slots)])

    def forward(j):
        at = pl.ds(j * block, block)
        arrived(DISPATCH + j, rx.at[s, at])
        send(rx.at[s, at], rx.at[s, at], FORWARD + j, {"section": 1 - s})

    def give_back(j):
        at = pl.ds(j * block, block)
        arrived(CORE + j, cr.at[at])
        rt[at] = low(full(cs[s, at]) + full(cr[at]))
        for k in range(j * per, (j + 1) * per):
            src = rt.at[pl.ds(k * slots, slots)]
            if offsets[k] == (0, 0):
                pltpu.make_async_copy(src, rb.at[me], recv_sem.at[RETURN]).start()
            else:
                dz, dy = offsets[k]
                send(src, rb.at[me], RETURN, {"expert": at_offset(side_size - dz, side_size - dy)})

    phase("dispatch_wait")
    dispatch(0)
    dispatch(1)
    forward(0)
    dispatched(0)
    dispatch(2)
    for copy in staged[3:6]:
        copy.wait()
    for j in range(blocks):
        at = pl.ds(j * block, block)
        phase("forward_wait%d" % j)
        arrived(FORWARD + j, rx.at[1 - s, at])
        phase("expert%d" % j)
        x0, x1 = rx[0, at, 0:half], rx[1, at, 0:half]
        g0, g1 = rx[0, at, half:], rx[1, at, half:]
        a = nn(x0, gate_ref[0:half]) + nn(x1, gate_ref[half:])
        u = nn(x0, up_ref[0:half]) + nn(x1, up_ref[half:])
        d = nt(g0, down_ref[:, 0:half]) + nt(g1, down_ref[:, half:])
        value, slope = gelu_parts(a)
        hid[at] = low(value * u)
        da[at] = low(d * u * slope)
        du[at] = low(d * value)
        for side in range(sections):
            w = slice(side * half, (side + 1) * half)
            cs[side, at, 0:half] = low(nn(hid[at], down_ref[:, w]))
            cs[side, at, half:] = low(nt(da[at], gate_ref[w]) + nt(du[at], up_ref[w]))
        send(cs.at[1 - s, at], cr.at[at], CORE + j, {"section": 1 - s})
        phase("give_back%d" % j)
        if j + 1 < blocks:
            forward(j + 1)
            dispatched(j + 1)
            if j + 3 < blocks:
                dispatch(j + 3)
        if j > 0:
            give_back(j - 1)
    give_back(blocks - 1)
    phase("expert_weights")
    for side in range(sections):
        w = slice(side * half, (side + 1) * half)
        ge_gate_ref[w] = low(tn(rx[side, :, 0:half], da[...]))
        ge_up_ref[w] = low(tn(rx[side, :, 0:half], du[...]))
        ge_down_ref[:, w] = low(tn(hid[...], rx[side, :, half:]))
    for copy in staged[6:]:
        copy.start()
    phase("return_wait")
    arrived(RETURN, rb)
    phase("combine")
    lane = lax.broadcasted_iota(jnp.int32, (length, 128), 1)
    for m in range(micro):
        r = slice(m * length, (m + 1) * length)
        held = rb[:, m * cap : (m + 1) * cap, :].reshape(experts * cap, width)
        scaled = low(full(held[:, 0:half]) * gate_slot[m][:, 0:1])
        first, second = tn(pick0[m], scaled), tn(pick1[m], scaled)
        gy = full(gy_ref[r, mine])
        t0 = jnp.sum(gy * first, axis=-1, keepdims=True)
        t1 = jnp.sum(gy * second, axis=-1, keepdims=True)
        moe_send[r, 0:half] = low(first + second)
        moe_send[r, half : 2 * half] = low(tn(pick0[m] + pick1[m], held[:, half:]))
        moe_send[r, 2 * half :] = low(jnp.where(lane == 0, t0, jnp.where(lane == 1, t1, 0.0)))
    scatter(moe_send, moe_recv, MOE)
    phase("moe_wait")
    arrived(MOE, moe_recv.at[pl.ds(0, group - 1)])
    phase("norm3_back")
    lower, upper = total(moe_recv, 0, mps), total(moe_recv, mps, group)
    h2 = chunk[H2]
    out_ref[own, 0:half] = low(h2[:, 0:half] + lower[:, 0:half])
    out_ref[own, half:] = low(h2[:, half:] + upper[:, 0:half])
    terms = lower[:, 2 * half :] + upper[:, 2 * half :]
    t0, t1 = terms[:, 0:1], terms[:, 1:2]
    ahead = lax.rem(place * part, length)
    token = lax.broadcasted_iota(jnp.int32, (part, length), 1)
    is_own = low(jnp.where(token == lax.broadcasted_iota(jnp.int32, (part, length), 0) + ahead, 1.0, 0.0))
    hot0, hot1 = (
        nt(is_own, low(jnp.where(place * part < length, named[0][ch], named[1][ch]))) for ch in range(2)
    )
    logits = nt(rows3[own], router_ref[...])
    l0 = jnp.sum(hot0 * logits, axis=-1, keepdims=True)
    l1 = jnp.sum(hot1 * logits, axis=-1, keepdims=True)
    top = jnp.maximum(l0, l1)
    e0, e1 = jnp.exp(l0 - top), jnp.exp(l1 - top)
    dlogits = hot0 * (t0 - e0 / (e0 + e1) * (t0 + t1)) + hot1 * (t1 - e1 / (e0 + e1) * (t0 + t1))
    dr = jnp.concatenate([lower[:, half : 2 * half], upper[:, half : 2 * half]], axis=1)
    dr = dr + nn(dlogits, full(router_ref[...]), HIGHEST)
    back, gain = normed_back(h2, gains[1, 1:2], dr)
    grad = full(gy_ref[own]) + back
    chunk[GRAD] = grad
    grad2[own] = low(grad)
    gather_to(1, grad2, GRAD2)
    small[...] = jnp.zeros_like(small)
    small[0:1] = gain
    small[8 : 8 + experts] = tn(dlogits, full(rows3[own]), HIGHEST)
    smallb_send[...] = jnp.zeros_like(smallb_send)
    gather_all(out_ref, OUT)

    phase("attention2_back")
    @pl.when(s == 1)
    def _():
        wait_all(grad2, GRAD2)
        attention_back(grad2, sends.at[3])
        scatter_from(sends.at[3], recv4.at[2], BACK2)
        attention_weights(rows2, grad2)

    phase("back2_wait")
    wait_from(1, recv4.at[2], BACK2)
    phase("norm2_back")
    back, gain = normed_back(chunk[Y1], gains[1, 0:1], total(recv4.at[2]))
    small[1:2] = gain
    grad = chunk[GRAD] + back
    chunk[GRAD] = grad
    grad1[own] = low(grad)
    gather_all(grad1, GRAD1)
    phase("grad1_wait")
    wait_all(grad1, GRAD1)
    phase("dense_back")
    d = nt(grad1[...], dense_down_ref[...])
    value, slope = gelu_parts(gate1[...])
    da1[...] = low(d * up1[...] * slope)
    du1[...] = low(d * value)
    sends[4] = low(nt(da1[...], dense_gate_ref[...]) + nt(du1[...], dense_up_ref[...]))
    scatter(sends.at[4], recv8.at[1], BACK1)
    phase("dense_weights")
    gate_grad = low(tn(rows1[...], da1[...]))
    up_grad = low(tn(rows1[...], du1[...]))
    for t in range(ff // 128):
        lanes = slice(t * 128, (t + 1) * 128)
        dense_own[t] = gate_grad[:, lanes]
        dense_own[ff // 128 + t] = up_grad[:, lanes]
    down_grad = low(tn(hid1[...], grad1[...]))
    for t in range(width // 128):
        at = slice(t % 2 * ff, t % 2 * ff + ff)
        dense_own[2 * (ff // 128) + t // 2, at] = down_grad[:, t * 128 : (t + 1) * 128]
    dense_sum[0]()
    phase("back1_wait")
    arrived(BACK1, recv8.at[1, pl.ds(0, group - 1)])
    phase("norm1_back")
    back, gain = normed_back(chunk[H1], gains[0, 1:2], total(recv8.at[1]))
    small[2:3] = gain
    grad = chunk[GRAD] + back
    chunk[GRAD] = grad
    grad0[own] = low(grad)
    gather_to(0, grad0, GRAD0)
    small_send[...] = low(small[...])
    for k in range(1, group):
        send(small_send, small_recv.at[place], SMALL_A, in_group(lax.rem(place + k, group)))
    small_recv[place] = small_send[...]

    phase("attention1_back")
    @pl.when(s == 0)
    def _():
        wait_all(grad0, GRAD0)
        dn = attention_back(grad0, sends.at[5])
        scatter_from(sends.at[5], recv4.at[3], BACK0)
        x = full(x_ref[...])
        smallb_send[0:1] = jnp.sum(dn * x * inverse_rms(x), axis=0, keepdims=True)

    @pl.when(s == 1)
    def _():
        for stage in attn_sum[1:]:
            stage()

    phase("dense_two")
    dense_sum[1]()

    phase("attn_one")
    @pl.when(s == 0)
    def _():
        attention_weights(n1, grad0)

    phase("dense_three")
    dense_sum[2]()
    for k in range(1, experts):
        send(smallb_send, smallb_recv.at[me], SMALL_B, on_expert(k))
    smallb_recv[me] = smallb_send[...]
    phase("back0_wait")
    wait_from(0, recv4.at[3], BACK0)
    phase("norm0_back")
    back, gain = normed_back(full(x_ref[own]), gains[0, 0:1], total(recv4.at[3]))
    input_ref[own] = low(chunk[GRAD] + back)
    gather_all(input_ref, INPUT)
    phase("attn_two")
    @pl.when(s == 0)
    def _():
        attn_sum[1]()

    phase("dense_four")
    dense_sum[3]()
    phase("small_a")
    arrived(SMALL_A, small_recv.at[pl.ds(0, group - 1)])
    small2_send[...] = low(total(small_recv))
    for k in range(1, experts):
        send(small2_send, small2_recv.at[me], SMALL_A2, on_expert(k))
    small2_recv[me] = small2_send[...]
    phase("attn_three")
    @pl.when(s == 0)
    def _():
        attn_sum[2]()

    phase("small_b")
    arrived(SMALL_B, smallb_recv.at[pl.ds(0, experts - 1)])
    smallb2_send[...] = total(smallb_recv)
    for k in range(1, mps):
        send(smallb2_send, smallb2_recv.at[mp], SMALL_B2, {"mp": lax.rem(mp + k, mps)})
    smallb2_recv[mp] = smallb2_send[...]
    phase("attn_four")
    @pl.when(s == 0)
    def _():
        attn_sum[3]()

    arrived(SMALL_A2, small2_recv.at[pl.ds(0, experts - 1)])
    summed = total(small2_recv)
    for h in range(heads):
        bias_grad_ref[h] = smallb2_send[1 + h : 2 + h, 0 : c["buckets"]]
    arrived(SMALL_B2, smallb2_recv.at[pl.ds(0, mps - 1)])
    gain0 = total(smallb2_recv)[0:1]
    small_ref[...] = summed
    small_ref[0:1] = jnp.where(s == 0, gain0, summed[1:2])
    small_ref[1:2] = jnp.where(s == 0, summed[2:3], summed[0:1])
    phase("last_waits")
    wait_all(out_ref, OUT)
    wait_all(input_ref, INPUT)
    dense_sum[4]()

    @pl.when(s == 0)
    def _():
        attn_sum[4]()
        attn_sum[5]()

    for copy in staged[6:]:
        copy.wait()
    dense_sum[5]()
    left(GAINS, gains.at[s])
    seven = pl.ds(0, (group - 1) * part)
    for phase, ref in ((ROWS1, rows1), (ROWS3, rows3), (OUT, out_ref), (GRAD1, grad1), (INPUT, input_ref)):
        left(phase, ref.at[seven])
    for phase, at in ((DENSE, 1), (BACK1, 4)):
        left(phase, sends.at[at, seven])
    left(MOE, moe_send.at[seven])
    left_to(1, rows2, ROWS2)
    left_to(1, grad2, GRAD2)
    left_to(0, grad0, GRAD0)

    @pl.when(s == 0)
    def _():
        left(TERM1, sends.at[0, seven])
        left(BACK0, sends.at[5, seven])

    @pl.when(s == 1)
    def _():
        left(TERM2, sends.at[2, seven])
        left(BACK2, sends.at[3, seven])

    for j in range(blocks):
        left(FORWARD + j, rx.at[0, pl.ds(0, block)])
        left(CORE + j, cr.at[pl.ds(0, block)])
    left(RETURN, rb.at[pl.ds(0, experts - 1)])
    left(SMALL_A, small_recv.at[pl.ds(0, group - 1)])
    left(SMALL_A2, small2_recv.at[pl.ds(0, experts - 1)])
    left(SMALL_B, smallb_recv.at[pl.ds(0, experts - 1)])
    left(SMALL_B2, smallb2_recv.at[pl.ds(0, mps - 1)])
    scopes.close()


def widen(tiles, experts, out, back, attn, gate, up, down, e_gate, e_up, e_down, small, bias, *to):
    to[0][...] = full(out[...])
    to[1][...] = full(back[...])
    for t in range(2 * tiles):
        lanes = slice(t * 128, (t + 1) * 128)
        for which in range(4):
            to[2 + which][:, lanes] = full(attn[t, which])
        to[8][:, lanes] = full(down[t // 2, t % 2])
    for t in range(tiles):
        lanes = slice(t * 128, (t + 1) * 128)
        to[6][:, lanes] = full(gate[t])
        to[7][:, lanes] = full(up[t])
    to[9][...] = full(e_gate[...])
    to[10][...] = full(e_up[...])
    to[11][...] = full(e_down[...])
    to[12][...] = small[0:1]
    to[13][...] = small[1:2]
    to[14][...] = small[8 : 8 + experts]
    to[15][...] = bias[...]


def shards(
    block_input,
    segments,
    routes,
    cotangent,
    attn_gain,
    query_weight,
    key_weight,
    value_weight,
    out_weight,
    pos_bias,
    ffn_gain,
    dense_gate,
    dense_up,
    dense_down,
    router,
    expert_gate,
    expert_up,
    expert_down,
):
    micro, _, length, width = block_input.shape
    experts = router.shape[1]
    cap = 4 * length // experts
    buckets, heads = pos_bias.shape[1:]
    local = query_weight.shape[2]
    size = local // heads
    ff = dense_gate.shape[1]
    sections, mps = lax.axis_size("section"), lax.axis_size("mp")
    group = sections * mps
    rows = micro * length
    part = rows // group
    half = width // sections
    slots = micro * cap
    every = experts * slots
    step = width // experts
    side = int(np.sqrt(experts))
    c = dict(
        side=side,
        section=sections, expert=experts, mp=mps, micro=micro, length=length, heads=heads, size=size,
        cap=cap, width=width, ff=ff, buckets=buckets,
    )
    vmem = pl.BlockSpec(memory_space=pltpu.VMEM)
    hbm = pl.BlockSpec(memory_space=pl.ANY)

    def held(*shape):
        return pltpu.VMEM(shape, BF16)

    def exact(*shape):
        return pltpu.VMEM(shape, F32)

    scratch = [
        pltpu.SemaphoreType.DMA((SEMAPHORES,)),
        pltpu.SemaphoreType.DMA((SEMAPHORES,)),
        exact(sections, 8, width),
        pltpu.VMEM((length, length), jnp.int32),
        exact(heads, length, length),
        exact(micro, length, length),
        held(rows, width),
        held(3, rows, local),
        exact(micro * heads, length, length),
        held(rows, local),
        held(rows, local),
        held(rows, 3 * local),
        exact(heads, length, length),
        exact(buckets, length),
        held(6, rows, width),
        held(4, mps, part, width),
        held(2, group, part, width),
        held(rows, width),
        held(rows, width),
        held(rows, width),
        held(rows, width),
        held(rows, width),
        held(rows, width),
        exact(4, part, width),
        held(rows, ff),
        exact(rows, ff),
        exact(rows, ff),
        held(rows, ff),
        held(rows, ff),
        held(micro, experts * cap, length),
        held(micro, experts * cap, length),
        exact(micro, experts * cap, 128),
        held(experts, slots, 2 * half),
        held(sections, every, 2 * half),
        held(every, ff),
        held(every, ff),
        held(every, ff),
        held(sections, every, 2 * half),
        held(every, 2 * half),
        held(every, 2 * half),
        held(experts, slots, 2 * half),
        held(rows, 2 * half + 128),
        held(group, part, 2 * half + 128),
        exact(32, width),
        held(32, width),
        held(group, 32, width),
        held(32, width),
        held(experts, 32, width),
        exact(8, width),
        exact(experts, 8, width),
        exact(8, width),
        exact(mps, 8, width),
        held(9, width, 128),
        held(side, 5, width // side, 128),
        held(side, 4, width // side, 128),
        held(5, width // side, 128),
        held(4, width // side, 128),
        held(side, 5, step, 128),
        held(side, 4, step, 128),
        held(6, width, 128),
        held(side, 3, width // side, 128),
        held(side, 3, width // side, 128),
        held(3, width // side, 128),
        held(3, width // side, 128),
        held(side, 3, step, 128),
        held(side, 3, step, 128),
        held(width, ff),
        held(width, ff),
        held(ff, width),
        held(width, ff),
        held(width, ff),
        held(ff, width),
        held(width, ff),
        held(width, ff),
        held(ff, width),
        pltpu.SemaphoreType.DMA((9,)),
    ]
    shape = jax.ShapeDtypeStruct
    block_output, input_grad, attn, dense, ge_gate, ge_up, ge_down, small, bias_grad = pl.pallas_call(
        functools.partial(kernel, c),
        out_shape=(
            shape((rows, width), BF16),
            shape((rows, width), BF16),
            shape((6, 4 * local, 128), BF16),
            shape((9, width, 128), BF16),
            shape((width, ff), BF16),
            shape((width, ff), BF16),
            shape((ff, width), BF16),
            shape((32, width), F32),
            shape((heads, 1, buckets), F32),
        ),
        in_specs=[vmem] * 12 + [hbm] * 6,
        out_specs=(vmem,) * 4 + (hbm,) * 3 + (vmem,) * 2,
        scratch_shapes=scratch,
        compiler_params=pltpu.CompilerParams(
            collective_id=0, has_side_effects=True, vmem_limit_bytes=60 * 1024 * 1024
        ),
    )(
        block_input.reshape(rows, width),
        cotangent.reshape(rows, width),
        segments.reshape(micro, length),
        routes[:, 0].transpose(0, 2, 1).reshape(2 * micro, length),
        attn_gain,
        ffn_gain,
        pos_bias.transpose(2, 0, 1),
        query_weight[0].T,
        key_weight[0].T,
        value_weight[0].T,
        out_weight[0],
        router.T,
        dense_gate,
        dense_up,
        dense_down,
        expert_gate[0],
        expert_up[0],
        expert_down[0],
    )
    steps = 4

    def rows_of(rows, width):
        return pl.BlockSpec((rows // steps, width), lambda i: (i, 0))

    def whole(*dims):
        return pl.BlockSpec(dims, lambda i: (0,) * len(dims))

    tiles = ff // 128
    attn_shape = shape((local, width), F32)
    results = pl.pallas_call(
        functools.partial(widen, tiles, experts),
        grid=(steps,),
        out_shape=(
            shape((rows, width), F32),
            shape((rows, width), F32),
            *[attn_shape] * 4,
            shape((width, ff), F32),
            shape((width, ff), F32),
            shape((ff, width), F32),
            shape((width, ff), F32),
            shape((width, ff), F32),
            shape((ff, width), F32),
            shape((1, width), F32),
            shape((1, width), F32),
            shape((experts, width), F32),
            shape((heads, 1, buckets), F32),
        ),
        in_specs=[
            rows_of(rows, width),
            rows_of(rows, width),
            pl.BlockSpec((2 * tiles, 4, local // steps, 128), lambda i: (0, 0, i, 0)),
            pl.BlockSpec((tiles, width // steps, 128), lambda i: (0, i, 0)),
            pl.BlockSpec((tiles, width // steps, 128), lambda i: (1, i, 0)),
            pl.BlockSpec((tiles, 2, ff // steps, 128), lambda i: (2, 0, i, 0)),
            rows_of(width, ff),
            rows_of(width, ff),
            rows_of(ff, width),
            whole(32, width),
            whole(heads, 1, buckets),
        ],
        out_specs=(
            rows_of(rows, width),
            rows_of(rows, width),
            *[rows_of(local, width)] * 4,
            rows_of(width, ff),
            rows_of(width, ff),
            rows_of(ff, width),
            rows_of(width, ff),
            rows_of(width, ff),
            rows_of(ff, width),
            whole(1, width),
            whole(1, width),
            whole(experts, width),
            whole(heads, 1, buckets),
        ),
        compiler_params=pltpu.CompilerParams(vmem_limit_bytes=63 * 1024 * 1024),
    )(
        block_output,
        input_grad,
        attn.reshape(2 * tiles, 4, local, 128),
        dense,
        dense,
        dense.reshape(3 * tiles, 2, ff, 128),
        ge_gate,
        ge_up,
        ge_down,
        small,
        bias_grad,
    )
    return (
        results[0].reshape(block_input.shape),
        results[1].reshape(block_input.shape),
        results[12],
        results[2].T[None],
        results[3].T[None],
        results[4].T[None],
        results[5][None],
        results[15].transpose(1, 2, 0),
        results[13],
        results[6],
        results[7],
        results[8],
        results[14].T,
        results[9][None],
        results[10][None],
        results[11][None],
    )


def solution(mesh):
    placed = (
        P(None, "expert", None, None),
        P(None, "expert", None),
        P(None, "expert", None, None),
        P(None, "expert", None, None),
        P("section", None),
        P("section", None, "mp"),
        P("section", None, "mp"),
        P("section", None, "mp"),
        P("section", "mp", None),
        P("section", None, "mp"),
        P("section", None),
        P(None, ("section", "mp")),
        P(None, ("section", "mp")),
        P(("section", "mp"), None),
        P(),
        P("expert", None, ("section", "mp")),
        P("expert", None, ("section", "mp")),
        P("expert", ("section", "mp"), None),
    )
    return jax.shard_map(
        shards,
        mesh=mesh,
        in_specs=placed,
        out_specs=(
            P(None, "expert", None, None),
            P(None, "expert", None, None),
            P("section", None),
            P("section", None, "mp"),
            P("section", None, "mp"),
            P("section", None, "mp"),
            P("section", "mp", None),
            P("section", None, "mp"),
            P("section", None),
            P(None, ("section", "mp")),
            P(None, ("section", "mp")),
            P(("section", "mp"), None),
            P(),
            P("expert", None, ("section", "mp")),
            P("expert", None, ("section", "mp")),
            P("expert", ("section", "mp"), None),
        ),
        check_vma=False,
    )
```

```python
import contextlib
import functools

import jax
import jax.numpy as jnp
import numpy as np
from jax import lax
from jax.experimental import pallas as pl
from jax.experimental.pallas import tpu as pltpu
from jax.sharding import PartitionSpec as P

EPSILON = 1e-06
NEGATIVE = -1e30
BF16, F32 = jnp.bfloat16, jnp.float32
MESH = pl.DeviceIdType.MESH
HIGHEST = lax.Precision.HIGHEST

GAINS, TERM1, ROWS1, DENSE, ROWS2, TERM2, ROWS3, MOE, OUT, GRAD2, BACK2 = range(11)
GRAD1, BACK1, GRAD0, BACK0, INPUT, SMALL_A, SMALL_A2, SMALL_B, SMALL_B2 = range(11, 20)
DISPATCH, FORWARD, CORE, RETURN = 20, 24, 28, 32
DENSE_SUM, ATTN_SUM = 33, 41
EARLY, EARLY_FORWARD, CORE2, RETURN2, MOE2 = range(49, 54)
SEMAPHORES = 54


def bucket_limits(count):
    exact = count // 2
    limits = []
    for level in range(1, count):
        if level < exact:
            limits.append(level)
        else:
            distance = exact
            while (
                min(
                    count - 1,
                    exact + int(np.floor(np.log(distance / exact) / np.log(128.0 / exact) * exact)),
                )
                < level
            ):
                distance += 1
            limits.append(distance)
    return limits


def dot(left, right, dims, precision=None):
    return lax.dot_general(
        left, right, (((dims[0],), (dims[1],)), ((), ())), precision=precision, preferred_element_type=F32
    )


def nn(left, right, precision=None):
    return dot(left, right, (1, 0), precision)


def nt(left, right, precision=None):
    return dot(left, right, (1, 1), precision)


def tn(left, right, precision=None):
    return dot(left, right, (0, 0), precision)


def low(value):
    return value.astype(BF16)


def full(value):
    return value.astype(F32)


def inverse_rms(rows):
    return lax.rsqrt(jnp.mean(rows * rows, axis=-1, keepdims=True) + EPSILON)


def normed(rows, gain):
    return low(rows * inverse_rms(rows) * gain)


def normed_back(rows, gain, grad):
    rho = inverse_rms(rows)
    scaled = grad * gain
    back = scaled * rho - rows * (rho * rho * rho) * jnp.mean(scaled * rows, axis=-1, keepdims=True)
    return back, jnp.sum(grad * rows * rho, axis=0, keepdims=True)


def gelu_parts(a):
    t = jnp.tanh(0.7978845608028654 * (a + 0.044715 * a * a * a))
    half = 0.5 * (1.0 + t)
    slope = half + 0.5 * a * (1.0 - t * t) * (0.7978845608028654 * (1.0 + 0.134145 * a * a))
    return a * half, slope


def kernel(
    c,
    x_ref,
    gy_ref,
    docs_ref,
    routes_ref,
    attn_gain_ref,
    ffn_gain_ref,
    table_ref,
    wq_ref,
    wk_ref,
    wv_ref,
    wo_ref,
    router_ref,
    dense_gate_hbm,
    dense_up_hbm,
    dense_down_hbm,
    gate_hbm,
    up_hbm,
    down_hbm,
    out_ref,
    input_ref,
    attn_ref,
    dense_ref,
    ge_gate_hbm,
    ge_up_hbm,
    ge_down_hbm,
    small_ref,
    bias_grad_ref,
    send_sem,
    recv_sem,
    gains,
    bucket,
    bias,
    mask,
    n1,
    qkv,
    probs,
    o,
    do,
    dqkv,
    dsum,
    bias_rows,
    sends,
    recv4,
    recv8,
    rows1,
    rows2,
    rows3,
    grad2,
    grad1,
    grad0,
    chunk,
    hid1,
    gate1,
    up1,
    da1,
    du1,
    pick0,
    pick1,
    ex,
    ey,
    sx,
    rx,
    hid,
    da,
    du,
    dout,
    gates,
    cs,
    cr,
    rt,
    rb,
    cs2,
    cr2,
    rt2,
    rb2,
    moe_send,
    moe_recv,
    out_send,
    out_recv,
    small,
    small_send,
    small_recv,
    small2_send,
    small2_recv,
    smallb_send,
    smallb_recv,
    smallb2_send,
    smallb2_recv,
    dense_own,
    dense_a1,
    dense_b1,
    dense_am,
    dense_bm,
    dense_a2,
    dense_b2,
    attn_own,
    attn_a1,
    attn_b1,
    attn_am,
    attn_bm,
    attn_a2,
    attn_b2,
    dense_gate_ref,
    dense_up_ref,
    dense_down_ref,
    gate_ref,
    up_ref,
    down_ref,
    ge_gate_ref,
    ge_up_ref,
    ge_down_ref,
    stage_sem,
    wide_router,
):
    sections, experts, mps = c["section"], c["expert"], c["mp"]
    micro, length, heads, size, cap = c["micro"], c["length"], c["heads"], c["size"], c["cap"]
    width, ff = c["width"], c["ff"]
    group = sections * mps
    rows = micro * length
    part = rows // group
    half = width // sections
    local = heads * size
    scale = size**-0.5
    slots = micro * cap
    s, me, mp = lax.axis_index("section"), lax.axis_index("expert"), lax.axis_index("mp")
    place = s * mps + mp
    own = pl.ds(pl.multiple_of(place * part, part), part)
    mine = pl.ds(pl.multiple_of(s * half, 128), half)
    H2, Y1, H1, GRAD = 0, 1, 2, 3
    staged = [
        pltpu.make_async_copy(src, dst, stage_sem.at[i])
        for i, (src, dst) in enumerate(
            (
                (dense_gate_hbm, dense_gate_ref),
                (dense_up_hbm, dense_up_ref),
                (dense_down_hbm, dense_down_ref),
                (gate_hbm, gate_ref),
                (up_hbm, up_ref),
                (down_hbm, down_ref),
                (ge_gate_ref, ge_gate_hbm),
                (ge_up_ref, ge_up_hbm),
                (ge_down_ref, ge_down_hbm),
            )
        )
    ]
    for copy in staged[0:6]:
        copy.start()
    blocks = 4
    per = experts // blocks
    block = per * slots
    side_size = c["side"]
    slow, fast = me // side_size, lax.rem(me, side_size)

    def at_offset(dz, dy):
        z, y = lax.rem(slow + dz, side_size), lax.rem(fast + dy, side_size)
        return z * side_size + y

    scopes = contextlib.ExitStack()

    def phase(name):
        scopes.close()
        scopes.enter_context(jax.named_scope(name))

    def on_expert(k):
        return {"expert": lax.rem(me + k, experts)}

    def in_group(p):
        return {"section": p // mps, "mp": lax.rem(p, mps)}

    def send(src, dst, which, device, arrival=None):
        pltpu.make_async_remote_copy(
            src_ref=src,
            dst_ref=dst,
            send_sem=send_sem.at[which],
            recv_sem=recv_sem.at[which if arrival is None else arrival],
            device_id=device,
            device_id_type=MESH,
        ).start()

    def drain(sem, view):
        pltpu.make_async_copy(view, view, sem).wait()

    def arrived(phase, view):
        drain(recv_sem.at[phase], view)

    def left(phase, view):
        drain(send_sem.at[phase], view)

    phase("signals")
    barrier = pltpu.get_barrier_semaphore()
    for k in range(1, group):
        pl.semaphore_signal(barrier, inc=1, device_id=in_group(lax.rem(place + k, group)), device_id_type=MESH)
    for k in range(1, experts):
        pl.semaphore_signal(barrier, inc=1, device_id=on_expert(k), device_id_type=MESH)

    phase("tables")
    gains[s] = jnp.zeros((8, width), F32)
    gains[s, 0:1] = attn_gain_ref[...]
    gains[s, 1:2] = ffn_gain_ref[...]
    row_at = lax.broadcasted_iota(jnp.int32, (length, length), 0)
    col_at = lax.broadcasted_iota(jnp.int32, (length, length), 1)
    found = jnp.zeros((length, length), jnp.int32)
    for limit in bucket_limits(c["buckets"]):
        found = found + jnp.where(row_at - col_at >= limit, 1, 0)
    bucket[...] = found
    wide_router[...] = jnp.zeros_like(wide_router)
    wide_router[0:experts] = router_ref[...]
    for h in range(heads):
        total = jnp.zeros((length, length), F32)
        for b in range(c["buckets"]):
            total = jnp.where(found == b, table_ref[h][:, b : b + 1], total)
        bias[h] = total
    for m in range(micro):
        docs = jnp.broadcast_to(full(docs_ref[m : m + 1, :]), (length, length))
        same = (docs == jnp.transpose(docs)) & (col_at <= row_at)
        mask[m] = jnp.where(same, 1.0, 0.0)
    phase("barrier")
    pl.semaphore_wait(barrier, group - 1 + experts - 1)
    send(gains.at[s], gains.at[s], GAINS, {"section": 1 - s})

    def gather_all(buf, phase):
        for k in range(1, group):
            send(buf.at[own], buf.at[own], phase, in_group(lax.rem(place + k, group)))

    def wait_all(buf, phase):
        arrived(phase, buf.at[pl.ds(0, (group - 1) * part)])

    def gather_to(target, buf, phase):
        for k in range(1, mps):
            send(buf.at[own], buf.at[own], phase, {"section": target, "mp": lax.rem(mp + k, mps)})

        @pl.when(s != target)
        def _():
            send(buf.at[own], buf.at[own], phase, {"section": 1 - s})

    def left_to(target, buf, phase):
        @pl.when(s != target)
        def _():
            left(phase, buf.at[pl.ds(0, mps * part)])

        @pl.when(s == target)
        def _():
            left(phase, buf.at[pl.ds(0, (mps - 1) * part)])

    def scatter(src, dst, phase):
        for k in range(1, group):
            p = lax.rem(place + k, group)
            send(src.at[pl.ds(pl.multiple_of(p * part, part), part)], dst.at[place], phase, in_group(p))
        dst[place] = src[own]

    def scatter_from(src, dst, phase):
        for k in range(1, group):
            p = lax.rem(place + k, group)
            send(src.at[pl.ds(pl.multiple_of(p * part, part), part)], dst.at[mp], phase, in_group(p))
        dst[mp] = src[own]

    def wait_from(source, dst, phase):
        @pl.when(s == source)
        def _():
            arrived(phase, dst.at[pl.ds(0, mps - 1)])

        @pl.when(s != source)
        def _():
            arrived(phase, dst)

    def total(ref, first=0, last=None):
        last = ref.shape[0] if last is None else last
        value = full(ref[first])
        for i in range(first + 1, last):
            value = value + full(ref[i])
        return value

    pairs = [
        (m, h, slice(m * length, (m + 1) * length), slice(h * size, (h + 1) * size))
        for m in range(micro)
        for h in range(heads)
    ]

    def attention(n_ref, out):
        for t, w in enumerate((wq_ref, wk_ref, wv_ref)):
            qkv[t] = low(nt(n_ref[...], w[...]))
        tops, scores = [], []
        for m, h, r, lanes in pairs:
            raw = nt(qkv[0, r, lanes], qkv[1, r, lanes]) * scale + bias[h]
            scores.append(jnp.where(mask[m] > 0, raw, NEGATIVE))
        tops = [jnp.max(raw, axis=-1, keepdims=True) for raw in scores]
        powers = [jnp.exp(raw - top) for raw, top in zip(scores, tops)]
        sums = [jnp.sum(e, axis=-1, keepdims=True) for e in powers]
        lows = []
        for i, (m, h, r, lanes) in enumerate(pairs):
            p = powers[i] / sums[i]
            probs[m * heads + h] = p
            lows.append(low(p))
        for i, (m, h, r, lanes) in enumerate(pairs):
            o[r, lanes] = low(nn(lows[i], qkv[2, r, lanes]))
        out[...] = low(nn(o[...], wo_ref[...]))

    def attention_back(g_ref, out):
        do[...] = low(nt(g_ref[...], wo_ref[...]))
        dps = [nt(do[r, lanes], qkv[2, r, lanes]) for m, h, r, lanes in pairs]
        for m, h, r, lanes in pairs:
            dv = tn(low(probs[m * heads + h]), do[r, lanes])
            dqkv[r, 2 * local + h * size : 2 * local + (h + 1) * size] = low(dv)
        sums = [
            jnp.sum(dp * probs[m * heads + h], axis=-1, keepdims=True)
            for dp, (m, h, r, lanes) in zip(dps, pairs)
        ]
        grads = [
            low(probs[m * heads + h] * (dp - total_row))
            for dp, total_row, (m, h, r, lanes) in zip(dps, sums, pairs)
        ]
        for ds, (m, h, r, lanes) in zip(grads, pairs):
            dqkv[r, h * size : (h + 1) * size] = low(nn(ds, qkv[1, r, lanes]) * scale)
        for ds, (m, h, r, lanes) in zip(grads, pairs):
            dqkv[r, local + h * size : local + (h + 1) * size] = low(tn(ds, qkv[0, r, lanes]) * scale)
        for h in range(heads):
            dsum[h] = sum(full(grads[m * heads + h]) for m in range(micro))
        dn = nn(dqkv[:, 0:local], wq_ref[...]) + nn(dqkv[:, local : 2 * local], wk_ref[...])
        dn = dn + nn(dqkv[:, 2 * local : 3 * local], wv_ref[...])
        out[...] = low(dn)
        return dn

    def attention_weights(n_ref, g_ref):
        grads = low(tn(dqkv[...], n_ref[...]))
        last = low(tn(o[...], g_ref[...]))
        for t in range(width // 128):
            lanes = slice(t * 128, (t + 1) * 128)
            attn_own[t, 0 : 3 * local] = grads[:, lanes]
            attn_own[t, 3 * local :] = last[:, lanes]
        attn_sum[0]()
        found = bucket[...]
        for h in range(heads):
            held = dsum[h]
            for b in range(c["buckets"]):
                bias_rows[b : b + 1, :] = jnp.sum(jnp.where(found == b, held, 0.0), axis=0, keepdims=True)
            sums = nt(jnp.ones((8, length), F32), bias_rows[...], HIGHEST)
            smallb_send[1 + h : 2 + h, 0 : c["buckets"]] = sums[0:1]

    def reducer(own, out, base, split, first_recv, middles, second_recv):
        n = side_size
        quarter, step = width // n, width // (n * n)
        tiles = own.shape[0]

        def half_of(i):
            f, g = (fast, slow) if i == 0 else (slow, fast)
            to_f = (lambda p: slow * n + p) if i == 0 else (lambda p: p * n + fast)
            to_g = (lambda p: p * n + fast) if i == 0 else (lambda p: slow * n + p)
            lanes = pl.ds(0, split) if i == 0 else pl.ds(split, tiles - split)
            return f, g, to_f, to_g, lanes, base + i

        def many(p, size):
            return pl.ds(pl.multiple_of(p * size, 16), size)

        def one():
            for i in range(2):
                f, g, to_f, to_g, lanes, which = half_of(i)
                for k in range(1, n):
                    p = lax.rem(f + k, n)
                    src = own.at[lanes, many(p, quarter)]
                    send(src, first_recv[i].at[f], which, {"expert": to_f(p)})
                first_recv[i][f] = own[lanes, many(f, quarter)]

        def two():
            for i in range(2):
                f, g, to_f, to_g, lanes, which = half_of(i)
                arrived(which, first_recv[i].at[pl.ds(0, n - 1)])
                middles[i][...] = low(total(first_recv[i]))
                for k in range(1, n):
                    p = lax.rem(g + k, n)
                    src = middles[i].at[:, many(p, step)]
                    send(src, second_recv[i].at[g], which + 2, {"expert": to_g(p)})
                second_recv[i][g] = middles[i][:, many(g, step)]

        def three():
            for i in range(2):
                f, g, to_f, to_g, lanes, which = half_of(i)
                arrived(which + 2, second_recv[i].at[pl.ds(0, n - 1)])
                at = out.at[lanes, many(f * n + g, step)]
                at[...] = low(total(second_recv[i]))
                for k in range(1, n):
                    send(at, at, which + 4, {"expert": to_g(lax.rem(g + k, n))})

        def four():
            for i in range(2):
                f, g, to_f, to_g, lanes, which = half_of(i)
                arrived(which + 4, second_recv[i].at[pl.ds(0, n - 1)])
                at = out.at[lanes, many(f, quarter)]
                for k in range(1, n):
                    send(at, at, which + 6, {"expert": to_f(lax.rem(f + k, n))})

        def five():
            for i in range(2):
                arrived(base + i + 6, first_recv[i].at[pl.ds(0, n - 1)])

        def done():
            for i in range(2):
                for stage in range(4):
                    ref = (first_recv, second_recv, second_recv, first_recv)[stage][i]
                    left(base + i + 2 * stage, ref.at[pl.ds(0, n - 1)])

        return one, two, three, four, five, done

    phase("attention1")
    dense_sum = reducer(
        dense_own, dense_ref, DENSE_SUM, 5, (dense_a1, dense_b1), (dense_am, dense_bm), (dense_a2, dense_b2)
    )
    attn_sum = reducer(
        attn_own, attn_ref, ATTN_SUM, 3, (attn_a1, attn_b1), (attn_am, attn_bm), (attn_a2, attn_b2)
    )

    x = full(x_ref[...])
    @pl.when(s == 0)
    def _():
        n1[...] = normed(x, gains[0, 0:1])
        attention(n1, sends.at[0])
        scatter_from(sends.at[0], recv4.at[0], TERM1)

    phase("early")
    named = []
    before = low(jnp.where(row_at < col_at, 1.0, 0.0))
    expert_at = lax.broadcasted_iota(jnp.int32, (length, length), 0)
    slot_at = full(lax.broadcasted_iota(jnp.int32, (cap, length), 0))
    for m in range(micro):
        r = slice(m * length, (m + 1) * length)
        wide = [
            jnp.where(expert_at == routes_ref[2 * m + ch : 2 * m + ch + 1, :], 1.0, 0.0)
            for ch in range(2)
        ]
        hots = [hot[0:experts] for hot in wide]
        rank = nn(low(hots[0] + hots[1]), before)
        for e in range(experts):
            fit = slot_at == rank[e : e + 1]
            at = slice(e * cap, (e + 1) * cap)
            pick0[m, at] = low(jnp.where(fit, hots[0][e : e + 1], 0.0))
            pick1[m, at] = low(jnp.where(fit, hots[1][e : e + 1], 0.0))
        named.append(hots)
        place_rows = slice(m * cap, (m + 1) * cap)
        out_rows = low(nn(pick0[m] + pick1[m], gy_ref[r, mine]))
        ex[:, place_rows, 0:half] = out_rows.reshape(experts, cap, half)
        other = low(nt(pick0[m], low(wide[1])) + nt(pick1[m], low(wide[0])))
        ex[:, place_rows, half:] = other.reshape(experts, cap, 128)
    if side_size == 4:
        offsets = [(0, 1), (0, 3), (1, 0), (3, 0), (1, 1), (3, 3), (1, 3), (3, 1)]
        offsets += [(2, 1), (2, 3), (1, 2), (3, 2), (0, 0), (0, 2), (2, 0), (2, 2)]
    else:
        offsets = [(a, b) for a in range(side_size) for b in range(side_size)]

    def to_slot(src, dst, k, which):
        if offsets[k] == (0, 0):
            pltpu.make_async_copy(src.at[me], dst.at[s, pl.ds(k * slots, slots)], recv_sem.at[which]).start()
        else:
            p = at_offset(*offsets[k])
            send(src.at[p], dst.at[s, pl.ds(k * slots, slots)], which, {"expert": p})

    def to_token(src, dst, k, which):
        src = src.at[pl.ds(k * slots, slots)]
        if offsets[k] == (0, 0):
            pltpu.make_async_copy(src, dst.at[me], recv_sem.at[which]).start()
        else:
            dz, dy = offsets[k]
            send(src, dst.at[me], which, {"expert": at_offset(side_size - dz, side_size - dy)})

    for k in range(experts):
        to_slot(ex, ey, k, EARLY)
    phase("term1_wait")
    arrived(GAINS, gains.at[1 - s])
    wait_from(0, recv4.at[0], TERM1)
    phase("norm1")
    h1 = full(x_ref[own]) + total(recv4.at[0])
    chunk[H1] = h1
    rows1[own] = normed(h1, gains[0, 1:2])
    gather_all(rows1, ROWS1)
    phase("rows1_wait")
    wait_all(rows1, ROWS1)
    phase("dense")
    for copy in staged[0:3]:
        copy.wait()
    gate1[...] = nn(rows1[...], dense_gate_ref[...])
    up1[...] = nn(rows1[...], dense_up_ref[...])
    hid1[...] = low(gelu_parts(gate1[...])[0] * up1[...])
    sends[1] = low(nn(hid1[...], dense_down_ref[...]))
    scatter(sends.at[1], recv8.at[0], DENSE)
    phase("dense_wait")
    arrived(DENSE, recv8.at[0, pl.ds(0, group - 1)])
    phase("norm2")
    y1 = chunk[H1] + total(recv8.at[0])
    chunk[Y1] = y1
    rows2[own] = normed(y1, gains[1, 0:1])
    gather_to(1, rows2, ROWS2)

    phase("attention2")
    @pl.when(s == 1)
    def _():
        wait_all(rows2, ROWS2)
        attention(rows2, sends.at[2])
        scatter_from(sends.at[2], recv4.at[1], TERM2)

    phase("early_forward")
    arrived(EARLY, ey.at[s])
    send(ey.at[s], ey.at[s], EARLY_FORWARD, {"section": 1 - s})

    phase("term2_wait")
    wait_from(1, recv4.at[1], TERM2)
    phase("norm3")
    h2 = chunk[Y1] + total(recv4.at[1])
    chunk[H2] = h2
    rows3[own] = normed(h2, gains[1, 1:2])
    gather_all(rows3, ROWS3)
    phase("rows3_wait")
    wait_all(rows3, ROWS3)
    phase("slots")
    for m in range(micro):
        r = slice(m * length, (m + 1) * length)
        out_rows = low(nn(pick0[m] + pick1[m], rows3[r, mine]))
        sx[:, m * cap : (m + 1) * cap, :] = out_rows.reshape(experts, cap, half)

    def dispatch(j):
        for k in range(j * per, (j + 1) * per):
            to_slot(sx, rx, k, DISPATCH + j)

    def dispatched(j):
        count = sum(offsets[k] != (0, 0) for k in range(j * per, (j + 1) * per))
        if count:
            left(DISPATCH + j, rx.at[0, pl.ds(0, count * slots)])

    def forward(j):
        at = pl.ds(j * block, block)
        arrived(DISPATCH + j, rx.at[s, at])
        send(rx.at[s, at], rx.at[s, at], FORWARD + j, {"section": 1 - s})

    def give_back(j):
        at = pl.ds(j * block, block)
        arrived(CORE + j, cr.at[at])
        rt[at, 0:half] = low(full(cs[s, at]) + full(cr[at]))
        for k in range(j * per, (j + 1) * per):
            to_token(rt, rb, k, RETURN)

    phase("dispatch_wait")
    dispatch(0)
    dispatch(1)
    forward(0)
    dispatched(0)
    dispatch(2)
    for copy in staged[3:6]:
        copy.wait()
    arrived(EARLY_FORWARD, ey.at[1 - s])
    named_here = lax.broadcasted_iota(jnp.int32, (block, 128), 1)
    for j in range(blocks):
        at = pl.ds(j * block, block)
        phase("forward_wait%d" % j)
        arrived(FORWARD + j, rx.at[1 - s, at])
        phase("expert%d" % j)
        x0, x1 = rx[0, at, 0:half], rx[1, at, 0:half]
        logits = nt(x0, wide_router[:, 0:half]) + nt(x1, wide_router[:, half:])
        this = jnp.sum(jnp.where(named_here == me, logits, 0.0), axis=-1, keepdims=True)
        other = jnp.sum(full(ey[0, at, half:]) * logits, axis=-1, keepdims=True)
        top = jnp.maximum(this, other)
        e0, e1 = jnp.exp(this - top), jnp.exp(other - top)
        gate = e0 / (e0 + e1)
        gates[at] = jnp.broadcast_to(gate, (block, 128))
        g0, g1 = low(gate * full(ey[0, at, 0:half])), low(gate * full(ey[1, at, 0:half]))
        dout[at, 0:half] = g0
        dout[at, half:] = g1
        a = nn(x0, gate_ref[0:half]) + nn(x1, gate_ref[half:])
        u = nn(x0, up_ref[0:half]) + nn(x1, up_ref[half:])
        d = nt(g0, down_ref[:, 0:half]) + nt(g1, down_ref[:, half:])
        value, slope = gelu_parts(a)
        held = low(value * u)
        hid[at] = held
        term = jnp.sum(d * full(held), axis=-1, keepdims=True)
        rt[at, half:] = low(jnp.where(named_here == 0, term, 0.0))
        da[at] = low(d * u * slope)
        du[at] = low(d * value)
        for side in range(sections):
            w = slice(side * half, (side + 1) * half)
            cs[side, at] = low(nt(da[at], gate_ref[w]) + nt(du[at], up_ref[w]))
        send(cs.at[1 - s, at], cr.at[at], CORE + j, {"section": 1 - s})
        phase("give_back%d" % j)
        if j + 1 < blocks:
            forward(j + 1)
            dispatched(j + 1)
            if j + 3 < blocks:
                dispatch(j + 3)
        if j > 0:
            give_back(j - 1)
    give_back(blocks - 1)
    phase("outputs")
    for j in range(blocks):
        at = pl.ds(j * block, block)
        for side in range(sections):
            w = slice(side * half, (side + 1) * half)
            cs2[side, at] = low(nn(hid[at], down_ref[:, w]) * gates[at][:, 0:1])
        send(cs2.at[1 - s, at], cr2.at[at], CORE2, {"section": 1 - s})
    phase("expert_weights")
    for side in range(sections):
        w = slice(side * half, (side + 1) * half)
        ge_gate_ref[w] = low(tn(rx[side], da[...]))
        ge_up_ref[w] = low(tn(rx[side], du[...]))
        ge_down_ref[:, w] = low(tn(hid[...], dout[:, w]))
    for copy in staged[6:]:
        copy.start()
    arrived(CORE2, cr2)
    for j in range(blocks):
        at = pl.ds(j * block, block)
        rt2[at] = low(full(cs2[s, at]) + full(cr2[at]))
        for k in range(j * per, (j + 1) * per):
            to_token(rt2, rb2, k, RETURN2)
    phase("return_wait")
    arrived(RETURN, rb)
    phase("combine")
    lane = lax.broadcasted_iota(jnp.int32, (length, 128), 1)
    for m in range(micro):
        r = slice(m * length, (m + 1) * length)
        held = rb[:, m * cap : (m + 1) * cap, :].reshape(experts * cap, half + 128)
        moe_send[r, 0:half] = low(tn(pick0[m] + pick1[m], held[:, 0:half]))
        t0, t1 = tn(pick0[m], held[:, half:]), tn(pick1[m], held[:, half:])
        moe_send[r, half:] = low(jnp.where(lane == 0, t0, jnp.where(lane == 1, t1[:, 0:1], 0.0)))
    scatter(moe_send, moe_recv, MOE)
    phase("moe_wait")
    arrived(MOE, moe_recv.at[pl.ds(0, group - 1)])
    phase("norm3_back")
    lower, upper = total(moe_recv, 0, mps), total(moe_recv, mps, group)
    h2 = chunk[H2]
    terms = lower[:, half:] + upper[:, half:]
    t0, t1 = terms[:, 0:1], terms[:, 1:2]
    ahead = lax.rem(place * part, length)
    token = lax.broadcasted_iota(jnp.int32, (part, length), 1)
    is_own = low(jnp.where(token == lax.broadcasted_iota(jnp.int32, (part, length), 0) + ahead, 1.0, 0.0))
    hot0, hot1 = (
        nt(is_own, low(jnp.where(place * part < length, named[0][ch], named[1][ch]))) for ch in range(2)
    )
    logits = nt(rows3[own], router_ref[...])
    l0 = jnp.sum(hot0 * logits, axis=-1, keepdims=True)
    l1 = jnp.sum(hot1 * logits, axis=-1, keepdims=True)
    top = jnp.maximum(l0, l1)
    e0, e1 = jnp.exp(l0 - top), jnp.exp(l1 - top)
    dlogits = hot0 * (t0 - e0 / (e0 + e1) * (t0 + t1)) + hot1 * (t1 - e1 / (e0 + e1) * (t0 + t1))
    dr = jnp.concatenate([lower[:, 0:half], upper[:, 0:half]], axis=1)
    dr = dr + nn(dlogits, full(router_ref[...]), HIGHEST)
    back, gain = normed_back(h2, gains[1, 1:2], dr)
    grad = full(gy_ref[own]) + back
    chunk[GRAD] = grad
    grad2[own] = low(grad)
    gather_to(1, grad2, GRAD2)
    small[...] = jnp.zeros_like(small)
    small[0:1] = gain
    small[8 : 8 + experts] = tn(dlogits, full(rows3[own]), HIGHEST)
    smallb_send[...] = jnp.zeros_like(smallb_send)

    phase("attention2_back")
    @pl.when(s == 1)
    def _():
        wait_all(grad2, GRAD2)
        attention_back(grad2, sends.at[3])
        scatter_from(sends.at[3], recv4.at[2], BACK2)
        attention_weights(rows2, grad2)

    phase("output")
    arrived(RETURN2, rb2)
    for m in range(micro):
        held = rb2[:, m * cap : (m + 1) * cap, :].reshape(experts * cap, half)
        out_send[m * length : (m + 1) * length] = low(tn(pick0[m] + pick1[m], held))
    scatter(out_send, out_recv, MOE2)
    phase("back2_wait")
    wait_from(1, recv4.at[2], BACK2)
    phase("norm2_back")
    back, gain = normed_back(chunk[Y1], gains[1, 0:1], total(recv4.at[2]))
    small[1:2] = gain
    grad = chunk[GRAD] + back
    chunk[GRAD] = grad
    grad1[own] = low(grad)
    gather_all(grad1, GRAD1)
    phase("grad1_wait")
    wait_all(grad1, GRAD1)
    phase("dense_back")
    d = nt(grad1[...], dense_down_ref[...])
    value, slope = gelu_parts(gate1[...])
    da1[...] = low(d * up1[...] * slope)
    du1[...] = low(d * value)
    sends[4] = low(nt(da1[...], dense_gate_ref[...]) + nt(du1[...], dense_up_ref[...]))
    scatter(sends.at[4], recv8.at[1], BACK1)
    phase("dense_weights")
    gate_grad = low(tn(rows1[...], da1[...]))
    up_grad = low(tn(rows1[...], du1[...]))
    for t in range(ff // 128):
        lanes = slice(t * 128, (t + 1) * 128)
        dense_own[t] = gate_grad[:, lanes]
        dense_own[ff // 128 + t] = up_grad[:, lanes]
    down_grad = low(tn(hid1[...], grad1[...]))
    for t in range(width // 128):
        at = slice(t % 2 * ff, t % 2 * ff + ff)
        dense_own[2 * (ff // 128) + t // 2, at] = down_grad[:, t * 128 : (t + 1) * 128]
    dense_sum[0]()
    phase("back1_wait")
    arrived(BACK1, recv8.at[1, pl.ds(0, group - 1)])
    phase("norm1_back")
    back, gain = normed_back(chunk[H1], gains[0, 1:2], total(recv8.at[1]))
    small[2:3] = gain
    grad = chunk[GRAD] + back
    chunk[GRAD] = grad
    grad0[own] = low(grad)
    gather_to(0, grad0, GRAD0)
    small_send[...] = low(small[...])
    for k in range(1, group):
        send(small_send, small_recv.at[place], SMALL_A, in_group(lax.rem(place + k, group)))
    small_recv[place] = small_send[...]

    phase("out")
    arrived(MOE2, out_recv.at[pl.ds(0, group - 1)])
    out_ref[own, 0:half] = low(chunk[H2][:, 0:half] + total(out_recv, 0, mps))
    out_ref[own, half:] = low(chunk[H2][:, half:] + total(out_recv, mps, group))
    gather_all(out_ref, OUT)
    phase("dense_two")
    dense_sum[1]()

    phase("attention1_back")
    @pl.when(s == 0)
    def _():
        wait_all(grad0, GRAD0)
        dn = attention_back(grad0, sends.at[5])
        scatter_from(sends.at[5], recv4.at[3], BACK0)
        x = full(x_ref[...])
        smallb_send[0:1] = jnp.sum(dn * x * inverse_rms(x), axis=0, keepdims=True)

    @pl.when(s == 1)
    def _():
        for stage in attn_sum[1:]:
            stage()

    phase("dense_three")
    dense_sum[2]()
    phase("attn_one")
    @pl.when(s == 0)
    def _():
        attention_weights(n1, grad0)

    phase("dense_four")
    dense_sum[3]()
    for k in range(1, experts):
        send(smallb_send, smallb_recv.at[me], SMALL_B, on_expert(k))
    smallb_recv[me] = smallb_send[...]
    phase("back0_wait")
    wait_from(0, recv4.at[3], BACK0)
    phase("norm0_back")
    back, gain = normed_back(full(x_ref[own]), gains[0, 0:1], total(recv4.at[3]))
    input_ref[own] = low(chunk[GRAD] + back)
    gather_all(input_ref, INPUT)
    phase("attn_two")
    @pl.when(s == 0)
    def _():
        attn_sum[1]()

    phase("small_a")
    arrived(SMALL_A, small_recv.at[pl.ds(0, group - 1)])
    small2_send[...] = low(total(small_recv))
    for k in range(1, experts):
        send(small2_send, small2_recv.at[me], SMALL_A2, on_expert(k))
    small2_recv[me] = small2_send[...]
    phase("attn_three")
    @pl.when(s == 0)
    def _():
        attn_sum[2]()

    phase("small_b")
    arrived(SMALL_B, smallb_recv.at[pl.ds(0, experts - 1)])
    smallb2_send[...] = total(smallb_recv)
    for k in range(1, mps):
        send(smallb2_send, smallb2_recv.at[mp], SMALL_B2, {"mp": lax.rem(mp + k, mps)})
    smallb2_recv[mp] = smallb2_send[...]
    phase("attn_four")
    @pl.when(s == 0)
    def _():
        attn_sum[3]()

    arrived(SMALL_A2, small2_recv.at[pl.ds(0, experts - 1)])
    summed = total(small2_recv)
    for h in range(heads):
        bias_grad_ref[h] = smallb2_send[1 + h : 2 + h, 0 : c["buckets"]]
    arrived(SMALL_B2, smallb2_recv.at[pl.ds(0, mps - 1)])
    gain0 = total(smallb2_recv)[0:1]
    small_ref[...] = summed
    small_ref[0:1] = jnp.where(s == 0, gain0, summed[1:2])
    small_ref[1:2] = jnp.where(s == 0, summed[2:3], summed[0:1])
    phase("last_waits")
    wait_all(out_ref, OUT)
    wait_all(input_ref, INPUT)
    dense_sum[4]()

    @pl.when(s == 0)
    def _():
        attn_sum[4]()
        attn_sum[5]()

    for copy in staged[6:]:
        copy.wait()
    dense_sum[5]()
    left(GAINS, gains.at[s])
    seven = pl.ds(0, (group - 1) * part)
    for phase, ref in ((ROWS1, rows1), (ROWS3, rows3), (OUT, out_ref), (GRAD1, grad1), (INPUT, input_ref)):
        left(phase, ref.at[seven])
    for phase, at in ((DENSE, 1), (BACK1, 4)):
        left(phase, sends.at[at, seven])
    left(MOE, moe_send.at[seven])
    left(MOE2, out_send.at[seven])
    left(EARLY, ey.at[0, pl.ds(0, (experts - 1) * slots)])
    left(EARLY_FORWARD, ey.at[0])
    left(CORE2, cr2)
    left(RETURN2, rb2.at[pl.ds(0, experts - 1)])
    left_to(1, rows2, ROWS2)
    left_to(1, grad2, GRAD2)
    left_to(0, grad0, GRAD0)

    @pl.when(s == 0)
    def _():
        left(TERM1, sends.at[0, seven])
        left(BACK0, sends.at[5, seven])

    @pl.when(s == 1)
    def _():
        left(TERM2, sends.at[2, seven])
        left(BACK2, sends.at[3, seven])

    for j in range(blocks):
        left(FORWARD + j, rx.at[0, pl.ds(0, block)])
        left(CORE + j, cr.at[pl.ds(0, block)])
    left(RETURN, rb.at[pl.ds(0, experts - 1)])
    left(SMALL_A, small_recv.at[pl.ds(0, group - 1)])
    left(SMALL_A2, small2_recv.at[pl.ds(0, experts - 1)])
    left(SMALL_B, smallb_recv.at[pl.ds(0, experts - 1)])
    left(SMALL_B2, smallb2_recv.at[pl.ds(0, mps - 1)])
    scopes.close()


def widen(tiles, experts, out, back, attn, gate, up, down, e_gate, e_up, e_down, small, bias, *to):
    to[0][...] = full(out[...])
    to[1][...] = full(back[...])
    for t in range(2 * tiles):
        lanes = slice(t * 128, (t + 1) * 128)
        for which in range(4):
            to[2 + which][:, lanes] = full(attn[t, which])
        to[8][:, lanes] = full(down[t // 2, t % 2])
    for t in range(tiles):
        lanes = slice(t * 128, (t + 1) * 128)
        to[6][:, lanes] = full(gate[t])
        to[7][:, lanes] = full(up[t])
    to[9][...] = full(e_gate[...])
    to[10][...] = full(e_up[...])
    to[11][...] = full(e_down[...])
    to[12][...] = small[0:1]
    to[13][...] = small[1:2]
    to[14][...] = small[8 : 8 + experts]
    to[15][...] = bias[...]


def shards(
    block_input,
    segments,
    routes,
    cotangent,
    attn_gain,
    query_weight,
    key_weight,
    value_weight,
    out_weight,
    pos_bias,
    ffn_gain,
    dense_gate,
    dense_up,
    dense_down,
    router,
    expert_gate,
    expert_up,
    expert_down,
):
    micro, _, length, width = block_input.shape
    experts = router.shape[1]
    cap = 4 * length // experts
    buckets, heads = pos_bias.shape[1:]
    local = query_weight.shape[2]
    size = local // heads
    ff = dense_gate.shape[1]
    sections, mps = lax.axis_size("section"), lax.axis_size("mp")
    group = sections * mps
    rows = micro * length
    part = rows // group
    half = width // sections
    slots = micro * cap
    every = experts * slots
    step = width // experts
    side = int(np.sqrt(experts))
    c = dict(
        side=side,
        section=sections, expert=experts, mp=mps, micro=micro, length=length, heads=heads, size=size,
        cap=cap, width=width, ff=ff, buckets=buckets,
    )
    vmem = pl.BlockSpec(memory_space=pltpu.VMEM)
    hbm = pl.BlockSpec(memory_space=pl.ANY)

    def held(*shape):
        return pltpu.VMEM(shape, BF16)

    def exact(*shape):
        return pltpu.VMEM(shape, F32)

    scratch = [
        pltpu.SemaphoreType.DMA((SEMAPHORES,)),
        pltpu.SemaphoreType.DMA((SEMAPHORES,)),
        exact(sections, 8, width),
        pltpu.VMEM((length, length), jnp.int32),
        exact(heads, length, length),
        exact(micro, length, length),
        held(rows, width),
        held(3, rows, local),
        exact(micro * heads, length, length),
        held(rows, local),
        held(rows, local),
        held(rows, 3 * local),
        exact(heads, length, length),
        exact(buckets, length),
        held(6, rows, width),
        held(4, mps, part, width),
        held(2, group, part, width),
        held(rows, width),
        held(rows, width),
        held(rows, width),
        held(rows, width),
        held(rows, width),
        held(rows, width),
        exact(4, part, width),
        held(rows, ff),
        exact(rows, ff),
        exact(rows, ff),
        held(rows, ff),
        held(rows, ff),
        held(micro, experts * cap, length),
        held(micro, experts * cap, length),
        held(experts, slots, half + 128),
        held(sections, every, half + 128),
        held(experts, slots, half),
        held(sections, every, half),
        held(every, ff),
        held(every, ff),
        held(every, ff),
        held(every, width),
        exact(every, 128),
        held(sections, every, half),
        held(every, half),
        held(every, half + 128),
        held(experts, slots, half + 128),
        held(sections, every, half),
        held(every, half),
        held(every, half),
        held(experts, slots, half),
        held(rows, half + 128),
        held(group, part, half + 128),
        held(rows, half),
        held(group, part, half),
        exact(32, width),
        held(32, width),
        held(group, 32, width),
        held(32, width),
        held(experts, 32, width),
        exact(8, width),
        exact(experts, 8, width),
        exact(8, width),
        exact(mps, 8, width),
        held(9, width, 128),
        held(side, 5, width // side, 128),
        held(side, 4, width // side, 128),
        held(5, width // side, 128),
        held(4, width // side, 128),
        held(side, 5, step, 128),
        held(side, 4, step, 128),
        held(6, width, 128),
        held(side, 3, width // side, 128),
        held(side, 3, width // side, 128),
        held(3, width // side, 128),
        held(3, width // side, 128),
        held(side, 3, step, 128),
        held(side, 3, step, 128),
        held(width, ff),
        held(width, ff),
        held(ff, width),
        held(width, ff),
        held(width, ff),
        held(ff, width),
        held(width, ff),
        held(width, ff),
        held(ff, width),
        pltpu.SemaphoreType.DMA((9,)),
        held(128, width),
    ]
    shape = jax.ShapeDtypeStruct
    block_output, input_grad, attn, dense, ge_gate, ge_up, ge_down, small, bias_grad = pl.pallas_call(
        functools.partial(kernel, c),
        out_shape=(
            shape((rows, width), BF16),
            shape((rows, width), BF16),
            shape((6, 4 * local, 128), BF16),
            shape((9, width, 128), BF16),
            shape((width, ff), BF16),
            shape((width, ff), BF16),
            shape((ff, width), BF16),
            shape((32, width), F32),
            shape((heads, 1, buckets), F32),
        ),
        in_specs=[vmem] * 12 + [hbm] * 6,
        out_specs=(vmem,) * 4 + (hbm,) * 3 + (vmem,) * 2,
        scratch_shapes=scratch,
        compiler_params=pltpu.CompilerParams(
            collective_id=0, has_side_effects=True, vmem_limit_bytes=60 * 1024 * 1024
        ),
    )(
        block_input.reshape(rows, width),
        cotangent.reshape(rows, width),
        segments.reshape(micro, length),
        routes[:, 0].transpose(0, 2, 1).reshape(2 * micro, length),
        attn_gain,
        ffn_gain,
        pos_bias.transpose(2, 0, 1),
        query_weight[0].T,
        key_weight[0].T,
        value_weight[0].T,
        out_weight[0],
        router.T,
        dense_gate,
        dense_up,
        dense_down,
        expert_gate[0],
        expert_up[0],
        expert_down[0],
    )
    steps = 4

    def rows_of(rows, width):
        return pl.BlockSpec((rows // steps, width), lambda i: (i, 0))

    def whole(*dims):
        return pl.BlockSpec(dims, lambda i: (0,) * len(dims))

    tiles = ff // 128
    attn_shape = shape((local, width), F32)
    results = pl.pallas_call(
        functools.partial(widen, tiles, experts),
        grid=(steps,),
        out_shape=(
            shape((rows, width), F32),
            shape((rows, width), F32),
            *[attn_shape] * 4,
            shape((width, ff), F32),
            shape((width, ff), F32),
            shape((ff, width), F32),
            shape((width, ff), F32),
            shape((width, ff), F32),
            shape((ff, width), F32),
            shape((1, width), F32),
            shape((1, width), F32),
            shape((experts, width), F32),
            shape((heads, 1, buckets), F32),
        ),
        in_specs=[
            rows_of(rows, width),
            rows_of(rows, width),
            pl.BlockSpec((2 * tiles, 4, local // steps, 128), lambda i: (0, 0, i, 0)),
            pl.BlockSpec((tiles, width // steps, 128), lambda i: (0, i, 0)),
            pl.BlockSpec((tiles, width // steps, 128), lambda i: (1, i, 0)),
            pl.BlockSpec((tiles, 2, ff // steps, 128), lambda i: (2, 0, i, 0)),
            rows_of(width, ff),
            rows_of(width, ff),
            rows_of(ff, width),
            whole(32, width),
            whole(heads, 1, buckets),
        ],
        out_specs=(
            rows_of(rows, width),
            rows_of(rows, width),
            *[rows_of(local, width)] * 4,
            rows_of(width, ff),
            rows_of(width, ff),
            rows_of(ff, width),
            rows_of(width, ff),
            rows_of(width, ff),
            rows_of(ff, width),
            whole(1, width),
            whole(1, width),
            whole(experts, width),
            whole(heads, 1, buckets),
        ),
        compiler_params=pltpu.CompilerParams(vmem_limit_bytes=63 * 1024 * 1024),
    )(
        block_output,
        input_grad,
        attn.reshape(2 * tiles, 4, local, 128),
        dense,
        dense,
        dense.reshape(3 * tiles, 2, ff, 128),
        ge_gate,
        ge_up,
        ge_down,
        small,
        bias_grad,
    )
    return (
        results[0].reshape(block_input.shape),
        results[1].reshape(block_input.shape),
        results[12],
        results[2].T[None],
        results[3].T[None],
        results[4].T[None],
        results[5][None],
        results[15].transpose(1, 2, 0),
        results[13],
        results[6],
        results[7],
        results[8],
        results[14].T,
        results[9][None],
        results[10][None],
        results[11][None],
    )


def solution(mesh):
    placed = (
        P(None, "expert", None, None),
        P(None, "expert", None),
        P(None, "expert", None, None),
        P(None, "expert", None, None),
        P("section", None),
        P("section", None, "mp"),
        P("section", None, "mp"),
        P("section", None, "mp"),
        P("section", "mp", None),
        P("section", None, "mp"),
        P("section", None),
        P(None, ("section", "mp")),
        P(None, ("section", "mp")),
        P(("section", "mp"), None),
        P(),
        P("expert", None, ("section", "mp")),
        P("expert", None, ("section", "mp")),
        P("expert", ("section", "mp"), None),
    )
    return jax.shard_map(
        shards,
        mesh=mesh,
        in_specs=placed,
        out_specs=(
            P(None, "expert", None, None),
            P(None, "expert", None, None),
            P("section", None),
            P("section", None, "mp"),
            P("section", None, "mp"),
            P("section", None, "mp"),
            P("section", "mp", None),
            P("section", None, "mp"),
            P("section", None),
            P(None, ("section", "mp")),
            P(None, ("section", "mp")),
            P(("section", "mp"), None),
            P(),
            P("expert", None, ("section", "mp")),
            P("expert", None, ("section", "mp")),
            P("expert", ("section", "mp"), None),
        ),
        check_vma=False,
    )
```

```python
import contextlib
import functools

import jax
import jax.numpy as jnp
import numpy as np
from jax import lax
from jax.experimental import pallas as pl
from jax.experimental.pallas import tpu as pltpu
from jax.sharding import PartitionSpec as P

EPSILON = 1e-06
NEGATIVE = -1e30
BF16, F32 = jnp.bfloat16, jnp.float32
MESH = pl.DeviceIdType.MESH
HIGHEST = lax.Precision.HIGHEST

GAINS, TERM1, ROWS1, DENSE, ROWS2, TERM2, ROWS3, MOE, OUT, GRAD2, BACK2 = range(11)
GRAD1, BACK1, GRAD0, BACK0, INPUT, SMALL_A, SMALL_A2, SMALL_B, SMALL_B2 = range(11, 20)
DISPATCH, FORWARD, CORE, RETURN = 20, 24, 28, 32
DENSE_SUM, ATTN_SUM = 33, 41
EARLY, EARLY_FORWARD, CORE2, RETURN2, MOE2 = range(49, 54)
SMALL_A3, SMALL_B3 = 54, 55
SEMAPHORES = 56


def bucket_limits(count):
    exact = count // 2
    limits = []
    for level in range(1, count):
        if level < exact:
            limits.append(level)
        else:
            distance = exact
            while (
                min(
                    count - 1,
                    exact + int(np.floor(np.log(distance / exact) / np.log(128.0 / exact) * exact)),
                )
                < level
            ):
                distance += 1
            limits.append(distance)
    return limits


def dot(left, right, dims, precision=None):
    return lax.dot_general(
        left, right, (((dims[0],), (dims[1],)), ((), ())), precision=precision, preferred_element_type=F32
    )


def nn(left, right, precision=None):
    return dot(left, right, (1, 0), precision)


def nt(left, right, precision=None):
    return dot(left, right, (1, 1), precision)


def tn(left, right, precision=None):
    return dot(left, right, (0, 0), precision)


def low(value):
    return value.astype(BF16)


def full(value):
    return value.astype(F32)


def inverse_rms(rows):
    return lax.rsqrt(jnp.mean(rows * rows, axis=-1, keepdims=True) + EPSILON)


def normed(rows, gain):
    return low(rows * inverse_rms(rows) * gain)


def normed_back(rows, gain, grad):
    rho = inverse_rms(rows)
    scaled = grad * gain
    back = scaled * rho - rows * (rho * rho * rho) * jnp.mean(scaled * rows, axis=-1, keepdims=True)
    return back, jnp.sum(grad * rows * rho, axis=0, keepdims=True)


def gelu_parts(a):
    t = jnp.tanh(0.7978845608028654 * (a + 0.044715 * a * a * a))
    half = 0.5 * (1.0 + t)
    slope = half + 0.5 * a * (1.0 - t * t) * (0.7978845608028654 * (1.0 + 0.134145 * a * a))
    return a * half, slope


def kernel(
    c,
    x_hbm,
    gy_hbm,
    docs_ref,
    routes_ref,
    attn_gain_ref,
    ffn_gain_ref,
    table_ref,
    wq_hbm,
    wk_hbm,
    wv_hbm,
    wo_hbm,
    router_hbm,
    dense_gate_hbm,
    dense_up_hbm,
    dense_down_hbm,
    gate_hbm,
    up_hbm,
    down_hbm,
    out_hbm,
    input_hbm,
    attn_hbm,
    dense_hbm,
    ge_gate_hbm,
    ge_up_hbm,
    ge_down_hbm,
    small_ref,
    bias_grad_ref,
    send_sem,
    recv_sem,
    gains,
    bucket,
    bias,
    mask,
    n1,
    qkv,
    probs,
    o,
    do,
    dqkv,
    dsum,
    bias_rows,
    sends,
    recv4,
    recv8,
    rows1,
    rows2,
    rows3,
    grad2,
    grad1,
    grad0,
    chunk,
    hid1,
    gate1,
    up1,
    da1,
    du1,
    pick0,
    pick1,
    ex,
    ey,
    sx,
    rx,
    hid,
    da,
    du,
    dout,
    gates,
    cs,
    cr,
    rt,
    rb,
    cs2,
    cr2,
    rt2,
    rb2,
    moe_send,
    moe_recv,
    out_send,
    out_recv,
    small,
    small_send,
    small_recv,
    small2_send,
    small2_recv,
    small3_send,
    small3_recv,
    smallb_send,
    smallb_recv,
    smallb3_send,
    smallb3_recv,
    smallb2_send,
    smallb2_recv,
    dense_own,
    dense_a1,
    dense_b1,
    dense_am,
    dense_bm,
    dense_a2,
    dense_b2,
    attn_own,
    attn_a1,
    attn_b1,
    attn_am,
    attn_bm,
    attn_a2,
    attn_b2,
    dense_gate_ref,
    dense_up_ref,
    dense_down_ref,
    gate_ref,
    up_ref,
    down_ref,
    ge_gate_ref,
    ge_up_ref,
    ge_down_ref,
    stage_sem,
    wide_router,
    x_ref,
    gy_ref,
    wq_ref,
    wk_ref,
    wv_ref,
    wo_ref,
    router_ref,
    out_ref,
    input_ref,
    attn_ref,
    dense_ref,
    d0,
):
    sections, experts, mps = c["section"], c["expert"], c["mp"]
    micro, length, heads, size, cap = c["micro"], c["length"], c["heads"], c["size"], c["cap"]
    width, ff = c["width"], c["ff"]
    group = sections * mps
    rows = micro * length
    part = rows // group
    half = width // sections
    local = heads * size
    scale = size**-0.5
    slots = micro * cap
    s, me, mp = lax.axis_index("section"), lax.axis_index("expert"), lax.axis_index("mp")
    place = s * mps + mp
    own = pl.ds(pl.multiple_of(place * part, part), part)
    mine = pl.ds(pl.multiple_of(s * half, 128), half)
    H2, Y1, H1, GRAD = 0, 1, 2, 3
    staged = [
        pltpu.make_async_copy(src, dst, stage_sem.at[i])
        for i, (src, dst) in enumerate(
            (
                (dense_gate_hbm, dense_gate_ref),
                (dense_up_hbm, dense_up_ref),
                (dense_down_hbm, dense_down_ref),
                (gate_hbm, gate_ref),
                (up_hbm, up_ref),
                (down_hbm, down_ref),
                (ge_gate_ref, ge_gate_hbm),
                (ge_up_ref, ge_up_hbm),
                (ge_down_ref, ge_down_hbm),
                (x_hbm, x_ref),
                (wq_hbm, wq_ref),
                (wk_hbm, wk_ref),
                (wv_hbm, wv_ref),
                (wo_hbm, wo_ref),
                (router_hbm, router_ref),
                (gy_hbm, gy_ref),
                (out_ref, out_hbm),
                (input_ref, input_hbm),
                (dense_ref, dense_hbm),
                (attn_ref, attn_hbm),
            )
        )
    ]
    for copy in staged[9:16] + staged[0:6]:
        copy.start()
    blocks = 4
    per = experts // blocks
    block = per * slots
    side_size = c["side"]
    slow, fast = me // side_size, lax.rem(me, side_size)

    def at_offset(dz, dy):
        z, y = lax.rem(slow + dz, side_size), lax.rem(fast + dy, side_size)
        return z * side_size + y

    scopes = contextlib.ExitStack()

    def phase(name):
        scopes.close()
        scopes.enter_context(jax.named_scope(name))

    def on_expert(k):
        return {"expert": lax.rem(me + k, experts)}

    def in_group(p):
        return {"section": p // mps, "mp": lax.rem(p, mps)}

    def send(src, dst, which, device, arrival=None):
        pltpu.make_async_remote_copy(
            src_ref=src,
            dst_ref=dst,
            send_sem=send_sem.at[which],
            recv_sem=recv_sem.at[which if arrival is None else arrival],
            device_id=device,
            device_id_type=MESH,
        ).start()

    def drain(sem, view):
        pltpu.make_async_copy(view, view, sem).wait()

    def arrived(phase, view):
        drain(recv_sem.at[phase], view)

    def left(phase, view):
        drain(send_sem.at[phase], view)

    phase("signals")
    barrier = pltpu.get_barrier_semaphore()
    for k in range(1, group):
        pl.semaphore_signal(barrier, inc=1, device_id=in_group(lax.rem(place + k, group)), device_id_type=MESH)
    for k in range(1, experts):
        pl.semaphore_signal(barrier, inc=1, device_id=on_expert(k), device_id_type=MESH)

    phase("tables")
    gains[s] = jnp.zeros((8, width), F32)
    gains[s, 0:1] = attn_gain_ref[...]
    gains[s, 1:2] = ffn_gain_ref[...]
    row_at = lax.broadcasted_iota(jnp.int32, (length, length), 0)
    col_at = lax.broadcasted_iota(jnp.int32, (length, length), 1)
    found = jnp.zeros((length, length), jnp.int32)
    for limit in bucket_limits(c["buckets"]):
        found = found + jnp.where(row_at - col_at >= limit, 1, 0)
    bucket[...] = found
    wide_router[...] = jnp.zeros_like(wide_router)
    for h in range(heads):
        total = jnp.zeros((length, length), F32)
        for b in range(c["buckets"]):
            total = jnp.where(found == b, table_ref[h][:, b : b + 1], total)
        bias[h] = total
    for m in range(micro):
        docs = jnp.broadcast_to(full(docs_ref[m : m + 1, :]), (length, length))
        same = (docs == jnp.transpose(docs)) & (col_at <= row_at)
        mask[m] = jnp.where(same, 1.0, 0.0)
    phase("barrier")
    pl.semaphore_wait(barrier, group - 1 + experts - 1)
    send(gains.at[s], gains.at[s], GAINS, {"section": 1 - s})

    def gather_all(buf, phase):
        for k in range(1, group):
            send(buf.at[own], buf.at[own], phase, in_group(lax.rem(place + k, group)))

    def wait_all(buf, phase):
        arrived(phase, buf.at[pl.ds(0, (group - 1) * part)])

    def gather_to(target, buf, phase):
        for k in range(1, mps):
            send(buf.at[own], buf.at[own], phase, {"section": target, "mp": lax.rem(mp + k, mps)})

        @pl.when(s != target)
        def _():
            send(buf.at[own], buf.at[own], phase, {"section": 1 - s})

    def left_to(target, buf, phase):
        @pl.when(s != target)
        def _():
            left(phase, buf.at[pl.ds(0, mps * part)])

        @pl.when(s == target)
        def _():
            left(phase, buf.at[pl.ds(0, (mps - 1) * part)])

    def scatter(src, dst, phase):
        for k in range(1, group):
            p = lax.rem(place + k, group)
            send(src.at[pl.ds(pl.multiple_of(p * part, part), part)], dst.at[place], phase, in_group(p))
        dst[place] = src[own]

    def scatter_from(src, dst, phase):
        for k in range(1, group):
            p = lax.rem(place + k, group)
            send(src.at[pl.ds(pl.multiple_of(p * part, part), part)], dst.at[mp], phase, in_group(p))
        dst[mp] = src[own]

    def wait_from(source, dst, phase):
        @pl.when(s == source)
        def _():
            arrived(phase, dst.at[pl.ds(0, mps - 1)])

        @pl.when(s != source)
        def _():
            arrived(phase, dst)

    def total(ref, first=0, last=None):
        last = ref.shape[0] if last is None else last
        value = full(ref[first])
        for i in range(first + 1, last):
            value = value + full(ref[i])
        return value

    pairs = [
        (m, h, slice(m * length, (m + 1) * length), slice(h * size, (h + 1) * size))
        for m in range(micro)
        for h in range(heads)
    ]

    def attention(n_ref, out):
        for t, w in enumerate((wq_ref, wk_ref, wv_ref)):
            qkv[t] = low(nt(n_ref[...], w[...]))
        tops, scores = [], []
        for m, h, r, lanes in pairs:
            raw = nt(qkv[0, r, lanes], qkv[1, r, lanes]) * scale + bias[h]
            scores.append(jnp.where(mask[m] > 0, raw, NEGATIVE))
        tops = [jnp.max(raw, axis=-1, keepdims=True) for raw in scores]
        powers = [jnp.exp(raw - top) for raw, top in zip(scores, tops)]
        sums = [jnp.sum(e, axis=-1, keepdims=True) for e in powers]
        lows = []
        for i, (m, h, r, lanes) in enumerate(pairs):
            p = powers[i] / sums[i]
            probs[m * heads + h] = p
            lows.append(low(p))
        for i, (m, h, r, lanes) in enumerate(pairs):
            o[r, lanes] = low(nn(lows[i], qkv[2, r, lanes]))
        out[...] = low(nn(o[...], wo_ref[...]))

    def attention_back(g_ref, out, between=None):
        do[...] = low(nt(g_ref[...], wo_ref[...]))
        dps = [nt(do[r, lanes], qkv[2, r, lanes]) for m, h, r, lanes in pairs]
        for m, h, r, lanes in pairs:
            dv = tn(low(probs[m * heads + h]), do[r, lanes])
            dqkv[r, 2 * local + h * size : 2 * local + (h + 1) * size] = low(dv)
        sums = [
            jnp.sum(dp * probs[m * heads + h], axis=-1, keepdims=True)
            for dp, (m, h, r, lanes) in zip(dps, pairs)
        ]
        grads = [
            low(probs[m * heads + h] * (dp - total_row))
            for dp, total_row, (m, h, r, lanes) in zip(dps, sums, pairs)
        ]
        if between is not None:
            between()
        for ds, (m, h, r, lanes) in zip(grads, pairs):
            dqkv[r, h * size : (h + 1) * size] = low(nn(ds, qkv[1, r, lanes]) * scale)
        for ds, (m, h, r, lanes) in zip(grads, pairs):
            dqkv[r, local + h * size : local + (h + 1) * size] = low(tn(ds, qkv[0, r, lanes]) * scale)
        for h in range(heads):
            dsum[h] = sum(full(grads[m * heads + h]) for m in range(micro))
        dn = nn(dqkv[:, 0:local], wq_ref[...]) + nn(dqkv[:, local : 2 * local], wk_ref[...])
        dn = dn + nn(dqkv[:, 2 * local : 3 * local], wv_ref[...])
        out[...] = low(dn)
        return dn

    def attention_weights(n_ref, g_ref):
        grads = low(tn(dqkv[...], n_ref[...]))
        last = low(tn(o[...], g_ref[...]))
        for t in range(width // 128):
            lanes = slice(t * 128, (t + 1) * 128)
            attn_own[t, 0 : 3 * local] = grads[:, lanes]
            attn_own[t, 3 * local :] = last[:, lanes]
        attn_sum[0]()

    def bias_sums():
        found = bucket[...]
        for h in range(heads):
            held = dsum[h]
            for b in range(c["buckets"]):
                bias_rows[b : b + 1, :] = jnp.sum(jnp.where(found == b, held, 0.0), axis=0, keepdims=True)
            sums = nt(jnp.ones((8, length), F32), bias_rows[...], HIGHEST)
            smallb_send[1 + h : 2 + h, 0 : c["buckets"]] = sums[0:1]

    def reducer(own, out, base, split, first_recv, middles, second_recv):
        n = side_size
        quarter, step = width // n, width // (n * n)
        tiles = own.shape[0]

        def half_of(i):
            f, g = (fast, slow) if i == 0 else (slow, fast)
            to_f = (lambda p: slow * n + p) if i == 0 else (lambda p: p * n + fast)
            to_g = (lambda p: p * n + fast) if i == 0 else (lambda p: slow * n + p)
            lanes = pl.ds(0, split) if i == 0 else pl.ds(split, tiles - split)
            return f, g, to_f, to_g, lanes, base + i

        def many(p, size):
            return pl.ds(pl.multiple_of(p * size, 16), size)

        def one():
            for i in range(2):
                f, g, to_f, to_g, lanes, which = half_of(i)
                for k in range(1, n):
                    p = lax.rem(f + k, n)
                    src = own.at[lanes, many(p, quarter)]
                    send(src, first_recv[i].at[f], which, {"expert": to_f(p)})
                first_recv[i][f] = own[lanes, many(f, quarter)]

        def two():
            for i in range(2):
                f, g, to_f, to_g, lanes, which = half_of(i)
                arrived(which, first_recv[i].at[pl.ds(0, n - 1)])
                middles[i][...] = low(total(first_recv[i]))
                for k in range(1, n):
                    p = lax.rem(g + k, n)
                    src = middles[i].at[:, many(p, step)]
                    send(src, second_recv[i].at[g], which + 2, {"expert": to_g(p)})
                second_recv[i][g] = middles[i][:, many(g, step)]

        def three():
            for i in range(2):
                f, g, to_f, to_g, lanes, which = half_of(i)
                arrived(which + 2, second_recv[i].at[pl.ds(0, n - 1)])
                at = out.at[lanes, many(f * n + g, step)]
                at[...] = low(total(second_recv[i]))
                for k in range(1, n):
                    send(at, at, which + 4, {"expert": to_g(lax.rem(g + k, n))})

        def four():
            for i in range(2):
                f, g, to_f, to_g, lanes, which = half_of(i)
                arrived(which + 4, second_recv[i].at[pl.ds(0, n - 1)])
                at = out.at[lanes, many(f, quarter)]
                for k in range(1, n):
                    send(at, at, which + 6, {"expert": to_f(lax.rem(f + k, n))})

        def five():
            for i in range(2):
                arrived(base + i + 6, first_recv[i].at[pl.ds(0, n - 1)])

        def done():
            for i in range(2):
                for stage in range(4):
                    ref = (first_recv, second_recv, second_recv, first_recv)[stage][i]
                    left(base + i + 2 * stage, ref.at[pl.ds(0, n - 1)])

        return one, two, three, four, five, done

    phase("attention1")
    dense_sum = reducer(
        dense_own, dense_ref, DENSE_SUM, 5, (dense_a1, dense_b1), (dense_am, dense_bm), (dense_a2, dense_b2)
    )
    attn_sum = reducer(
        attn_own, attn_ref, ATTN_SUM, 3, (attn_a1, attn_b1), (attn_am, attn_bm), (attn_a2, attn_b2)
    )

    for copy in staged[9:16]:
        copy.wait()
    wide_router[0:experts] = router_ref[...]
    x = full(x_ref[...])
    @pl.when(s == 0)
    def _():
        n1[...] = normed(x, gains[0, 0:1])
        attention(n1, sends.at[0])
        scatter_from(sends.at[0], recv4.at[0], TERM1)

    phase("early")
    named = []
    before = low(jnp.where(row_at < col_at, 1.0, 0.0))
    expert_at = lax.broadcasted_iota(jnp.int32, (length, length), 0)
    slot_at = full(lax.broadcasted_iota(jnp.int32, (cap, length), 0))
    for m in range(micro):
        r = slice(m * length, (m + 1) * length)
        wide = [
            jnp.where(expert_at == routes_ref[2 * m + ch : 2 * m + ch + 1, :], 1.0, 0.0)
            for ch in range(2)
        ]
        hots = [hot[0:experts] for hot in wide]
        rank = nn(low(hots[0] + hots[1]), before)
        for e in range(experts):
            fit = slot_at == rank[e : e + 1]
            at = slice(e * cap, (e + 1) * cap)
            pick0[m, at] = low(jnp.where(fit, hots[0][e : e + 1], 0.0))
            pick1[m, at] = low(jnp.where(fit, hots[1][e : e + 1], 0.0))
        named.append(hots)
        place_rows = slice(m * cap, (m + 1) * cap)
        out_rows = low(nn(pick0[m] + pick1[m], gy_ref[r, mine]))
        ex[:, place_rows, 0:half] = out_rows.reshape(experts, cap, half)
        other = low(nt(pick0[m], low(wide[1])) + nt(pick1[m], low(wide[0])))
        ex[:, place_rows, half:] = other.reshape(experts, cap, 128)
    if side_size == 4:
        offsets = [(0, 1), (0, 3), (1, 0), (3, 0), (1, 1), (3, 3), (1, 3), (3, 1)]
        offsets += [(2, 1), (2, 3), (1, 2), (3, 2), (0, 0), (0, 2), (2, 0), (2, 2)]
    else:
        offsets = [(a, b) for a in range(side_size) for b in range(side_size)]

    def to_slot(src, dst, k, which):
        if offsets[k] == (0, 0):
            pltpu.make_async_copy(src.at[me], dst.at[s, pl.ds(k * slots, slots)], recv_sem.at[which]).start()
        else:
            p = at_offset(*offsets[k])
            send(src.at[p], dst.at[s, pl.ds(k * slots, slots)], which, {"expert": p})

    def to_token(src, dst, k, which):
        src = src.at[pl.ds(k * slots, slots)]
        if offsets[k] == (0, 0):
            pltpu.make_async_copy(src, dst.at[me], recv_sem.at[which]).start()
        else:
            dz, dy = offsets[k]
            send(src, dst.at[me], which, {"expert": at_offset(side_size - dz, side_size - dy)})

    for k in range(experts):
        to_slot(ex, ey, k, EARLY)
    phase("term1_wait")
    arrived(GAINS, gains.at[1 - s])
    wait_from(0, recv4.at[0], TERM1)
    phase("norm1")
    h1 = full(x_ref[own]) + total(recv4.at[0])
    chunk[H1] = h1
    rows1[own] = normed(h1, gains[0, 1:2])
    gather_all(rows1, ROWS1)
    phase("rows1_wait")
    wait_all(rows1, ROWS1)
    phase("dense")
    for copy in staged[0:3]:
        copy.wait()
    gate1[...] = nn(rows1[...], dense_gate_ref[...])
    up1[...] = nn(rows1[...], dense_up_ref[...])
    hid1[...] = low(gelu_parts(gate1[...])[0] * up1[...])
    sends[1] = low(nn(hid1[...], dense_down_ref[...]))
    scatter(sends.at[1], recv8.at[0], DENSE)
    phase("dense_wait")
    arrived(DENSE, recv8.at[0, pl.ds(0, group - 1)])
    phase("norm2")
    y1 = chunk[H1] + total(recv8.at[0])
    chunk[Y1] = y1
    rows2[own] = normed(y1, gains[1, 0:1])
    gather_to(1, rows2, ROWS2)

    phase("early_forward")
    arrived(EARLY, ey.at[s])
    send(ey.at[s], ey.at[s], EARLY_FORWARD, {"section": 1 - s})
    phase("attention2")
    @pl.when(s == 1)
    def _():
        wait_all(rows2, ROWS2)
        attention(rows2, sends.at[2])
        scatter_from(sends.at[2], recv4.at[1], TERM2)

    phase("early_hidden")
    staged[5].wait()
    arrived(EARLY_FORWARD, ey.at[1 - s])
    for j in range(blocks):
        at = pl.ds(j * block, block)
        d0[at] = nt(ey[0, at, 0:half], down_ref[:, 0:half]) + nt(ey[1, at, 0:half], down_ref[:, half:])

    phase("term2_wait")
    wait_from(1, recv4.at[1], TERM2)
    phase("norm3")
    h2 = chunk[Y1] + total(recv4.at[1])
    chunk[H2] = h2
    rows3[own] = normed(h2, gains[1, 1:2])
    for k in range(1, group):
        p = in_group(lax.rem(place + k, group))
        src = rows3.at[own, pl.ds(pl.multiple_of(p["section"] * half, 128), half)]
        send(src, src, ROWS3, p)
    phase("rows3_wait")
    arrived(ROWS3, rows3.at[pl.ds(0, (group - 1) * part), pl.ds(0, half)])
    phase("slots")
    for m in range(micro):
        r = slice(m * length, (m + 1) * length)
        out_rows = low(nn(pick0[m] + pick1[m], rows3[r, mine]))
        sx[:, m * cap : (m + 1) * cap, :] = out_rows.reshape(experts, cap, half)

    def dispatch(j):
        for k in range(j * per, (j + 1) * per):
            to_slot(sx, rx, k, DISPATCH + j)

    def dispatched(j):
        count = sum(offsets[k] != (0, 0) for k in range(j * per, (j + 1) * per))
        if count:
            left(DISPATCH + j, rx.at[0, pl.ds(0, count * slots)])

    def forward(j):
        at = pl.ds(j * block, block)
        arrived(DISPATCH + j, rx.at[s, at])
        send(rx.at[s, at], rx.at[s, at], FORWARD + j, {"section": 1 - s})

    def give_back(j):
        at = pl.ds(j * block, block)
        arrived(CORE + j, cr.at[at])
        rt[at, 0:half] = low(full(cs[s, at]) + full(cr[at]))
        for k in range(j * per, (j + 1) * per):
            to_token(rt, rb, k, RETURN)

    phase("dispatch_wait")
    dispatch(0)
    dispatch(1)
    forward(0)
    dispatched(0)
    dispatch(2)
    for copy in staged[3:5]:
        copy.wait()
    named_here = lax.broadcasted_iota(jnp.int32, (block, 128), 1)
    for j in range(blocks):
        at = pl.ds(j * block, block)
        phase("forward_wait%d" % j)
        arrived(FORWARD + j, rx.at[1 - s, at])
        phase("expert%d" % j)
        x0, x1 = rx[0, at, 0:half], rx[1, at, 0:half]
        logits = nt(x0, wide_router[:, 0:half]) + nt(x1, wide_router[:, half:])
        this = jnp.sum(jnp.where(named_here == me, logits, 0.0), axis=-1, keepdims=True)
        other = jnp.sum(full(ey[0, at, half:]) * logits, axis=-1, keepdims=True)
        top = jnp.maximum(this, other)
        e0, e1 = jnp.exp(this - top), jnp.exp(other - top)
        gate = e0 / (e0 + e1)
        gates[at] = jnp.broadcast_to(gate, (block, 128))
        a = nn(x0, gate_ref[0:half]) + nn(x1, gate_ref[half:])
        u = nn(x0, up_ref[0:half]) + nn(x1, up_ref[half:])
        d = gate * d0[at]
        value, slope = gelu_parts(a)
        held = low(value * u)
        hid[at] = held
        term = jnp.sum(d * full(held), axis=-1, keepdims=True)
        rt[at, half:] = low(jnp.where(named_here == 0, term, 0.0))
        da[at] = low(d * u * slope)
        du[at] = low(d * value)
        for side in range(sections):
            w = slice(side * half, (side + 1) * half)
            cs[side, at] = low(nt(da[at], gate_ref[w]) + nt(du[at], up_ref[w]))
        send(cs.at[1 - s, at], cr.at[at], CORE + j, {"section": 1 - s})
        phase("give_back%d" % j)
        if j + 1 < blocks:
            forward(j + 1)
            dispatched(j + 1)
            if j + 3 < blocks:
                dispatch(j + 3)
        if j > 0:
            give_back(j - 1)
    give_back(blocks - 1)
    phase("outputs")
    for j in range(blocks):
        at = pl.ds(j * block, block)
        for side in range(sections):
            w = slice(side * half, (side + 1) * half)
            cs2[side, at] = low(nn(hid[at], down_ref[:, w]) * gates[at][:, 0:1])
        send(cs2.at[1 - s, at], cr2.at[at], CORE2, {"section": 1 - s})
    phase("expert_weights")
    for j in range(blocks):
        at = pl.ds(j * block, block)
        for side in range(sections):
            w = slice(side * half, (side + 1) * half)
            dout[at, w] = low(gates[at][:, 0:1] * full(ey[side, at, 0:half]))
    for side in range(sections):
        w = slice(side * half, (side + 1) * half)
        ge_gate_ref[w] = low(tn(rx[side], da[...]))
        ge_up_ref[w] = low(tn(rx[side], du[...]))
        ge_down_ref[:, w] = low(tn(hid[...], dout[:, w]))
    for copy in staged[6:9]:
        copy.start()
    arrived(CORE2, cr2)
    for j in range(blocks):
        at = pl.ds(j * block, block)
        rt2[at] = low(full(cs2[s, at]) + full(cr2[at]))
        for k in range(j * per, (j + 1) * per):
            to_token(rt2, rb2, k, RETURN2)
    phase("return_wait")
    arrived(RETURN, rb)
    phase("combine")
    lane = lax.broadcasted_iota(jnp.int32, (length, 128), 1)
    for m in range(micro):
        r = slice(m * length, (m + 1) * length)
        held = rb[:, m * cap : (m + 1) * cap, :].reshape(experts * cap, half + 128)
        moe_send[r, 0:half] = low(tn(pick0[m] + pick1[m], held[:, 0:half]))
        t0, t1 = tn(pick0[m], held[:, half:]), tn(pick1[m], held[:, half:])
        moe_send[r, half:] = low(jnp.where(lane == 0, t0, jnp.where(lane == 1, t1[:, 0:1], 0.0)))
    scatter(moe_send, moe_recv, MOE)
    phase("moe_wait")
    arrived(MOE, moe_recv.at[pl.ds(0, group - 1)])
    phase("norm3_back")
    lower, upper = total(moe_recv, 0, mps), total(moe_recv, mps, group)
    h2 = chunk[H2]
    terms = lower[:, half:] + upper[:, half:]
    t0, t1 = terms[:, 0:1], terms[:, 1:2]
    ahead = lax.rem(place * part, length)
    token = lax.broadcasted_iota(jnp.int32, (part, length), 1)
    is_own = low(jnp.where(token == lax.broadcasted_iota(jnp.int32, (part, length), 0) + ahead, 1.0, 0.0))
    hot0, hot1 = (
        nt(is_own, low(jnp.where(place * part < length, named[0][ch], named[1][ch]))) for ch in range(2)
    )
    logits = nt(rows3[own], router_ref[...])
    l0 = jnp.sum(hot0 * logits, axis=-1, keepdims=True)
    l1 = jnp.sum(hot1 * logits, axis=-1, keepdims=True)
    top = jnp.maximum(l0, l1)
    e0, e1 = jnp.exp(l0 - top), jnp.exp(l1 - top)
    dlogits = hot0 * (t0 - e0 / (e0 + e1) * (t0 + t1)) + hot1 * (t1 - e1 / (e0 + e1) * (t0 + t1))
    dr = jnp.concatenate([lower[:, 0:half], upper[:, 0:half]], axis=1)
    dr = dr + nn(dlogits, full(router_ref[...]), HIGHEST)
    back, gain = normed_back(h2, gains[1, 1:2], dr)
    grad = full(gy_ref[own]) + back
    chunk[GRAD] = grad
    grad2[own] = low(grad)
    gather_to(1, grad2, GRAD2)
    small[...] = jnp.zeros_like(small)
    small[0:1] = gain
    small[8 : 8 + experts] = tn(dlogits, full(rows3[own]), HIGHEST)
    smallb_send[...] = jnp.zeros_like(smallb_send)

    phase("attention2_back")
    @pl.when(s == 1)
    def _():
        wait_all(grad2, GRAD2)
        attention_back(grad2, sends.at[3])
        scatter_from(sends.at[3], recv4.at[2], BACK2)
        attention_weights(rows2, grad2)
        bias_sums()

    phase("output")
    arrived(RETURN2, rb2)
    for m in range(micro):
        held = rb2[:, m * cap : (m + 1) * cap, :].reshape(experts * cap, half)
        out_send[m * length : (m + 1) * length] = low(tn(pick0[m] + pick1[m], held))
    scatter(out_send, out_recv, MOE2)
    phase("back2_wait")
    wait_from(1, recv4.at[2], BACK2)
    phase("norm2_back")
    back, gain = normed_back(chunk[Y1], gains[1, 0:1], total(recv4.at[2]))
    small[1:2] = gain
    grad = chunk[GRAD] + back
    chunk[GRAD] = grad
    grad1[own] = low(grad)
    gather_all(grad1, GRAD1)
    phase("grad1_wait")
    wait_all(grad1, GRAD1)
    phase("dense_back")
    d = nt(grad1[...], dense_down_ref[...])
    value, slope = gelu_parts(gate1[...])
    da1[...] = low(d * up1[...] * slope)
    du1[...] = low(d * value)
    sends[4] = low(nt(da1[...], dense_gate_ref[...]) + nt(du1[...], dense_up_ref[...]))
    scatter(sends.at[4], recv8.at[1], BACK1)
    phase("dense_weights")
    gate_grad = low(tn(rows1[...], da1[...]))
    up_grad = low(tn(rows1[...], du1[...]))
    for t in range(ff // 128):
        lanes = slice(t * 128, (t + 1) * 128)
        dense_own[t] = gate_grad[:, lanes]
        dense_own[ff // 128 + t] = up_grad[:, lanes]
    down_grad = low(tn(hid1[...], grad1[...]))
    for t in range(width // 128):
        at = slice(t % 2 * ff, t % 2 * ff + ff)
        dense_own[2 * (ff // 128) + t // 2, at] = down_grad[:, t * 128 : (t + 1) * 128]
    dense_sum[0]()
    phase("back1_wait")
    arrived(BACK1, recv8.at[1, pl.ds(0, group - 1)])
    phase("norm1_back")
    back, gain = normed_back(chunk[H1], gains[0, 1:2], total(recv8.at[1]))
    small[2:3] = gain
    grad = chunk[GRAD] + back
    chunk[GRAD] = grad
    grad0[own] = low(grad)
    gather_to(0, grad0, GRAD0)
    small_send[...] = low(small[...])
    for k in range(1, group):
        send(small_send, small_recv.at[place], SMALL_A, in_group(lax.rem(place + k, group)))
    small_recv[place] = small_send[...]

    phase("out")
    arrived(MOE2, out_recv.at[pl.ds(0, group - 1)])
    out_ref[own, 0:half] = low(chunk[H2][:, 0:half] + total(out_recv, 0, mps))
    out_ref[own, half:] = low(chunk[H2][:, half:] + total(out_recv, mps, group))
    gather_all(out_ref, OUT)
    phase("attention1_back")
    @pl.when(s == 0)
    def _():
        wait_all(grad0, GRAD0)
        dn = attention_back(grad0, sends.at[5], dense_sum[1])
        scatter_from(sends.at[5], recv4.at[3], BACK0)
        dense_sum[2]()
        attention_weights(n1, grad0)
        x = full(x_ref[...])
        smallb_send[0:1] = jnp.sum(dn * x * inverse_rms(x), axis=0, keepdims=True)

    @pl.when(s == 1)
    def _():
        for stage in attn_sum[1:3]:
            stage()
        dense_sum[1]()
        attn_sum[3]()
        dense_sum[2]()

    def along(src, dst, which, fast_side):
        for k in range(1, side_size):
            p = at_offset(0, k) if fast_side else at_offset(k, 0)
            send(src, dst.at[fast if fast_side else slow], which, {"expert": p})
        dst[fast if fast_side else slow] = src[...]

    phase("small_a")
    arrived(SMALL_A, small_recv.at[pl.ds(0, group - 1)])
    small2_send[...] = low(total(small_recv))
    along(small2_send, small2_recv, SMALL_A2, True)
    phase("dense_four")
    dense_sum[3]()
    phase("bias")
    @pl.when(s == 0)
    def _():
        bias_sums()

    along(smallb_send, smallb_recv, SMALL_B, True)
    phase("back0_wait")
    wait_from(0, recv4.at[3], BACK0)
    phase("norm0_back")
    back, gain = normed_back(full(x_ref[own]), gains[0, 0:1], total(recv4.at[3]))
    input_ref[own] = low(chunk[GRAD] + back)
    gather_all(input_ref, INPUT)
    phase("attn_two")
    @pl.when(s == 0)
    def _():
        attn_sum[1]()

    phase("small_two")
    arrived(SMALL_A2, small2_recv.at[pl.ds(0, side_size - 1)])
    small3_send[...] = low(total(small2_recv))
    along(small3_send, small3_recv, SMALL_A3, False)
    arrived(SMALL_B, smallb_recv.at[pl.ds(0, side_size - 1)])
    smallb3_send[...] = total(smallb_recv)
    along(smallb3_send, smallb3_recv, SMALL_B3, False)
    phase("attn_three")
    @pl.when(s == 0)
    def _():
        attn_sum[2]()

    phase("small_three")
    arrived(SMALL_B3, smallb3_recv.at[pl.ds(0, side_size - 1)])
    smallb2_send[...] = total(smallb3_recv)
    for k in range(1, mps):
        send(smallb2_send, smallb2_recv.at[mp], SMALL_B2, {"mp": lax.rem(mp + k, mps)})
    smallb2_recv[mp] = smallb2_send[...]
    phase("attn_four")
    @pl.when(s == 0)
    def _():
        attn_sum[3]()

    arrived(SMALL_A3, small3_recv.at[pl.ds(0, side_size - 1)])
    summed = total(small3_recv)
    for h in range(heads):
        bias_grad_ref[h] = smallb2_send[1 + h : 2 + h, 0 : c["buckets"]]
    arrived(SMALL_B2, smallb2_recv.at[pl.ds(0, mps - 1)])
    gain0 = total(smallb2_recv)[0:1]
    small_ref[...] = summed
    small_ref[0:1] = jnp.where(s == 0, gain0, summed[1:2])
    small_ref[1:2] = jnp.where(s == 0, summed[2:3], summed[0:1])
    phase("last_waits")
    wait_all(out_ref, OUT)
    staged[16].start()
    wait_all(input_ref, INPUT)
    staged[17].start()
    dense_sum[4]()
    staged[18].start()
    attn_sum[4]()
    staged[19].start()
    attn_sum[5]()
    dense_sum[5]()
    left(GAINS, gains.at[s])
    seven = pl.ds(0, (group - 1) * part)
    left(ROWS3, rows3.at[seven, pl.ds(0, half)])
    for phase, ref in ((ROWS1, rows1), (OUT, out_ref), (GRAD1, grad1), (INPUT, input_ref)):
        left(phase, ref.at[seven])
    for phase, at in ((DENSE, 1), (BACK1, 4)):
        left(phase, sends.at[at, seven])
    left(MOE, moe_send.at[seven])
    left(MOE2, out_send.at[seven])
    left(EARLY, ey.at[0, pl.ds(0, (experts - 1) * slots)])
    left(EARLY_FORWARD, ey.at[0])
    left(CORE2, cr2)
    left(RETURN2, rb2.at[pl.ds(0, experts - 1)])
    left_to(1, rows2, ROWS2)
    left_to(1, grad2, GRAD2)
    left_to(0, grad0, GRAD0)

    @pl.when(s == 0)
    def _():
        left(TERM1, sends.at[0, seven])
        left(BACK0, sends.at[5, seven])

    @pl.when(s == 1)
    def _():
        left(TERM2, sends.at[2, seven])
        left(BACK2, sends.at[3, seven])

    for j in range(blocks):
        left(FORWARD + j, rx.at[0, pl.ds(0, block)])
        left(CORE + j, cr.at[pl.ds(0, block)])
    left(RETURN, rb.at[pl.ds(0, experts - 1)])
    left(SMALL_A, small_recv.at[pl.ds(0, group - 1)])
    three = pl.ds(0, side_size - 1)
    left(SMALL_A2, small2_recv.at[three])
    left(SMALL_A3, small3_recv.at[three])
    left(SMALL_B, smallb_recv.at[three])
    left(SMALL_B3, smallb3_recv.at[three])
    left(SMALL_B2, smallb2_recv.at[pl.ds(0, mps - 1)])
    for copy in staged[6:9] + staged[16:]:
        copy.wait()
    scopes.close()


def widen(tiles, experts, out, back, attn, gate, up, down, e_gate, e_up, e_down, small, bias, *to):
    to[0][...] = full(out[...])
    to[1][...] = full(back[...])
    for t in range(2 * tiles):
        lanes = slice(t * 128, (t + 1) * 128)
        for which in range(4):
            to[2 + which][:, lanes] = full(attn[t, which])
        to[8][:, lanes] = full(down[t // 2, t % 2])
    for t in range(tiles):
        lanes = slice(t * 128, (t + 1) * 128)
        to[6][:, lanes] = full(gate[t])
        to[7][:, lanes] = full(up[t])
    to[9][...] = full(e_gate[...])
    to[10][...] = full(e_up[...])
    to[11][...] = full(e_down[...])
    to[12][...] = small[0:1]
    to[13][...] = small[1:2]
    to[14][...] = small[8 : 8 + experts]
    to[15][...] = bias[...]


def shards(
    block_input,
    segments,
    routes,
    cotangent,
    attn_gain,
    query_weight,
    key_weight,
    value_weight,
    out_weight,
    pos_bias,
    ffn_gain,
    dense_gate,
    dense_up,
    dense_down,
    router,
    expert_gate,
    expert_up,
    expert_down,
):
    micro, _, length, width = block_input.shape
    experts = router.shape[1]
    cap = 4 * length // experts
    buckets, heads = pos_bias.shape[1:]
    local = query_weight.shape[2]
    size = local // heads
    ff = dense_gate.shape[1]
    sections, mps = lax.axis_size("section"), lax.axis_size("mp")
    group = sections * mps
    rows = micro * length
    part = rows // group
    half = width // sections
    slots = micro * cap
    every = experts * slots
    step = width // experts
    side = int(np.sqrt(experts))
    c = dict(
        side=side,
        section=sections, expert=experts, mp=mps, micro=micro, length=length, heads=heads, size=size,
        cap=cap, width=width, ff=ff, buckets=buckets,
    )
    vmem = pl.BlockSpec(memory_space=pltpu.VMEM)
    hbm = pl.BlockSpec(memory_space=pl.ANY)

    def held(*shape):
        return pltpu.VMEM(shape, BF16)

    def exact(*shape):
        return pltpu.VMEM(shape, F32)

    scratch = [
        pltpu.SemaphoreType.DMA((SEMAPHORES,)),
        pltpu.SemaphoreType.DMA((SEMAPHORES,)),
        exact(sections, 8, width),
        pltpu.VMEM((length, length), jnp.int32),
        exact(heads, length, length),
        exact(micro, length, length),
        held(rows, width),
        held(3, rows, local),
        exact(micro * heads, length, length),
        held(rows, local),
        held(rows, local),
        held(rows, 3 * local),
        exact(heads, length, length),
        exact(buckets, length),
        held(6, rows, width),
        held(4, mps, part, width),
        held(2, group, part, width),
        held(rows, width),
        held(rows, width),
        held(rows, width),
        held(rows, width),
        held(rows, width),
        held(rows, width),
        exact(4, part, width),
        held(rows, ff),
        exact(rows, ff),
        exact(rows, ff),
        held(rows, ff),
        held(rows, ff),
        held(micro, experts * cap, length),
        held(micro, experts * cap, length),
        held(experts, slots, half + 128),
        held(sections, every, half + 128),
        held(experts, slots, half),
        held(sections, every, half),
        held(every, ff),
        held(every, ff),
        held(every, ff),
        held(every, width),
        exact(every, 128),
        held(sections, every, half),
        held(every, half),
        held(every, half + 128),
        held(experts, slots, half + 128),
        held(sections, every, half),
        held(every, half),
        held(every, half),
        held(experts, slots, half),
        held(rows, half + 128),
        held(group, part, half + 128),
        held(rows, half),
        held(group, part, half),
        exact(32, width),
        held(32, width),
        held(group, 32, width),
        held(32, width),
        held(side, 32, width),
        held(32, width),
        held(side, 32, width),
        exact(8, width),
        exact(side, 8, width),
        exact(8, width),
        exact(side, 8, width),
        exact(8, width),
        exact(mps, 8, width),
        held(9, width, 128),
        held(side, 5, width // side, 128),
        held(side, 4, width // side, 128),
        held(5, width // side, 128),
        held(4, width // side, 128),
        held(side, 5, step, 128),
        held(side, 4, step, 128),
        held(6, width, 128),
        held(side, 3, width // side, 128),
        held(side, 3, width // side, 128),
        held(3, width // side, 128),
        held(3, width // side, 128),
        held(side, 3, step, 128),
        held(side, 3, step, 128),
        held(width, ff),
        held(width, ff),
        held(ff, width),
        held(width, ff),
        held(width, ff),
        held(ff, width),
        held(width, ff),
        held(width, ff),
        held(ff, width),
        pltpu.SemaphoreType.DMA((20,)),
        held(128, width),
        held(rows, width),
        held(rows, width),
        held(local, width),
        held(local, width),
        held(local, width),
        held(local, width),
        held(experts, width),
        held(rows, width),
        held(rows, width),
        held(6, 4 * local, 128),
        held(9, width, 128),
        exact(every, ff),
    ]
    shape = jax.ShapeDtypeStruct
    block_output, input_grad, attn, dense, ge_gate, ge_up, ge_down, small, bias_grad = pl.pallas_call(
        functools.partial(kernel, c),
        out_shape=(
            shape((rows, width), BF16),
            shape((rows, width), BF16),
            shape((6, 4 * local, 128), BF16),
            shape((9, width, 128), BF16),
            shape((width, ff), BF16),
            shape((width, ff), BF16),
            shape((ff, width), BF16),
            shape((32, width), F32),
            shape((heads, 1, buckets), F32),
        ),
        in_specs=[hbm] * 2 + [vmem] * 5 + [hbm] * 11,
        out_specs=(hbm,) * 7 + (vmem,) * 2,
        scratch_shapes=scratch,
        compiler_params=pltpu.CompilerParams(
            collective_id=0, has_side_effects=True, vmem_limit_bytes=60 * 1024 * 1024
        ),
    )(
        block_input.reshape(rows, width),
        cotangent.reshape(rows, width),
        segments.reshape(micro, length),
        routes[:, 0].transpose(0, 2, 1).reshape(2 * micro, length),
        attn_gain,
        ffn_gain,
        pos_bias.transpose(2, 0, 1),
        query_weight[0].T,
        key_weight[0].T,
        value_weight[0].T,
        out_weight[0],
        router.T,
        dense_gate,
        dense_up,
        dense_down,
        expert_gate[0],
        expert_up[0],
        expert_down[0],
    )
    steps = 4

    def rows_of(rows, width):
        return pl.BlockSpec((rows // steps, width), lambda i: (i, 0))

    def whole(*dims):
        return pl.BlockSpec(dims, lambda i: (0,) * len(dims))

    tiles = ff // 128
    attn_shape = shape((local, width), F32)
    results = pl.pallas_call(
        functools.partial(widen, tiles, experts),
        grid=(steps,),
        out_shape=(
            shape((rows, width), F32),
            shape((rows, width), F32),
            *[attn_shape] * 4,
            shape((width, ff), F32),
            shape((width, ff), F32),
            shape((ff, width), F32),
            shape((width, ff), F32),
            shape((width, ff), F32),
            shape((ff, width), F32),
            shape((1, width), F32),
            shape((1, width), F32),
            shape((experts, width), F32),
            shape((heads, 1, buckets), F32),
        ),
        in_specs=[
            rows_of(rows, width),
            rows_of(rows, width),
            pl.BlockSpec((2 * tiles, 4, local // steps, 128), lambda i: (0, 0, i, 0)),
            pl.BlockSpec((tiles, width // steps, 128), lambda i: (0, i, 0)),
            pl.BlockSpec((tiles, width // steps, 128), lambda i: (1, i, 0)),
            pl.BlockSpec((tiles, 2, ff // steps, 128), lambda i: (2, 0, i, 0)),
            rows_of(width, ff),
            rows_of(width, ff),
            rows_of(ff, width),
            whole(32, width),
            whole(heads, 1, buckets),
        ],
        out_specs=(
            rows_of(rows, width),
            rows_of(rows, width),
            *[rows_of(local, width)] * 4,
            rows_of(width, ff),
            rows_of(width, ff),
            rows_of(ff, width),
            rows_of(width, ff),
            rows_of(width, ff),
            rows_of(ff, width),
            whole(1, width),
            whole(1, width),
            whole(experts, width),
            whole(heads, 1, buckets),
        ),
        compiler_params=pltpu.CompilerParams(vmem_limit_bytes=63 * 1024 * 1024),
    )(
        block_output,
        input_grad,
        attn.reshape(2 * tiles, 4, local, 128),
        dense,
        dense,
        dense.reshape(3 * tiles, 2, ff, 128),
        ge_gate,
        ge_up,
        ge_down,
        small,
        bias_grad,
    )
    return (
        results[0].reshape(block_input.shape),
        results[1].reshape(block_input.shape),
        results[12],
        results[2].T[None],
        results[3].T[None],
        results[4].T[None],
        results[5][None],
        results[15].transpose(1, 2, 0),
        results[13],
        results[6],
        results[7],
        results[8],
        results[14].T,
        results[9][None],
        results[10][None],
        results[11][None],
    )


def solution(mesh):
    placed = (
        P(None, "expert", None, None),
        P(None, "expert", None),
        P(None, "expert", None, None),
        P(None, "expert", None, None),
        P("section", None),
        P("section", None, "mp"),
        P("section", None, "mp"),
        P("section", None, "mp"),
        P("section", "mp", None),
        P("section", None, "mp"),
        P("section", None),
        P(None, ("section", "mp")),
        P(None, ("section", "mp")),
        P(("section", "mp"), None),
        P(),
        P("expert", None, ("section", "mp")),
        P("expert", None, ("section", "mp")),
        P("expert", ("section", "mp"), None),
    )
    return jax.shard_map(
        shards,
        mesh=mesh,
        in_specs=placed,
        out_specs=(
            P(None, "expert", None, None),
            P(None, "expert", None, None),
            P("section", None),
            P("section", None, "mp"),
            P("section", None, "mp"),
            P("section", None, "mp"),
            P("section", "mp", None),
            P("section", None, "mp"),
            P("section", None),
            P(None, ("section", "mp")),
            P(None, ("section", "mp")),
            P(("section", "mp"), None),
            P(),
            P("expert", None, ("section", "mp")),
            P("expert", None, ("section", "mp")),
            P("expert", ("section", "mp"), None),
        ),
        check_vma=False,
    )
```

```python
import contextlib
import functools

import jax
import jax.numpy as jnp
import numpy as np
from jax import lax
from jax.experimental import pallas as pl
from jax.experimental.pallas import tpu as pltpu
from jax.sharding import PartitionSpec as P

EPSILON = 1e-06
NEGATIVE = -1e30
BF16, F32 = jnp.bfloat16, jnp.float32
MESH = pl.DeviceIdType.MESH
HIGHEST = lax.Precision.HIGHEST

GAINS, TERM1, ROWS1, DENSE, ROWS2, TERM2, ROWS3, MOE, OUT, GRAD2, BACK2 = range(11)
GRAD1, BACK1, GRAD0, BACK0, INPUT, SMALL_A, SMALL_A2, SMALL_B, SMALL_B2 = range(11, 20)
DISPATCH, FORWARD, CORE, RETURN = 20, 24, 28, 32
DENSE_SUM, ATTN_SUM = 33, 41
EARLY, EARLY_FORWARD, CORE2, RETURN2, MOE2 = range(49, 54)
SMALL_A3, SMALL_B3 = 54, 55
SEMAPHORES = 56


def bucket_limits(count):
    exact = count // 2
    limits = []
    for level in range(1, count):
        if level < exact:
            limits.append(level)
        else:
            distance = exact
            while (
                min(
                    count - 1,
                    exact + int(np.floor(np.log(distance / exact) / np.log(128.0 / exact) * exact)),
                )
                < level
            ):
                distance += 1
            limits.append(distance)
    return limits


def dot(left, right, dims, precision=None):
    return lax.dot_general(
        left, right, (((dims[0],), (dims[1],)), ((), ())), precision=precision, preferred_element_type=F32
    )


def nn(left, right, precision=None):
    return dot(left, right, (1, 0), precision)


def nt(left, right, precision=None):
    return dot(left, right, (1, 1), precision)


def tn(left, right, precision=None):
    return dot(left, right, (0, 0), precision)


def low(value):
    return value.astype(BF16)


def full(value):
    return value.astype(F32)


def inverse_rms(rows):
    return lax.rsqrt(jnp.mean(rows * rows, axis=-1, keepdims=True) + EPSILON)


def normed(rows, gain):
    return low(rows * inverse_rms(rows) * gain)


def normed_back(rows, gain, grad):
    rho = inverse_rms(rows)
    scaled = grad * gain
    back = scaled * rho - rows * (rho * rho * rho) * jnp.mean(scaled * rows, axis=-1, keepdims=True)
    return back, jnp.sum(grad * rows * rho, axis=0, keepdims=True)


def gelu_parts(a):
    t = jnp.tanh(0.7978845608028654 * (a + 0.044715 * a * a * a))
    half = 0.5 * (1.0 + t)
    slope = half + 0.5 * a * (1.0 - t * t) * (0.7978845608028654 * (1.0 + 0.134145 * a * a))
    return a * half, slope


def kernel(
    c,
    x_hbm,
    gy_hbm,
    docs_ref,
    routes_ref,
    attn_gain_ref,
    ffn_gain_ref,
    table_ref,
    wq_hbm,
    wk_hbm,
    wv_hbm,
    wo_hbm,
    router_hbm,
    dense_gate_hbm,
    dense_up_hbm,
    dense_down_hbm,
    gate_hbm,
    up_hbm,
    down_hbm,
    out_hbm,
    input_hbm,
    attn_hbm,
    dense_hbm,
    ge_gate_hbm,
    ge_up_hbm,
    ge_down_hbm,
    small_ref,
    bias_grad_ref,
    send_sem,
    recv_sem,
    gains,
    bucket,
    bias,
    mask,
    n1,
    qkv,
    probs,
    o,
    do,
    dqkv,
    dsum,
    bias_rows,
    sends,
    recv4,
    recv8,
    rows1,
    rows2,
    rows3,
    grad2,
    grad1,
    grad0,
    chunk,
    hid1,
    gate1,
    up1,
    da1,
    du1,
    pick0,
    pick1,
    ex,
    ey,
    sx,
    rx,
    hid,
    da,
    du,
    dout,
    gates,
    cs,
    cr,
    rt,
    rb,
    cs2,
    cr2,
    rt2,
    rb2,
    moe_send,
    moe_recv,
    out_send,
    out_recv,
    small,
    small_send,
    small_recv,
    small2_send,
    small2_recv,
    small3_send,
    small3_recv,
    smallb_send,
    smallb_recv,
    smallb3_send,
    smallb3_recv,
    smallb2_send,
    smallb2_recv,
    dense_own,
    dense_a1,
    dense_b1,
    dense_am,
    dense_bm,
    dense_a2,
    dense_b2,
    attn_own,
    attn_a1,
    attn_b1,
    attn_am,
    attn_bm,
    attn_a2,
    attn_b2,
    dense_gate_ref,
    dense_up_ref,
    dense_down_ref,
    gate_ref,
    up_ref,
    down_ref,
    ge_gate_ref,
    ge_up_ref,
    ge_down_ref,
    stage_sem,
    wide_router,
    x_ref,
    gy_ref,
    wq_ref,
    wk_ref,
    wv_ref,
    wo_ref,
    router_ref,
    out_ref,
    input_ref,
    attn_ref,
    dense_ref,
    d0,
):
    sections, experts, mps = c["section"], c["expert"], c["mp"]
    micro, length, heads, size, cap = c["micro"], c["length"], c["heads"], c["size"], c["cap"]
    width, ff = c["width"], c["ff"]
    group = sections * mps
    rows = micro * length
    part = rows // group
    half = width // sections
    local = heads * size
    scale = size**-0.5
    slots = micro * cap
    s, me, mp = lax.axis_index("section"), lax.axis_index("expert"), lax.axis_index("mp")
    place = s * mps + mp
    own = pl.ds(pl.multiple_of(place * part, part), part)
    mine = pl.ds(pl.multiple_of(s * half, 128), half)
    H2, Y1, H1, GRAD = 0, 1, 2, 3
    staged = [
        pltpu.make_async_copy(src, dst, stage_sem.at[i])
        for i, (src, dst) in enumerate(
            (
                (dense_gate_hbm, dense_gate_ref),
                (dense_up_hbm, dense_up_ref),
                (dense_down_hbm, dense_down_ref),
                (gate_hbm, gate_ref),
                (up_hbm, up_ref),
                (down_hbm, down_ref),
                (ge_gate_ref, ge_gate_hbm),
                (ge_up_ref, ge_up_hbm),
                (ge_down_ref, ge_down_hbm),
                (x_hbm, x_ref),
                (wq_hbm, wq_ref),
                (wk_hbm, wk_ref),
                (wv_hbm, wv_ref),
                (wo_hbm, wo_ref),
                (router_hbm, router_ref),
                (gy_hbm, gy_ref),
                (out_ref, out_hbm),
                (input_ref, input_hbm),
                (dense_ref, dense_hbm),
                (attn_ref, attn_hbm),
            )
        )
    ]
    for copy in staged[9:16] + staged[0:6]:
        copy.start()
    blocks = 4
    per = experts // blocks
    block = per * slots
    side_size = c["side"]
    slow, fast = me // side_size, lax.rem(me, side_size)

    def at_offset(dz, dy):
        z, y = lax.rem(slow + dz, side_size), lax.rem(fast + dy, side_size)
        return z * side_size + y

    scopes = contextlib.ExitStack()

    def phase(name):
        scopes.close()
        scopes.enter_context(jax.named_scope(name))

    def on_expert(k):
        return {"expert": lax.rem(me + k, experts)}

    def in_group(p):
        return {"section": p // mps, "mp": lax.rem(p, mps)}

    def send(src, dst, which, device, arrival=None):
        pltpu.make_async_remote_copy(
            src_ref=src,
            dst_ref=dst,
            send_sem=send_sem.at[which],
            recv_sem=recv_sem.at[which if arrival is None else arrival],
            device_id=device,
            device_id_type=MESH,
        ).start()

    def drain(sem, view):
        pltpu.make_async_copy(view, view, sem).wait()

    def arrived(phase, view):
        drain(recv_sem.at[phase], view)

    def left(phase, view):
        drain(send_sem.at[phase], view)

    phase("signals")
    barrier = pltpu.get_barrier_semaphore()
    for k in range(1, group):
        pl.semaphore_signal(barrier, inc=1, device_id=in_group(lax.rem(place + k, group)), device_id_type=MESH)
    for k in range(1, experts):
        pl.semaphore_signal(barrier, inc=1, device_id=on_expert(k), device_id_type=MESH)

    phase("tables")
    gains[s] = jnp.zeros((8, width), F32)
    gains[s, 0:1] = attn_gain_ref[...]
    gains[s, 1:2] = ffn_gain_ref[...]
    row_at = lax.broadcasted_iota(jnp.int32, (length, length), 0)
    col_at = lax.broadcasted_iota(jnp.int32, (length, length), 1)
    found = jnp.zeros((length, length), jnp.int32)
    for limit in bucket_limits(c["buckets"]):
        found = found + jnp.where(row_at - col_at >= limit, 1, 0)
    bucket[...] = found
    wide_router[...] = jnp.zeros_like(wide_router)
    for h in range(heads):
        total = jnp.zeros((length, length), F32)
        for b in range(c["buckets"]):
            total = jnp.where(found == b, table_ref[h][:, b : b + 1], total)
        bias[h] = total
    for m in range(micro):
        docs = jnp.broadcast_to(full(docs_ref[m : m + 1, :]), (length, length))
        same = (docs == jnp.transpose(docs)) & (col_at <= row_at)
        mask[m] = jnp.where(same, 1.0, 0.0)
    phase("barrier")
    pl.semaphore_wait(barrier, group - 1 + experts - 1)
    send(gains.at[s], gains.at[s], GAINS, {"section": 1 - s})

    def gather_all(buf, phase):
        for k in range(1, group):
            send(buf.at[own], buf.at[own], phase, in_group(lax.rem(place + k, group)))

    def wait_all(buf, phase):
        arrived(phase, buf.at[pl.ds(0, (group - 1) * part)])

    def gather_to(target, buf, phase):
        for k in range(1, mps):
            send(buf.at[own], buf.at[own], phase, {"section": target, "mp": lax.rem(mp + k, mps)})

        @pl.when(s != target)
        def _():
            send(buf.at[own], buf.at[own], phase, {"section": 1 - s})

    def left_to(target, buf, phase):
        @pl.when(s != target)
        def _():
            left(phase, buf.at[pl.ds(0, mps * part)])

        @pl.when(s == target)
        def _():
            left(phase, buf.at[pl.ds(0, (mps - 1) * part)])

    def scatter(src, dst, phase):
        for k in range(1, group):
            p = lax.rem(place + k, group)
            send(src.at[pl.ds(pl.multiple_of(p * part, part), part)], dst.at[place], phase, in_group(p))
        dst[place] = src[own]

    def scatter_from(src, dst, phase):
        for k in range(1, group):
            p = lax.rem(place + k, group)
            send(src.at[pl.ds(pl.multiple_of(p * part, part), part)], dst.at[mp], phase, in_group(p))
        dst[mp] = src[own]

    def wait_from(source, dst, phase):
        @pl.when(s == source)
        def _():
            arrived(phase, dst.at[pl.ds(0, mps - 1)])

        @pl.when(s != source)
        def _():
            arrived(phase, dst)

    def total(ref, first=0, last=None):
        last = ref.shape[0] if last is None else last
        value = full(ref[first])
        for i in range(first + 1, last):
            value = value + full(ref[i])
        return value

    pairs = [
        (m, h, slice(m * length, (m + 1) * length), slice(h * size, (h + 1) * size))
        for m in range(micro)
        for h in range(heads)
    ]

    def attention(n_ref, out):
        for t, w in enumerate((wq_ref, wk_ref, wv_ref)):
            qkv[t] = low(nt(n_ref[...], w[...]))
        tops, scores = [], []
        for m, h, r, lanes in pairs:
            raw = nt(qkv[0, r, lanes], qkv[1, r, lanes]) * scale + bias[h]
            scores.append(jnp.where(mask[m] > 0, raw, NEGATIVE))
        tops = [jnp.max(raw, axis=-1, keepdims=True) for raw in scores]
        powers = [jnp.exp(raw - top) for raw, top in zip(scores, tops)]
        sums = [jnp.sum(e, axis=-1, keepdims=True) for e in powers]
        lows = []
        for i, (m, h, r, lanes) in enumerate(pairs):
            p = powers[i] / sums[i]
            probs[m * heads + h] = p
            lows.append(low(p))
        for i, (m, h, r, lanes) in enumerate(pairs):
            o[r, lanes] = low(nn(lows[i], qkv[2, r, lanes]))
        out[...] = low(nn(o[...], wo_ref[...]))

    def attention_back(g_ref, out, between=None):
        do[...] = low(nt(g_ref[...], wo_ref[...]))
        dps = [nt(do[r, lanes], qkv[2, r, lanes]) for m, h, r, lanes in pairs]
        for m, h, r, lanes in pairs:
            dv = tn(low(probs[m * heads + h]), do[r, lanes])
            dqkv[r, 2 * local + h * size : 2 * local + (h + 1) * size] = low(dv)
        sums = [
            jnp.sum(dp * probs[m * heads + h], axis=-1, keepdims=True)
            for dp, (m, h, r, lanes) in zip(dps, pairs)
        ]
        grads = [
            low(probs[m * heads + h] * (dp - total_row))
            for dp, total_row, (m, h, r, lanes) in zip(dps, sums, pairs)
        ]
        if between is not None:
            between()
        for ds, (m, h, r, lanes) in zip(grads, pairs):
            dqkv[r, h * size : (h + 1) * size] = low(nn(ds, qkv[1, r, lanes]) * scale)
        for ds, (m, h, r, lanes) in zip(grads, pairs):
            dqkv[r, local + h * size : local + (h + 1) * size] = low(tn(ds, qkv[0, r, lanes]) * scale)
        for h in range(heads):
            dsum[h] = sum(full(grads[m * heads + h]) for m in range(micro))
        dn = nn(dqkv[:, 0:local], wq_ref[...]) + nn(dqkv[:, local : 2 * local], wk_ref[...])
        dn = dn + nn(dqkv[:, 2 * local : 3 * local], wv_ref[...])
        out[...] = low(dn)
        return dn

    def attention_weights(n_ref, g_ref):
        grads = low(tn(dqkv[...], n_ref[...]))
        last = low(tn(o[...], g_ref[...]))
        for t in range(width // 128):
            lanes = slice(t * 128, (t + 1) * 128)
            attn_own[t, 0 : 3 * local] = grads[:, lanes]
            attn_own[t, 3 * local :] = last[:, lanes]
        attn_sum[0]()

    def bias_sums():
        found = bucket[...]
        for h in range(heads):
            held = dsum[h]
            for b in range(c["buckets"]):
                bias_rows[b : b + 1, :] = jnp.sum(jnp.where(found == b, held, 0.0), axis=0, keepdims=True)
            sums = nt(jnp.ones((8, length), F32), bias_rows[...], HIGHEST)
            smallb_send[1 + h : 2 + h, 0 : c["buckets"]] = sums[0:1]

    def reducer(own, out, base, split, first_recv, middles, second_recv):
        n = side_size
        quarter, step = width // n, width // (n * n)
        tiles = own.shape[0]

        def half_of(i):
            f, g = (fast, slow) if i == 0 else (slow, fast)
            to_f = (lambda p: slow * n + p) if i == 0 else (lambda p: p * n + fast)
            to_g = (lambda p: p * n + fast) if i == 0 else (lambda p: slow * n + p)
            lanes = pl.ds(0, split) if i == 0 else pl.ds(split, tiles - split)
            return f, g, to_f, to_g, lanes, base + i

        def many(p, size):
            return pl.ds(pl.multiple_of(p * size, 16), size)

        def one():
            for i in range(2):
                f, g, to_f, to_g, lanes, which = half_of(i)
                for k in range(1, n):
                    p = lax.rem(f + k, n)
                    src = own.at[lanes, many(p, quarter)]
                    send(src, first_recv[i].at[f], which, {"expert": to_f(p)})
                first_recv[i][f] = own[lanes, many(f, quarter)]

        def two():
            for i in range(2):
                f, g, to_f, to_g, lanes, which = half_of(i)
                arrived(which, first_recv[i].at[pl.ds(0, n - 1)])
                middles[i][...] = low(total(first_recv[i]))
                for k in range(1, n):
                    p = lax.rem(g + k, n)
                    src = middles[i].at[:, many(p, step)]
                    send(src, second_recv[i].at[g], which + 2, {"expert": to_g(p)})
                second_recv[i][g] = middles[i][:, many(g, step)]

        def three():
            for i in range(2):
                f, g, to_f, to_g, lanes, which = half_of(i)
                arrived(which + 2, second_recv[i].at[pl.ds(0, n - 1)])
                at = out.at[lanes, many(f * n + g, step)]
                at[...] = low(total(second_recv[i]))
                for k in range(1, n):
                    send(at, at, which + 4, {"expert": to_g(lax.rem(g + k, n))})

        def four():
            for i in range(2):
                f, g, to_f, to_g, lanes, which = half_of(i)
                arrived(which + 4, second_recv[i].at[pl.ds(0, n - 1)])
                at = out.at[lanes, many(f, quarter)]
                for k in range(1, n):
                    send(at, at, which + 6, {"expert": to_f(lax.rem(f + k, n))})

        def five():
            for i in range(2):
                arrived(base + i + 6, first_recv[i].at[pl.ds(0, n - 1)])

        def done():
            for i in range(2):
                for stage in range(4):
                    ref = (first_recv, second_recv, second_recv, first_recv)[stage][i]
                    left(base + i + 2 * stage, ref.at[pl.ds(0, n - 1)])

        return one, two, three, four, five, done

    phase("attention1")
    dense_sum = reducer(
        dense_own, dense_ref, DENSE_SUM, 5, (dense_a1, dense_b1), (dense_am, dense_bm), (dense_a2, dense_b2)
    )
    attn_sum = reducer(
        attn_own, attn_ref, ATTN_SUM, 3, (attn_a1, attn_b1), (attn_am, attn_bm), (attn_a2, attn_b2)
    )

    for copy in staged[9:16]:
        copy.wait()
    wide_router[0:experts] = router_ref[...]
    x = full(x_ref[...])
    @pl.when(s == 0)
    def _():
        n1[...] = normed(x, gains[0, 0:1])
        attention(n1, sends.at[0])
        scatter_from(sends.at[0], recv4.at[0], TERM1)

    phase("early")
    named = []
    before = low(jnp.where(row_at < col_at, 1.0, 0.0))
    expert_at = lax.broadcasted_iota(jnp.int32, (length, length), 0)
    slot_at = full(lax.broadcasted_iota(jnp.int32, (cap, length), 0))
    for m in range(micro):
        r = slice(m * length, (m + 1) * length)
        wide = [
            jnp.where(expert_at == routes_ref[2 * m + ch : 2 * m + ch + 1, :], 1.0, 0.0)
            for ch in range(2)
        ]
        hots = [hot[0:experts] for hot in wide]
        rank = nn(low(hots[0] + hots[1]), before)
        for e in range(experts):
            fit = slot_at == rank[e : e + 1]
            at = slice(e * cap, (e + 1) * cap)
            pick0[m, at] = low(jnp.where(fit, hots[0][e : e + 1], 0.0))
            pick1[m, at] = low(jnp.where(fit, hots[1][e : e + 1], 0.0))
        named.append(hots)
        place_rows = slice(m * cap, (m + 1) * cap)
        out_rows = low(nn(pick0[m] + pick1[m], gy_ref[r, mine]))
        ex[:, place_rows, 0:half] = out_rows.reshape(experts, cap, half)
        other = low(nt(pick0[m], low(wide[1])) + nt(pick1[m], low(wide[0])))
        ex[:, place_rows, half:] = other.reshape(experts, cap, 128)
    if side_size == 4:
        offsets = [(0, 1), (0, 3), (1, 0), (3, 0), (1, 1), (3, 3), (1, 3), (3, 1)]
        offsets += [(2, 1), (2, 3), (1, 2), (3, 2), (0, 0), (0, 2), (2, 0), (2, 2)]
    else:
        offsets = [(a, b) for a in range(side_size) for b in range(side_size)]

    def to_slot(src, dst, k, which):
        if offsets[k] == (0, 0):
            pltpu.make_async_copy(src.at[me], dst.at[s, pl.ds(k * slots, slots)], recv_sem.at[which]).start()
        else:
            p = at_offset(*offsets[k])
            send(src.at[p], dst.at[s, pl.ds(k * slots, slots)], which, {"expert": p})

    def to_token(src, dst, k, which):
        src = src.at[pl.ds(k * slots, slots)]
        if offsets[k] == (0, 0):
            pltpu.make_async_copy(src, dst.at[me], recv_sem.at[which]).start()
        else:
            dz, dy = offsets[k]
            send(src, dst.at[me], which, {"expert": at_offset(side_size - dz, side_size - dy)})

    for k in range(experts):
        to_slot(ex, ey, k, EARLY)
    phase("term1_wait")
    arrived(GAINS, gains.at[1 - s])
    wait_from(0, recv4.at[0], TERM1)
    phase("norm1")
    h1 = full(x_ref[own]) + total(recv4.at[0])
    chunk[H1] = h1
    rows1[own] = normed(h1, gains[0, 1:2])
    gather_all(rows1, ROWS1)
    phase("rows1_wait")
    wait_all(rows1, ROWS1)
    phase("dense")
    for copy in staged[0:3]:
        copy.wait()
    gate1[...] = nn(rows1[...], dense_gate_ref[...])
    up1[...] = nn(rows1[...], dense_up_ref[...])
    hid1[...] = low(gelu_parts(gate1[...])[0] * up1[...])
    sends[1] = low(nn(hid1[...], dense_down_ref[...]))
    scatter(sends.at[1], recv8.at[0], DENSE)
    phase("dense_wait")
    arrived(DENSE, recv8.at[0, pl.ds(0, group - 1)])
    phase("norm2")
    y1 = chunk[H1] + total(recv8.at[0])
    chunk[Y1] = y1
    rows2[own] = normed(y1, gains[1, 0:1])
    gather_to(1, rows2, ROWS2)

    phase("early_forward")
    arrived(EARLY, ey.at[s])
    send(ey.at[s], ey.at[s], EARLY_FORWARD, {"section": 1 - s})
    phase("attention2")
    @pl.when(s == 1)
    def _():
        wait_all(rows2, ROWS2)
        attention(rows2, sends.at[2])
        scatter_from(sends.at[2], recv4.at[1], TERM2)

    phase("early_hidden")
    staged[5].wait()
    arrived(EARLY_FORWARD, ey.at[1 - s])
    for j in range(blocks):
        at = pl.ds(j * block, block)
        d0[at] = nt(ey[0, at, 0:half], down_ref[:, 0:half]) + nt(ey[1, at, 0:half], down_ref[:, half:])

    phase("term2_wait")
    wait_from(1, recv4.at[1], TERM2)
    phase("norm3")
    h2 = chunk[Y1] + total(recv4.at[1])
    chunk[H2] = h2
    rows3[own] = normed(h2, gains[1, 1:2])
    for k in range(1, group):
        p = in_group(lax.rem(place + k, group))
        src = rows3.at[own, pl.ds(pl.multiple_of(p["section"] * half, 128), half)]
        send(src, src, ROWS3, p)
    phase("rows3_wait")
    arrived(ROWS3, rows3.at[pl.ds(0, (group - 1) * part), pl.ds(0, half)])
    phase("slots")
    for m in range(micro):
        r = slice(m * length, (m + 1) * length)
        out_rows = low(nn(pick0[m] + pick1[m], rows3[r, mine]))
        sx[:, m * cap : (m + 1) * cap, :] = out_rows.reshape(experts, cap, half)

    def dispatch(j):
        for k in range(j * per, (j + 1) * per):
            to_slot(sx, rx, k, DISPATCH + j)

    def dispatched(j):
        count = sum(offsets[k] != (0, 0) for k in range(j * per, (j + 1) * per))
        if count:
            left(DISPATCH + j, rx.at[0, pl.ds(0, count * slots)])

    def forward(j):
        at = pl.ds(j * block, block)
        arrived(DISPATCH + j, rx.at[s, at])
        send(rx.at[s, at], rx.at[s, at], FORWARD + j, {"section": 1 - s})

    def give_back(j):
        at = pl.ds(j * block, block)
        arrived(CORE + j, cr.at[at])
        rt[at, 0:half] = low(full(cs[s, at]) + full(cr[at]))
        for k in range(j * per, (j + 1) * per):
            to_token(rt, rb, k, RETURN)

    phase("dispatch_wait")
    dispatch(0)
    dispatch(1)
    forward(0)
    dispatched(0)
    dispatch(2)
    for copy in staged[3:5]:
        copy.wait()
    named_here = lax.broadcasted_iota(jnp.int32, (block, 128), 1)
    for j in range(blocks):
        at = pl.ds(j * block, block)
        phase("forward_wait%d" % j)
        arrived(FORWARD + j, rx.at[1 - s, at])
        phase("expert%d" % j)
        x0, x1 = rx[0, at, 0:half], rx[1, at, 0:half]
        logits = nt(x0, wide_router[:, 0:half]) + nt(x1, wide_router[:, half:])
        this = jnp.sum(jnp.where(named_here == me, logits, 0.0), axis=-1, keepdims=True)
        other = jnp.sum(full(ey[0, at, half:]) * logits, axis=-1, keepdims=True)
        top = jnp.maximum(this, other)
        e0, e1 = jnp.exp(this - top), jnp.exp(other - top)
        gate = e0 / (e0 + e1)
        gates[at] = jnp.broadcast_to(gate, (block, 128))
        a = nn(x0, gate_ref[0:half]) + nn(x1, gate_ref[half:])
        u = nn(x0, up_ref[0:half]) + nn(x1, up_ref[half:])
        d = gate * d0[at]
        value, slope = gelu_parts(a)
        held = low(value * u)
        hid[at] = held
        term = jnp.sum(d * full(held), axis=-1, keepdims=True)
        rt[at, half:] = low(jnp.where(named_here == 0, term, 0.0))
        da[at] = low(d * u * slope)
        du[at] = low(d * value)
        for side in range(sections):
            w = slice(side * half, (side + 1) * half)
            cs[side, at] = low(nt(da[at], gate_ref[w]) + nt(du[at], up_ref[w]))
        send(cs.at[1 - s, at], cr.at[at], CORE + j, {"section": 1 - s})
        phase("give_back%d" % j)
        if j + 1 < blocks:
            forward(j + 1)
            dispatched(j + 1)
            if j + 3 < blocks:
                dispatch(j + 3)
        if j > 0:
            give_back(j - 1)
    give_back(blocks - 1)
    phase("outputs")
    for j in range(blocks):
        at = pl.ds(j * block, block)
        for side in range(sections):
            w = slice(side * half, (side + 1) * half)
            cs2[side, at] = low(nn(hid[at], down_ref[:, w]) * gates[at][:, 0:1])
        send(cs2.at[1 - s, at], cr2.at[at], CORE2, {"section": 1 - s})
    phase("expert_weights")
    for j in range(blocks):
        at = pl.ds(j * block, block)
        for side in range(sections):
            w = slice(side * half, (side + 1) * half)
            dout[at, w] = low(gates[at][:, 0:1] * full(ey[side, at, 0:half]))
    for side in range(sections):
        w = slice(side * half, (side + 1) * half)
        ge_gate_ref[w] = low(tn(rx[side], da[...]))
        ge_up_ref[w] = low(tn(rx[side], du[...]))
        ge_down_ref[:, w] = low(tn(hid[...], dout[:, w]))
    for copy in staged[6:9]:
        copy.start()
    arrived(CORE2, cr2)
    for j in range(blocks):
        at = pl.ds(j * block, block)
        rt2[at] = low(full(cs2[s, at]) + full(cr2[at]))
        for k in range(j * per, (j + 1) * per):
            to_token(rt2, rb2, k, RETURN2)
    phase("return_wait")
    arrived(RETURN, rb)
    phase("combine")
    lane = lax.broadcasted_iota(jnp.int32, (length, 128), 1)
    for m in range(micro):
        r = slice(m * length, (m + 1) * length)
        held = rb[:, m * cap : (m + 1) * cap, :].reshape(experts * cap, half + 128)
        moe_send[r, 0:half] = low(tn(pick0[m] + pick1[m], held[:, 0:half]))
        t0, t1 = tn(pick0[m], held[:, half:]), tn(pick1[m], held[:, half:])
        moe_send[r, half:] = low(jnp.where(lane == 0, t0, jnp.where(lane == 1, t1[:, 0:1], 0.0)))
    scatter(moe_send, moe_recv, MOE)
    phase("moe_wait")
    arrived(MOE, moe_recv.at[pl.ds(0, group - 1)])
    phase("norm3_back")
    lower, upper = total(moe_recv, 0, mps), total(moe_recv, mps, group)
    h2 = chunk[H2]
    terms = lower[:, half:] + upper[:, half:]
    t0, t1 = terms[:, 0:1], terms[:, 1:2]
    ahead = lax.rem(place * part, length)
    token = lax.broadcasted_iota(jnp.int32, (part, length), 1)
    is_own = low(jnp.where(token == lax.broadcasted_iota(jnp.int32, (part, length), 0) + ahead, 1.0, 0.0))
    hot0, hot1 = (
        nt(is_own, low(jnp.where(place * part < length, named[0][ch], named[1][ch]))) for ch in range(2)
    )
    logits = nt(rows3[own], router_ref[...])
    l0 = jnp.sum(hot0 * logits, axis=-1, keepdims=True)
    l1 = jnp.sum(hot1 * logits, axis=-1, keepdims=True)
    top = jnp.maximum(l0, l1)
    e0, e1 = jnp.exp(l0 - top), jnp.exp(l1 - top)
    dlogits = hot0 * (t0 - e0 / (e0 + e1) * (t0 + t1)) + hot1 * (t1 - e1 / (e0 + e1) * (t0 + t1))
    dr = jnp.concatenate([lower[:, 0:half], upper[:, 0:half]], axis=1)
    dr = dr + nn(dlogits, full(router_ref[...]), HIGHEST)
    back, gain = normed_back(h2, gains[1, 1:2], dr)
    grad = full(gy_ref[own]) + back
    chunk[GRAD] = grad
    grad2[own] = low(grad)
    gather_to(1, grad2, GRAD2)
    small[...] = jnp.zeros_like(small)
    small[0:1] = gain
    small[8 : 8 + experts] = tn(dlogits, full(rows3[own]), HIGHEST)
    smallb_send[...] = jnp.zeros_like(smallb_send)

    phase("attention2_back")
    @pl.when(s == 1)
    def _():
        wait_all(grad2, GRAD2)
        attention_back(grad2, sends.at[3])
        scatter_from(sends.at[3], recv4.at[2], BACK2)
        attention_weights(rows2, grad2)

    def output():
        arrived(RETURN2, rb2)
        for m in range(micro):
            held = rb2[:, m * cap : (m + 1) * cap, :].reshape(experts * cap, half)
            out_send[m * length : (m + 1) * length] = low(tn(pick0[m] + pick1[m], held))
        scatter(out_send, out_recv, MOE2)

    phase("output")
    @pl.when(s == 0)
    def _():
        output()

    phase("back2_wait")
    wait_from(1, recv4.at[2], BACK2)
    phase("norm2_back")
    back, gain = normed_back(chunk[Y1], gains[1, 0:1], total(recv4.at[2]))
    small[1:2] = gain
    grad = chunk[GRAD] + back
    chunk[GRAD] = grad
    grad1[own] = low(grad)
    gather_all(grad1, GRAD1)
    phase("output1")
    @pl.when(s == 1)
    def _():
        output()

    phase("grad1_wait")
    wait_all(grad1, GRAD1)
    phase("dense_back")
    d = nt(grad1[...], dense_down_ref[...])
    value, slope = gelu_parts(gate1[...])
    da1[...] = low(d * up1[...] * slope)
    du1[...] = low(d * value)
    sends[4] = low(nt(da1[...], dense_gate_ref[...]) + nt(du1[...], dense_up_ref[...]))
    scatter(sends.at[4], recv8.at[1], BACK1)
    phase("dense_weights")
    gate_grad = low(tn(rows1[...], da1[...]))
    up_grad = low(tn(rows1[...], du1[...]))
    for t in range(ff // 128):
        lanes = slice(t * 128, (t + 1) * 128)
        dense_own[t] = gate_grad[:, lanes]
        dense_own[ff // 128 + t] = up_grad[:, lanes]
    down_grad = low(tn(hid1[...], grad1[...]))
    for t in range(width // 128):
        at = slice(t % 2 * ff, t % 2 * ff + ff)
        dense_own[2 * (ff // 128) + t // 2, at] = down_grad[:, t * 128 : (t + 1) * 128]
    dense_sum[0]()
    phase("back1_wait")
    arrived(BACK1, recv8.at[1, pl.ds(0, group - 1)])
    phase("norm1_back")
    back, gain = normed_back(chunk[H1], gains[0, 1:2], total(recv8.at[1]))
    small[2:3] = gain
    grad = chunk[GRAD] + back
    chunk[GRAD] = grad
    grad0[own] = low(grad)
    gather_to(0, grad0, GRAD0)
    small_send[...] = low(small[...])
    for k in range(1, group):
        send(small_send, small_recv.at[place], SMALL_A, in_group(lax.rem(place + k, group)))
    small_recv[place] = small_send[...]

    phase("attention1_back")
    @pl.when(s == 0)
    def _():
        wait_all(grad0, GRAD0)
        dn = attention_back(grad0, sends.at[5], dense_sum[1])
        scatter_from(sends.at[5], recv4.at[3], BACK0)
        dense_sum[2]()
        attention_weights(n1, grad0)
        x = full(x_ref[...])
        smallb_send[0:1] = jnp.sum(dn * x * inverse_rms(x), axis=0, keepdims=True)

    @pl.when(s == 1)
    def _():
        for stage in attn_sum[1:3]:
            stage()
        dense_sum[1]()
        attn_sum[3]()
        dense_sum[2]()

    def along(src, dst, which, fast_side):
        for k in range(1, side_size):
            p = at_offset(0, k) if fast_side else at_offset(k, 0)
            send(src, dst.at[fast if fast_side else slow], which, {"expert": p})
        dst[fast if fast_side else slow] = src[...]

    phase("small_a")
    arrived(SMALL_A, small_recv.at[pl.ds(0, group - 1)])
    small2_send[...] = low(total(small_recv))
    along(small2_send, small2_recv, SMALL_A2, True)
    phase("dense_four")
    dense_sum[3]()
    phase("bias")
    bias_sums()

    along(smallb_send, smallb_recv, SMALL_B, True)
    phase("back0_wait")
    wait_from(0, recv4.at[3], BACK0)
    phase("norm0_back")
    back, gain = normed_back(full(x_ref[own]), gains[0, 0:1], total(recv4.at[3]))
    input_ref[own] = low(chunk[GRAD] + back)
    gather_all(input_ref, INPUT)
    phase("out")
    arrived(MOE2, out_recv.at[pl.ds(0, group - 1)])
    out_ref[own, 0:half] = low(chunk[H2][:, 0:half] + total(out_recv, 0, mps))
    out_ref[own, half:] = low(chunk[H2][:, half:] + total(out_recv, mps, group))
    gather_all(out_ref, OUT)
    phase("attn_two")
    @pl.when(s == 0)
    def _():
        attn_sum[1]()

    phase("small_two")
    arrived(SMALL_A2, small2_recv.at[pl.ds(0, side_size - 1)])
    small3_send[...] = low(total(small2_recv))
    along(small3_send, small3_recv, SMALL_A3, False)
    arrived(SMALL_B, smallb_recv.at[pl.ds(0, side_size - 1)])
    smallb3_send[...] = total(smallb_recv)
    along(smallb3_send, smallb3_recv, SMALL_B3, False)
    phase("attn_three")
    @pl.when(s == 0)
    def _():
        attn_sum[2]()

    phase("small_three")
    arrived(SMALL_B3, smallb3_recv.at[pl.ds(0, side_size - 1)])
    smallb2_send[...] = total(smallb3_recv)
    for k in range(1, mps):
        send(smallb2_send, smallb2_recv.at[mp], SMALL_B2, {"mp": lax.rem(mp + k, mps)})
    smallb2_recv[mp] = smallb2_send[...]
    phase("attn_four")
    @pl.when(s == 0)
    def _():
        attn_sum[3]()

    arrived(SMALL_A3, small3_recv.at[pl.ds(0, side_size - 1)])
    summed = total(small3_recv)
    for h in range(heads):
        bias_grad_ref[h] = smallb2_send[1 + h : 2 + h, 0 : c["buckets"]]
    arrived(SMALL_B2, smallb2_recv.at[pl.ds(0, mps - 1)])
    gain0 = total(smallb2_recv)[0:1]
    small_ref[...] = summed
    small_ref[0:1] = jnp.where(s == 0, gain0, summed[1:2])
    small_ref[1:2] = jnp.where(s == 0, summed[2:3], summed[0:1])
    phase("last_waits")
    wait_all(out_ref, OUT)
    staged[16].start()
    wait_all(input_ref, INPUT)
    staged[17].start()
    dense_sum[4]()
    staged[18].start()
    attn_sum[4]()
    staged[19].start()
    attn_sum[5]()
    dense_sum[5]()
    left(GAINS, gains.at[s])
    seven = pl.ds(0, (group - 1) * part)
    left(ROWS3, rows3.at[seven, pl.ds(0, half)])
    for phase, ref in ((ROWS1, rows1), (OUT, out_ref), (GRAD1, grad1), (INPUT, input_ref)):
        left(phase, ref.at[seven])
    for phase, at in ((DENSE, 1), (BACK1, 4)):
        left(phase, sends.at[at, seven])
    left(MOE, moe_send.at[seven])
    left(MOE2, out_send.at[seven])
    left(EARLY, ey.at[0, pl.ds(0, (experts - 1) * slots)])
    left(EARLY_FORWARD, ey.at[0])
    left(CORE2, cr2)
    left(RETURN2, rb2.at[pl.ds(0, experts - 1)])
    left_to(1, rows2, ROWS2)
    left_to(1, grad2, GRAD2)
    left_to(0, grad0, GRAD0)

    @pl.when(s == 0)
    def _():
        left(TERM1, sends.at[0, seven])
        left(BACK0, sends.at[5, seven])

    @pl.when(s == 1)
    def _():
        left(TERM2, sends.at[2, seven])
        left(BACK2, sends.at[3, seven])

    for j in range(blocks):
        left(FORWARD + j, rx.at[0, pl.ds(0, block)])
        left(CORE + j, cr.at[pl.ds(0, block)])
    left(RETURN, rb.at[pl.ds(0, experts - 1)])
    left(SMALL_A, small_recv.at[pl.ds(0, group - 1)])
    three = pl.ds(0, side_size - 1)
    left(SMALL_A2, small2_recv.at[three])
    left(SMALL_A3, small3_recv.at[three])
    left(SMALL_B, smallb_recv.at[three])
    left(SMALL_B3, smallb3_recv.at[three])
    left(SMALL_B2, smallb2_recv.at[pl.ds(0, mps - 1)])
    for copy in staged[6:9] + staged[16:]:
        copy.wait()
    scopes.close()


def widen(tiles, experts, out, back, attn, gate, up, down, e_gate, e_up, e_down, small, bias, *to):
    to[0][...] = full(out[...])
    to[1][...] = full(back[...])
    for t in range(2 * tiles):
        lanes = slice(t * 128, (t + 1) * 128)
        for which in range(4):
            to[2 + which][:, lanes] = full(attn[t, which])
        to[8][:, lanes] = full(down[t // 2, t % 2])
    for t in range(tiles):
        lanes = slice(t * 128, (t + 1) * 128)
        to[6][:, lanes] = full(gate[t])
        to[7][:, lanes] = full(up[t])
    to[9][...] = full(e_gate[...])
    to[10][...] = full(e_up[...])
    to[11][...] = full(e_down[...])
    to[12][...] = small[0:1]
    to[13][...] = small[1:2]
    to[14][...] = small[8 : 8 + experts]
    to[15][...] = bias[...]


def shards(
    block_input,
    segments,
    routes,
    cotangent,
    attn_gain,
    query_weight,
    key_weight,
    value_weight,
    out_weight,
    pos_bias,
    ffn_gain,
    dense_gate,
    dense_up,
    dense_down,
    router,
    expert_gate,
    expert_up,
    expert_down,
):
    micro, _, length, width = block_input.shape
    experts = router.shape[1]
    cap = 4 * length // experts
    buckets, heads = pos_bias.shape[1:]
    local = query_weight.shape[2]
    size = local // heads
    ff = dense_gate.shape[1]
    sections, mps = lax.axis_size("section"), lax.axis_size("mp")
    group = sections * mps
    rows = micro * length
    part = rows // group
    half = width // sections
    slots = micro * cap
    every = experts * slots
    step = width // experts
    side = int(np.sqrt(experts))
    c = dict(
        side=side,
        section=sections, expert=experts, mp=mps, micro=micro, length=length, heads=heads, size=size,
        cap=cap, width=width, ff=ff, buckets=buckets,
    )
    vmem = pl.BlockSpec(memory_space=pltpu.VMEM)
    hbm = pl.BlockSpec(memory_space=pl.ANY)

    def held(*shape):
        return pltpu.VMEM(shape, BF16)

    def exact(*shape):
        return pltpu.VMEM(shape, F32)

    scratch = [
        pltpu.SemaphoreType.DMA((SEMAPHORES,)),
        pltpu.SemaphoreType.DMA((SEMAPHORES,)),
        exact(sections, 8, width),
        pltpu.VMEM((length, length), jnp.int32),
        exact(heads, length, length),
        exact(micro, length, length),
        held(rows, width),
        held(3, rows, local),
        exact(micro * heads, length, length),
        held(rows, local),
        held(rows, local),
        held(rows, 3 * local),
        exact(heads, length, length),
        exact(buckets, length),
        held(6, rows, width),
        held(4, mps, part, width),
        held(2, group, part, width),
        held(rows, width),
        held(rows, width),
        held(rows, width),
        held(rows, width),
        held(rows, width),
        held(rows, width),
        exact(4, part, width),
        held(rows, ff),
        exact(rows, ff),
        exact(rows, ff),
        held(rows, ff),
        held(rows, ff),
        held(micro, experts * cap, length),
        held(micro, experts * cap, length),
        held(experts, slots, half + 128),
        held(sections, every, half + 128),
        held(experts, slots, half),
        held(sections, every, half),
        held(every, ff),
        held(every, ff),
        held(every, ff),
        held(every, width),
        exact(every, 128),
        held(sections, every, half),
        held(every, half),
        held(every, half + 128),
        held(experts, slots, half + 128),
        held(sections, every, half),
        held(every, half),
        held(every, half),
        held(experts, slots, half),
        held(rows, half + 128),
        held(group, part, half + 128),
        held(rows, half),
        held(group, part, half),
        exact(32, width),
        held(32, width),
        held(group, 32, width),
        held(32, width),
        held(side, 32, width),
        held(32, width),
        held(side, 32, width),
        exact(8, width),
        exact(side, 8, width),
        exact(8, width),
        exact(side, 8, width),
        exact(8, width),
        exact(mps, 8, width),
        held(9, width, 128),
        held(side, 5, width // side, 128),
        held(side, 4, width // side, 128),
        held(5, width // side, 128),
        held(4, width // side, 128),
        held(side, 5, step, 128),
        held(side, 4, step, 128),
        held(6, width, 128),
        held(side, 3, width // side, 128),
        held(side, 3, width // side, 128),
        held(3, width // side, 128),
        held(3, width // side, 128),
        held(side, 3, step, 128),
        held(side, 3, step, 128),
        held(width, ff),
        held(width, ff),
        held(ff, width),
        held(width, ff),
        held(width, ff),
        held(ff, width),
        held(width, ff),
        held(width, ff),
        held(ff, width),
        pltpu.SemaphoreType.DMA((20,)),
        held(128, width),
        held(rows, width),
        held(rows, width),
        held(local, width),
        held(local, width),
        held(local, width),
        held(local, width),
        held(experts, width),
        held(rows, width),
        held(rows, width),
        held(6, 4 * local, 128),
        held(9, width, 128),
        exact(every, ff),
    ]
    shape = jax.ShapeDtypeStruct
    block_output, input_grad, attn, dense, ge_gate, ge_up, ge_down, small, bias_grad = pl.pallas_call(
        functools.partial(kernel, c),
        out_shape=(
            shape((rows, width), BF16),
            shape((rows, width), BF16),
            shape((6, 4 * local, 128), BF16),
            shape((9, width, 128), BF16),
            shape((width, ff), BF16),
            shape((width, ff), BF16),
            shape((ff, width), BF16),
            shape((32, width), F32),
            shape((heads, 1, buckets), F32),
        ),
        in_specs=[hbm] * 2 + [vmem] * 5 + [hbm] * 11,
        out_specs=(hbm,) * 7 + (vmem,) * 2,
        scratch_shapes=scratch,
        compiler_params=pltpu.CompilerParams(
            collective_id=0, has_side_effects=True, vmem_limit_bytes=60 * 1024 * 1024
        ),
    )(
        block_input.reshape(rows, width),
        cotangent.reshape(rows, width),
        segments.reshape(micro, length),
        routes[:, 0].transpose(0, 2, 1).reshape(2 * micro, length),
        attn_gain,
        ffn_gain,
        pos_bias.transpose(2, 0, 1),
        query_weight[0].T,
        key_weight[0].T,
        value_weight[0].T,
        out_weight[0],
        router.T,
        dense_gate,
        dense_up,
        dense_down,
        expert_gate[0],
        expert_up[0],
        expert_down[0],
    )
    steps = 2

    def rows_of(rows, width):
        return pl.BlockSpec((rows // steps, width), lambda i: (i, 0))

    def whole(*dims):
        return pl.BlockSpec(dims, lambda i: (0,) * len(dims))

    tiles = ff // 128
    attn_shape = shape((local, width), F32)
    results = pl.pallas_call(
        functools.partial(widen, tiles, experts),
        grid=(steps,),
        out_shape=(
            shape((rows, width), F32),
            shape((rows, width), F32),
            *[attn_shape] * 4,
            shape((width, ff), F32),
            shape((width, ff), F32),
            shape((ff, width), F32),
            shape((width, ff), F32),
            shape((width, ff), F32),
            shape((ff, width), F32),
            shape((1, width), F32),
            shape((1, width), F32),
            shape((experts, width), F32),
            shape((heads, 1, buckets), F32),
        ),
        in_specs=[
            rows_of(rows, width),
            rows_of(rows, width),
            pl.BlockSpec((2 * tiles, 4, local // steps, 128), lambda i: (0, 0, i, 0)),
            pl.BlockSpec((tiles, width // steps, 128), lambda i: (0, i, 0)),
            pl.BlockSpec((tiles, width // steps, 128), lambda i: (1, i, 0)),
            pl.BlockSpec((tiles, 2, ff // steps, 128), lambda i: (2, 0, i, 0)),
            rows_of(width, ff),
            rows_of(width, ff),
            rows_of(ff, width),
            whole(32, width),
            whole(heads, 1, buckets),
        ],
        out_specs=(
            rows_of(rows, width),
            rows_of(rows, width),
            *[rows_of(local, width)] * 4,
            rows_of(width, ff),
            rows_of(width, ff),
            rows_of(ff, width),
            rows_of(width, ff),
            rows_of(width, ff),
            rows_of(ff, width),
            whole(1, width),
            whole(1, width),
            whole(experts, width),
            whole(heads, 1, buckets),
        ),
        compiler_params=pltpu.CompilerParams(vmem_limit_bytes=63 * 1024 * 1024),
    )(
        block_output,
        input_grad,
        attn.reshape(2 * tiles, 4, local, 128),
        dense,
        dense,
        dense.reshape(3 * tiles, 2, ff, 128),
        ge_gate,
        ge_up,
        ge_down,
        small,
        bias_grad,
    )
    return (
        results[0].reshape(block_input.shape),
        results[1].reshape(block_input.shape),
        results[12],
        results[2].T[None],
        results[3].T[None],
        results[4].T[None],
        results[5][None],
        results[15].transpose(1, 2, 0),
        results[13],
        results[6],
        results[7],
        results[8],
        results[14].T,
        results[9][None],
        results[10][None],
        results[11][None],
    )


def solution(mesh):
    placed = (
        P(None, "expert", None, None),
        P(None, "expert", None),
        P(None, "expert", None, None),
        P(None, "expert", None, None),
        P("section", None),
        P("section", None, "mp"),
        P("section", None, "mp"),
        P("section", None, "mp"),
        P("section", "mp", None),
        P("section", None, "mp"),
        P("section", None),
        P(None, ("section", "mp")),
        P(None, ("section", "mp")),
        P(("section", "mp"), None),
        P(),
        P("expert", None, ("section", "mp")),
        P("expert", None, ("section", "mp")),
        P("expert", ("section", "mp"), None),
    )
    return jax.shard_map(
        shards,
        mesh=mesh,
        in_specs=placed,
        out_specs=(
            P(None, "expert", None, None),
            P(None, "expert", None, None),
            P("section", None),
            P("section", None, "mp"),
            P("section", None, "mp"),
            P("section", None, "mp"),
            P("section", "mp", None),
            P("section", None, "mp"),
            P("section", None),
            P(None, ("section", "mp")),
            P(None, ("section", "mp")),
            P(("section", "mp"), None),
            P(),
            P("expert", None, ("section", "mp")),
            P("expert", None, ("section", "mp")),
            P("expert", ("section", "mp"), None),
        ),
        check_vma=False,
    )
```
